512 devices in a mesh: bal: 32 (over x, y), uly: 8 (over z), cfg: 2 (over core).
Axes of the slice: x: 4, y: 8, z: 8, core: 2. Of those that a mesh axis runs over, the one named last changes fastest.
Arguments:
- hidden: bfloat16 [2, 16384, 3072], P('cfg', ('bal', 'uly')), may hold values from -32 to 32
- w_qkv: bfloat16 [3072, 6144], P(None, ('uly', 'cfg')), may hold values from -0.109375 to 0.109375
- q_gain: float32 [2048], P('uly'), may hold values from 2 to 4
- cache_k: bfloat16 [2, 16384, 2048], P('cfg', 'bal', 'uly'), may hold values from -80 to 80
- cache_v: bfloat16 [2, 16384, 2048], P('cfg', 'bal', 'uly'), may hold values from -6 to 6
- fresh_list: int32 [2, 32, 8, 4], P('cfg', 'bal', 'uly'), may hold values from 0 to 8, as said below
Outputs:
- fresh_out: bfloat16 [2, 32, 8, 32, 2048], P('cfg', 'bal', 'uly')
The draws below stay inside these ranges and needn't reach their ends.
Inputs may be any that keep to these rules, and one draw needn't show every extreme that they name: `fresh_list`: for each branch and uly index, the 32 lists along bal name 32 blocks in all, at most 4 on one device, and some device names exactly 4, some none; within a list the used entries are distinct, rising and come first, and the unused ones hold 8.
All inputs are finite; a program needn't handle non-finite values.
Results may differ from the reference program's by a relative error of at most 0.014.
Values may be sent and summed in bfloat16 or wider, within the bound.
A program may use at most 64 MiB of HBM per device.

```python
import math
import jax
import jax.numpy as jnp
from jax import lax

D = 3072
HEADS = 16
HEAD_DIM = 128
TOK_DEV = 64
BLOCK = 8
MOST_BLOCKS = 4
BRANCHES = 2
SEQ = 16384
FRESH = 2048
N_BAL = 32
N_ULY = 8


def draw_hidden(key, part):
    key = jax.random.fold_in(key, 5)
    base_key, scale_key = jax.random.split(key)
    base = jnp.clip(jax.random.normal(base_key, (BRANCHES, SEQ, D), jnp.float32), -4.0, 4.0)
    spread = math.log(8.0)
    scale = jnp.exp(jax.random.uniform(scale_key, (BRANCHES, SEQ, 1), jnp.float32, 0.0, spread))
    return (base * scale).astype(jnp.bfloat16)


def draw_cache_k(key, part):
    key = jax.random.fold_in(key, 9)
    base_key, row_key, column_key = jax.random.split(key, 3)
    base = jnp.clip(jax.random.normal(base_key, (BRANCHES, SEQ, HEADS, HEAD_DIM), jnp.float32), -4.0, 4.0)
    spread = math.log(10.0)
    rows = jnp.exp(jax.random.uniform(row_key, (BRANCHES, SEQ, HEADS, 1), jnp.float32, 0.0, spread))
    columns = jnp.exp(jax.random.uniform(column_key, (HEADS, HEAD_DIM), jnp.float32, math.log(0.5), math.log(2.0)))
    return (base * rows * columns).reshape(BRANCHES, SEQ, HEADS * HEAD_DIM).astype(jnp.bfloat16)


def draw_fresh_list(key, part):
    key = jax.random.fold_in(key, 11)
    block_count = TOK_DEV // BLOCK
    pattern = jnp.tile(jnp.array([4, 2, 1, 1, 0, 0, 0, 0], jnp.int32), N_BAL // 8)
    row_keys = jax.random.split(jax.random.fold_in(key, 1), BRANCHES * N_ULY)
    counts = jax.vmap(lambda each: jax.random.permutation(each, pattern))(row_keys)
    counts = jnp.transpose(counts.reshape(BRANCHES, N_ULY, N_BAL), (0, 2, 1))
    owner_keys = jax.random.split(jax.random.fold_in(key, 2), BRANCHES * N_BAL * N_ULY)
    chosen_ids = jax.vmap(lambda each: jax.random.permutation(each, block_count)[:MOST_BLOCKS])(owner_keys)
    chosen_ids = chosen_ids.reshape(BRANCHES, N_BAL, N_ULY, MOST_BLOCKS).astype(jnp.int32)
    entry_ids = jnp.arange(MOST_BLOCKS, dtype=jnp.int32)
    chosen_ids = jnp.where(entry_ids < counts[..., None], chosen_ids, block_count)
    return jnp.sort(chosen_ids, axis=-1).astype(jnp.int32)


def levels(rng, shape, cuts, least, high):
    level = 1.0
    for dim, parts in cuts:
        steps = jax.random.uniform(jax.random.fold_in(jax.random.fold_in(rng, 6), dim), (parts,), jnp.float32, least / len(cuts), high / len(cuts))
        level = level * jnp.repeat(jnp.exp(steps), shape[dim] // parts).reshape((-1,) + (1,) * (len(shape) - 1 - dim))
    return level


def bell_draw(stream_key, shape, scale, limit, cuts=(), kind=jnp.bfloat16):
    values = jax.random.normal(stream_key, shape, jnp.float32) * scale
    if len(cuts) > 0:
        values = levels(stream_key, shape, cuts, -0.22, 0.18) * values
    return jnp.clip(values, min=-limit, max=limit).astype(kind)


def setup_inputs(seed: int = 0) -> dict:
    seeds = jax.random.split(jax.random.key(seed), 7)
    return {
        "hidden": draw_hidden(jax.random.fold_in(seeds[6], 71), 0),
        "w_qkv": bell_draw(seeds[1], (D, 3 * HEADS * HEAD_DIM), D ** -0.5, 0.109375, ((1, 16),)),
        "q_gain": jnp.clip(jnp.exp(math.log(4.0) - 0.6931472 * jax.random.uniform(seeds[2], (HEADS * HEAD_DIM,), jnp.float32) ** levels(seeds[2], (HEADS * HEAD_DIM,), ((0, 8),), -0.2, 0.2)), 2.0, 4.0),
        "cache_k": draw_cache_k(jax.random.fold_in(seeds[6], 71), 0),
        "cache_v": bell_draw(seeds[4], (BRANCHES, SEQ, HEADS * HEAD_DIM), 1.0, 6.0, ((0, 2), (1, 32), (2, 8))),
        "fresh_list": draw_fresh_list(jax.random.fold_in(seeds[6], 71), 0),
    }


def normalize(values):
    return values * lax.rsqrt(lax.optimization_barrier(jnp.mean(values * values, axis=-1, keepdims=True)) + 1e-06)

def layout(id_lists, tok_count, block_rows):
    bal_size, uly_size, list_len = id_lists.shape
    block_count = tok_count // block_rows
    counts = lax.optimization_barrier(jnp.sum((id_lists < block_count).astype(jnp.int32), axis=2))
    row_ends = jnp.cumsum(counts, axis=0).astype(jnp.int32) * block_rows
    row_start = row_ends - counts * block_rows
    owner_ids = jnp.arange(bal_size, dtype=jnp.int32)[:, None, None]
    slot_ids = jnp.arange(block_rows, dtype=jnp.int32)[None, None, :]
    uly_ids = jnp.arange(uly_size, dtype=jnp.int32)[None, :, None]
    global_row = slot_ids * bal_size + owner_ids + 0 * uly_ids
    ends_t = jnp.transpose(row_ends)[None, :, None, :]
    source = lax.optimization_barrier(jnp.sum((ends_t <= global_row[..., None]).astype(jnp.int32), axis=3))
    source_hit = (source[..., None] == jnp.arange(bal_size, dtype=jnp.int32)).astype(jnp.int32)
    local_row = global_row - lax.optimization_barrier(jnp.sum(source_hit * jnp.transpose(row_start)[None, :, None, :], axis=3))
    chosen = lax.optimization_barrier(jnp.sum(source_hit[..., None] * jnp.transpose(id_lists, (1, 0, 2))[None, :, None, :, :], axis=3))
    entry_hit = ((local_row // block_rows)[..., None] == jnp.arange(list_len, dtype=jnp.int32)).astype(jnp.int32)
    block_ids = lax.optimization_barrier(jnp.sum(entry_hit * chosen, axis=3))
    position = (source * uly_size + uly_ids) * tok_count + block_ids * block_rows + local_row % block_rows
    return (counts, row_start, source, local_row, position)

def reference(hidden, w_qkv, q_gain, cache_k, cache_v, fresh_list):
    gains = q_gain.reshape(HEADS, HEAD_DIM)
    scale = 1.0 / math.sqrt(HEAD_DIM)
    weight_full = w_qkv.astype(jnp.float32)
    results = []
    for branch in range(BRANCHES):
        counts, row_start, source, local_row, position = layout(fresh_list[branch], TOK_DEV, BLOCK)
        spots = position.reshape(-1).astype(jnp.int32)
        inputs = hidden[branch][spots].astype(jnp.float32)
        projected = jnp.dot(inputs, weight_full, precision=lax.Precision.HIGHEST)
        projected = projected.reshape(FRESH, HEADS, 3, HEAD_DIM)
        query = (normalize(projected[:, :, 0]) * gains).astype(jnp.bfloat16)
        keys = cache_k[branch].reshape(SEQ, HEADS, HEAD_DIM).at[spots].set(projected[:, :, 1].astype(jnp.bfloat16))
        values = cache_v[branch].reshape(SEQ, HEADS, HEAD_DIM).at[spots].set(projected[:, :, 2].astype(jnp.bfloat16))
        normed = normalize(keys.astype(jnp.float32)).astype(jnp.bfloat16)

        def one_head(operands):
            query_head, key_head, value_head = operands
            scores = jnp.dot(query_head.astype(jnp.float32), key_head.astype(jnp.float32).T, precision=lax.Precision.HIGHEST) * scale
            weights = jnp.exp(scores)
            totals = lax.optimization_barrier(jnp.sum(weights, axis=1, keepdims=True))
            rounded = lax.optimization_barrier(weights.astype(jnp.bfloat16))
            sums = jnp.dot(rounded.astype(jnp.float32), value_head.astype(jnp.float32), precision=lax.Precision.HIGHEST)
            return sums / totals
        attended = lax.map(one_head, (jnp.transpose(query, (1, 0, 2)), jnp.transpose(normed, (1, 0, 2)), jnp.transpose(values, (1, 0, 2))))
        attended = jnp.transpose(attended, (1, 0, 2)).reshape(FRESH, HEADS * HEAD_DIM).astype(jnp.bfloat16)
        uly_grid = jnp.zeros(source.shape, jnp.int32) + jnp.arange(N_ULY, dtype=jnp.int32)[None, :, None]
        placed = jnp.zeros((N_BAL, N_ULY, MOST_BLOCKS * BLOCK, HEADS * HEAD_DIM), jnp.bfloat16)
        placed = placed.at[source.reshape(-1), uly_grid.reshape(-1), local_row.reshape(-1)].set(attended)
        results.append(placed)
    return jnp.stack(results)
```

```python
import functools
import math

import jax
import jax.numpy as jnp
from jax import lax
from jax.experimental import pallas as pl
from jax.experimental.pallas import tpu as pltpu
from jax.sharding import PartitionSpec as P

HEAD_DIM = 128
BLOCK = 8
SIDE_X = 4
LANES = 128
MESH = pl.DeviceIdType.MESH
F32 = jnp.float32
BF16 = jnp.bfloat16


def normalize(values):
    return values * lax.rsqrt(jnp.mean(values * values, axis=-1, keepdims=True) + 1e-06)


def iota(shape, dim):
    return lax.broadcasted_iota(jnp.int32, shape, dim)


def dot(a, b):
    return jnp.dot(a, b, preferred_element_type=F32)


def dot_t(a, b):
    return lax.dot_general(a, b, (((1,), (1,)), ((), ())), preferred_element_type=F32)


def kernel(
    nx, nu, list_ref, hidden_ref, w_ref, gain_ref, ck_ref, cv_ref, out_ref,
    w_buf, lists, stage, out1, in1, xbuf, pkv, kv, qbuf, kvf, vaug, acc, rsout, rsin, ret_out, ret1,
    stage2, out2, in2,
    w_sem, list_s, list_r, p1_s, p1_r, z_s, z_r, f_s, kv_s, kv_r, q_s, q_r, kf_s, kf_r, rs_s, rs_r,
    ret_s, ret_r, back_s, back_r,
):
    b, u, c = lax.axis_index("bal"), lax.axis_index("uly"), lax.axis_index("cfg")
    nb, width = lists.shape[0], hidden_ref.shape[1]
    ny = nb // nx
    x, y = b // ny, b % ny
    toks = hidden_ref.shape[0]
    blocks = toks // BLOCK
    entries = list_ref.shape[0]
    keys = ck_ref.shape[0]
    half = nu * BLOCK
    pieces = width // LANES
    nh = 2 * nu
    other = 1 - c

    def bal_dev(k):
        return (lax.rem(b + k, nb), u, c)

    def x_dev(k):
        return (lax.rem(x + k, nx) * ny + y, u, c)

    def y_dev(k):
        return (x * ny + lax.rem(y + k, ny), u, c)

    def remote(src, dst, s, r, dev):
        return pltpu.make_async_remote_copy(
            src_ref=src, dst_ref=dst, send_sem=s, recv_sem=r, device_id=dev, device_id_type=MESH
        )

    def each(lo, hi, body):
        lax.fori_loop(lo, hi, lambda i, z: (body(i), z)[1], 0)

    w_copy = pltpu.make_async_copy(w_ref, w_buf, w_sem)
    w_copy.start()

    barrier = pltpu.get_barrier_semaphore()

    def greet_bal(k):
        pl.semaphore_signal(barrier, inc=1, device_id=bal_dev(k), device_id_type=MESH)

    def greet_z(k):
        flat = lax.rem(2 * u + c + k, nh)
        pl.semaphore_signal(
            barrier, inc=1, device_id=(b, flat // 2, lax.rem(flat, 2)), device_id_type=MESH
        )

    each(1, nb, greet_bal)
    each(1, nh, greet_z)

    for head in range(2):
        k_head = normalize(ck_ref[:, head * HEAD_DIM : (head + 1) * HEAD_DIM].astype(F32)).astype(BF16)
        v_head = cv_ref[:, head * HEAD_DIM : (head + 1) * HEAD_DIM]
        pkv[head, 0] = k_head
        pkv[head, 1] = v_head
    kv[x, c] = pkv[c]

    row = jnp.full((1, LANES), blocks, jnp.int32)
    lane = iota((1, LANES), 1)
    for j in range(entries):
        row = jnp.where(lane == j, list_ref[j], row)
    lists[b] = row

    pl.semaphore_wait(barrier, nb - 1 + nh - 1)

    def list_copy(k, slot):
        return remote(lists.at[b], lists.at[slot], list_s.at[k], list_r.at[slot], bal_dev(k))

    each(1, nb, lambda k: list_copy(k, b).start())

    partner_kv = remote(pkv.at[other], kv.at[x, c], kv_s.at[0], kv_r.at[x, c], (b, u, other))
    partner_kv.start()
    prev_x, next_x = lax.rem(x + nx - 1, nx), lax.rem(x + 1, nx)

    def ring(slot_x, branch, s, way):
        return remote(
            kv.at[slot_x, branch], kv.at[slot_x, branch], kv_s.at[s], kv_r.at[slot_x, branch], x_dev(way)
        )

    own_up, own_down = ring(x, c, 1, 1), ring(x, c, 2, nx - 1)
    own_up.start()
    own_down.start()

    each(1, nb, lambda k: list_copy(k, lax.rem(b + k, nb)).wait_recv())
    table = lists[...].reshape(nb, LANES)
    count = jnp.sum((table < blocks).astype(F32), axis=1, keepdims=True)
    sub_n, lane_n = iota((nb, nb), 0), iota((nb, nb), 1)
    start_row = jnp.sum(jnp.where(sub_n < lane_n, count, 0.0), axis=0, keepdims=True)
    count_row = jnp.sum(jnp.where(sub_n == lane_n, count, 0.0), axis=0, keepdims=True)
    start_col = jnp.sum(jnp.where(lane_n < sub_n, count_row, 0.0), axis=1, keepdims=True)
    my_start = jnp.sum(jnp.where(iota((1, nb), 1) == b, start_row, 0.0), axis=1, keepdims=True)
    my_count = jnp.sum(jnp.where(iota((1, nb), 1) == b, count_row, 0.0), axis=1, keepdims=True)
    start_row, count_row, start_col, count_col, my_start, my_count = (
        each_one.astype(jnp.int32) * BLOCK
        for each_one in (start_row, count_row, start_col, count, my_start, my_count)
    )

    dest = iota((nb, toks), 0)
    local = jnp.bitwise_and(dest - my_start, nb - 1)
    entry = local // BLOCK
    token = jnp.zeros((nb, toks), jnp.int32)
    for j in range(entries):
        token = jnp.where(entry == j, list_ref[j], token)
    token = token * BLOCK + local % BLOCK
    pick = (token == iota((nb, toks), 1)).astype(F32).astype(BF16)
    for j in range(pieces):
        stage[:, j, :] = dot(pick, hidden_ref[:, j * LANES : (j + 1) * LANES])
    out1[...] = stage[...].astype(BF16)

    def p1_copy(k, slot):
        to = lax.rem(b + k, nb)
        return remote(out1.at[to], in1.at[slot], p1_s.at[k], p1_r.at[slot], bal_dev(k))

    each(1, nb, lambda k: p1_copy(k, b).start())
    in1[b] = out1[b]

    remote(pkv.at[other], kv.at[x, other], kv_s.at[0], kv_r.at[x, other], (b, u, other)).wait_recv()
    their_up, their_down = ring(x, other, 3, 1), ring(x, other, 4, nx - 1)
    their_up.start()
    their_down.start()

    local_row = jnp.bitwise_and(b - start_row, nb - 1)
    slot_row = (start_row + local_row) // nb
    sel = (local_row < count_row) & (slot_row == iota((BLOCK, nb), 0))
    sel = sel.astype(F32).astype(BF16)
    near = (iota((BLOCK, nb), 1) == iota((BLOCK, nb), 0) * ny + y) & (iota((BLOCK, nb), 0) < nx)
    xbuf[c, u, :, width:] = dot(near.astype(F32).astype(BF16), table.astype(F32).astype(BF16)).astype(BF16)
    each(1, nb, lambda k: p1_copy(k, lax.rem(b + k, nb)).wait_recv())
    stage[...] = in1[...].astype(F32)
    for j in range(pieces):
        xbuf[c, u, :, j * LANES : (j + 1) * LANES] = dot(sel, stage[:, j, :].astype(BF16)).astype(BF16)

    def z_copy(k, slot):
        return remote(
            xbuf.at[c, u], xbuf.at[c, slot], z_s.at[k], z_r.at[c, slot], (b, lax.rem(u + k, nu), c)
        )

    def forward(branch, slot):
        return remote(
            xbuf.at[branch, slot], xbuf.at[branch, slot], f_s.at[slot], z_r.at[branch, slot], (b, u, other)
        )

    forward(c, u).start()
    order = []
    for k in range(1, nu // 2 + 1):
        order += [k] if 2 * k == nu else [k, nu - k]
    for k in order:
        z_copy(k, u).start()
    for k in order:
        slot = lax.rem(u + k, nu)
        z_copy(k, slot).wait_recv()
        forward(c, slot).start()

    ring(prev_x, c, 5, 1).wait_recv()
    on_up = ring(prev_x, c, 5, 1)
    on_up.start()
    ring(next_x, other, 6, nx - 1).wait_recv()
    on_down = ring(next_x, other, 6, nx - 1)
    on_down.start()

    each(0, nu, lambda k: forward(other, k).wait_recv())
    w_copy.wait()
    chunk = math.gcd(width, 1024)
    projected = jnp.zeros((2 * half, 3 * HEAD_DIM), F32)
    for j in range(0, width, chunk):
        rows = xbuf[:, :, :, j : j + chunk].astype(F32).reshape(2 * half, chunk).astype(BF16)
        projected = projected + dot(rows, w_buf[j : j + chunk, :])
    gains = gain_ref[pl.ds(c, 1), :]
    qbuf[y] = (normalize(projected[:, :HEAD_DIM]) * gains).astype(BF16)
    k_fresh = projected[:, HEAD_DIM : 2 * HEAD_DIM].astype(BF16).astype(F32)
    kvf[x, 0] = normalize(k_fresh).astype(BF16)
    kvf[x, 1] = projected[:, 2 * HEAD_DIM :].astype(BF16)

    def q_copy(k, slot):
        return remote(qbuf.at[y], qbuf.at[slot], q_s.at[k], q_r.at[slot], y_dev(k))

    def kf_copy(k, slot):
        return remote(kvf.at[x], kvf.at[slot], kf_s.at[k], kf_r.at[slot], x_dev(k))

    each(1, ny, lambda k: q_copy(k, y).start())
    each(1, nx, lambda k: kf_copy(k, x).start())

    for k in range(1, nx):
        slot = lax.rem(x + k, nx)
        if k == 1:
            ring(slot, c, 1, 1).wait_recv()
        elif k == nx - 1:
            ring(slot, other, 1, 1).wait_recv()
        else:
            ring(slot, c, 1, 1).wait_recv()
            ring(slot, other, 1, 1).wait_recv()
    span = nx * keys
    owner_hit = (iota((keys, nu), 0) // toks == iota((keys, nu), 1)).astype(F32).astype(BF16)
    block_hit = (iota((keys, LANES), 0) % toks) // BLOCK == iota((keys, LANES), 1)
    ones = jnp.ones((LANES, LANES), BF16)
    lane_u = iota((nu, LANES), 1).astype(F32)
    for branch in range(2):
        extra = xbuf[branch, :, :, width:].astype(F32)
        for k in range(nx):
            named = extra[:, k, :]
            hit = jnp.zeros((nu, LANES), F32)
            for j in range(entries):
                hit = hit + (named[:, j : j + 1] == lane_u).astype(F32)
            spread = jnp.where(block_hit, dot(owner_hit, hit.astype(BF16)), 0.0).astype(BF16)
            mask = 1.0 - dot(spread, ones)
            rows = pl.ds(k * keys, keys)
            vaug[branch, rows, :HEAD_DIM] = (kv[k, branch, 1].astype(F32) * mask).astype(BF16)
            vaug[branch, rows, HEAD_DIM:] = mask.astype(BF16)

    each(1, ny, lambda k: q_copy(k, lax.rem(y + k, ny)).wait_recv())
    each(1, nx, lambda k: kf_copy(k, lax.rem(x + k, nx)).wait_recv())
    factor = 1.0 / math.sqrt(HEAD_DIM)
    fresh_keys = nx * half

    for branch in range(2):
        mine = slice(branch * half, (branch + 1) * half)
        vaug[branch, span:, :HEAD_DIM] = kvf[:, 1, mine, :].reshape(fresh_keys, HEAD_DIM)
        vaug[branch, span:, HEAD_DIM:] = jnp.ones((fresh_keys, HEAD_DIM), BF16)
        queries = qbuf[:, mine, :].reshape(ny * half, HEAD_DIM)
        k_last = kvf[:, 0, mine, :].reshape(fresh_keys, HEAD_DIM)
        weights = jnp.exp(dot_t(queries, k_last) * factor).astype(BF16)
        acc[...] = dot(weights, vaug[branch, span:, :])

        def attend(k, branch=branch, queries=queries):
            weights = jnp.exp(dot_t(queries, kv[k, branch, 0]) * factor).astype(BF16)
            start = pl.multiple_of(k * keys, keys)
            acc[...] += dot(weights, vaug[branch, pl.ds(start, keys), :])

        each(0, nx, attend)
        rsout[:, mine, :] = acc[:, :HEAD_DIM].reshape(ny, half, HEAD_DIM).astype(BF16)
        totals = acc[:, HEAD_DIM:].reshape(ny, half, HEAD_DIM)
        place = iota((1, half, LANES), 2) == iota((1, half, LANES), 1) + branch * half
        flat = jnp.sum(jnp.where(place, totals, 0.0), axis=1, keepdims=True)
        all_totals = flat if branch == 0 else all_totals + flat
    coarse = all_totals.astype(BF16).astype(F32)
    tail = rsout.shape[1] - 2 * half
    tail_row = iota((ny, tail, LANES), 1)
    rsout[:, 2 * half :, :] = jnp.where(
        tail_row == 0, coarse, jnp.where(tail_row == 1, all_totals - coarse, 0.0)
    ).astype(BF16)

    def rs_copy(k, slot):
        to = lax.rem(y + k, ny)
        return remote(rsout.at[to], rsin.at[slot], rs_s.at[k], rs_r.at[slot], y_dev(k))

    each(1, ny, lambda k: rs_copy(k, y).start())
    rsin[y] = rsout[y]
    each(1, ny, lambda k: rs_copy(k, lax.rem(y + k, ny)).wait_recv())
    summed = jnp.sum(rsin[...].astype(F32), axis=0)
    total = summed[2 * half : 2 * half + 1, :] + summed[2 * half + 1 : 2 * half + 2, :]
    square = iota((2 * half, LANES), 0) == iota((2 * half, LANES), 1)
    total = jnp.sum(jnp.where(square, total, 0.0), axis=1, keepdims=True)
    attended = summed[: 2 * half, :] / total
    ret_out[...] = attended.reshape(nh, BLOCK, HEAD_DIM).astype(BF16)

    def ret_copy(k, slot):
        flat = lax.rem(2 * u + c + k, nh)
        to_u, to_c = flat // 2, lax.rem(flat, 2)
        return remote(
            ret_out.at[to_c * nu + to_u], ret1.at[slot], ret_s.at[k], ret_r.at[slot], (b, to_u, to_c)
        )

    each(1, nh, lambda k: ret_copy(k, 2 * u + c).start())
    ret1[2 * u + c] = ret_out[c * nu + u]
    slot_col = start_col + jnp.bitwise_and(b - start_col, nb - 1)
    give = (slot_col < start_col + count_col) & (slot_col // nb == iota((nb, BLOCK), 1))
    give = give.astype(F32).astype(BF16)
    each(1, nh, lambda k: ret_copy(k, lax.rem(2 * u + c + k, nh)).wait_recv())
    for h in range(nh):
        stage2[:, h, :] = dot(give, ret1[h])
    out2[...] = stage2[...].astype(BF16)

    def back_copy(k, slot):
        to = lax.rem(b + k, nb)
        return remote(out2.at[to], in2.at[slot], back_s.at[k], back_r.at[slot], bal_dev(k))

    each(1, nb, lambda k: back_copy(k, b).start())
    in2[b] = out2[b]
    spread_rows = iota((nb, nb), 0)
    final = (jnp.bitwise_and(my_start + spread_rows, nb - 1) == lane_n) & (spread_rows < my_count)
    final = final.astype(F32).astype(BF16)
    each(1, nb, lambda k: back_copy(k, lax.rem(b + k, nb)).wait_recv())
    stage2[...] = in2[...].astype(F32)
    for h in range(nh):
        out_ref[:, h * HEAD_DIM : (h + 1) * HEAD_DIM] = dot(final, stage2[:, h, :].astype(BF16)).astype(BF16)

    def sent_bal(k):
        list_copy(k, b).wait_send()
        p1_copy(k, b).wait_send()
        back_copy(k, b).wait_send()

    each(1, nb, sent_bal)
    each(1, nu, lambda k: z_copy(k, u).wait_send())
    each(0, nu, lambda k: forward(c, k).wait_send())
    for copy in (partner_kv, own_up, own_down, their_up, their_down, on_up, on_down):
        copy.wait_send()

    def sent_y(k):
        q_copy(k, y).wait_send()
        rs_copy(k, y).wait_send()

    each(1, ny, sent_y)
    each(1, nx, lambda k: kf_copy(k, x).wait_send())
    each(1, nh, lambda k: ret_copy(k, 2 * u + c).wait_send())


def on_device(hidden, w_qkv, q_gain, cache_k, cache_v, fresh_list):
    nb, nu = lax.axis_size("bal"), lax.axis_size("uly")
    nx = SIDE_X
    ny = nb // nx
    toks, width = hidden.shape[1:]
    keys = cache_k.shape[1]
    entries = fresh_list.shape[3]
    half = nu * BLOCK
    nh = 2 * nu
    pieces = width // LANES
    span = nx * (keys + half)
    vmem = pl.BlockSpec(memory_space=pltpu.VMEM)
    dma = pltpu.SemaphoreType.DMA
    out = pl.pallas_call(
        functools.partial(kernel, nx, nu),
        out_shape=jax.ShapeDtypeStruct((entries * BLOCK, nh * HEAD_DIM), BF16),
        in_specs=[
            pl.BlockSpec(memory_space=pltpu.SMEM),
            vmem,
            pl.BlockSpec(memory_space=pl.ANY),
            vmem,
            vmem,
            vmem,
        ],
        out_specs=vmem,
        scratch_shapes=[
            pltpu.VMEM(w_qkv.shape, BF16),
            pltpu.VMEM((nb, 1, LANES), jnp.int32),
            pltpu.VMEM((nb, pieces, LANES), F32),
            pltpu.VMEM((nb, pieces, LANES), BF16),
            pltpu.VMEM((nb, pieces, LANES), BF16),
            pltpu.VMEM((2, nu, BLOCK, width + LANES), BF16),
            pltpu.VMEM((2, 2, keys, HEAD_DIM), BF16),
            pltpu.VMEM((nx, 2, 2, keys, HEAD_DIM), BF16),
            pltpu.VMEM((ny, 2 * half, HEAD_DIM), BF16),
            pltpu.VMEM((nx, 2, 2 * half, HEAD_DIM), BF16),
            pltpu.VMEM((2, span, 2 * HEAD_DIM), BF16),
            pltpu.VMEM((ny * half, 2 * HEAD_DIM), F32),
            pltpu.VMEM((ny, 2 * half + 16, HEAD_DIM), BF16),
            pltpu.VMEM((ny, 2 * half + 16, HEAD_DIM), BF16),
            pltpu.VMEM((nh, BLOCK, HEAD_DIM), BF16),
            pltpu.VMEM((nh, BLOCK, HEAD_DIM), BF16),
            pltpu.VMEM((nb, nh, HEAD_DIM), F32),
            pltpu.VMEM((nb, nh, HEAD_DIM), BF16),
            pltpu.VMEM((nb, nh, HEAD_DIM), BF16),
            dma,
            dma((nb,)), dma((nb,)),
            dma((nb,)), dma((nb,)),
            dma((nu,)), dma((2, nu)),
            dma((nu,)),
            dma((7,)), dma((nx, 2)),
            dma((ny,)), dma((ny,)),
            dma((nx,)), dma((nx,)),
            dma((ny,)), dma((ny,)),
            dma((nh,)), dma((nh,)),
            dma((nb,)), dma((nb,)),
        ],
        compiler_params=pltpu.CompilerParams(
            collective_id=0, has_side_effects=True, vmem_limit_bytes=48 * 1024 * 1024
        ),
    )(
        fresh_list.reshape(entries),
        hidden.reshape(toks, width),
        w_qkv,
        q_gain.reshape(2, HEAD_DIM),
        cache_k.reshape(keys, 2 * HEAD_DIM),
        cache_v.reshape(keys, 2 * HEAD_DIM),
    )
    return out.reshape(1, 1, 1, entries * BLOCK, nh * HEAD_DIM)


def solution(mesh):
    in_specs = (
        P("cfg", ("bal", "uly"), None),
        P(None, ("uly", "cfg")),
        P("uly"),
        P("cfg", "bal", "uly"),
        P("cfg", "bal", "uly"),
        P("cfg", "bal", "uly", None),
    )
    out_specs = P("cfg", "bal", "uly", None, None)
    return jax.shard_map(
        on_device, mesh=mesh, in_specs=in_specs, out_specs=out_specs, check_vma=False
    )
```

```python
import functools
import math

import jax
import jax.numpy as jnp
from jax import lax
from jax.experimental import pallas as pl
from jax.experimental.pallas import tpu as pltpu
from jax.sharding import PartitionSpec as P

HEAD_DIM = 128
BLOCK = 8
SIDE_X = 4
LANES = 128
MESH = pl.DeviceIdType.MESH
F32 = jnp.float32
BF16 = jnp.bfloat16


def normalize(values):
    return values * lax.rsqrt(jnp.mean(values * values, axis=-1, keepdims=True) + 1e-06)


def iota(shape, dim):
    return lax.broadcasted_iota(jnp.int32, shape, dim)


def dot(a, b):
    return jnp.dot(a, b, preferred_element_type=F32)


def dot_t(a, b):
    return lax.dot_general(a, b, (((1,), (1,)), ((), ())), preferred_element_type=F32)


def kernel(
    nx, nu, list_in, hidden_in, w_in, gain_in, ck_in, cv_in, out_ref,
    list_ref, hidden_ref, w_buf, gain_ref, ck_ref, cv_ref, lists, stage, out1, in1, xbuf, kv, qbuf, kvf,
    vaug, rsout, rsin, ret_out, ret1, stage2, out2, in2,
    in_sem, w_s, w_r, list_s, list_r, p1_s, p1_r, z_s, z_r, kv_s, kv_r, q_s, q_r, kf_s, kf_r, rs_s, rs_r,
    ret_s, ret_r, back_s, back_r,
):
    b, u, c = lax.axis_index("bal"), lax.axis_index("uly"), lax.axis_index("cfg")
    nb, width = lists.shape[0], hidden_ref.shape[1]
    ny = nb // nx
    x, y = b // ny, b % ny
    toks = hidden_ref.shape[0]
    blocks = toks // BLOCK
    entries = list_ref.shape[0]
    keys = ck_ref.shape[0]
    half = nu * BLOCK
    pieces = width // LANES
    nh = 2 * nu
    other = 1 - c

    def bal_dev(k):
        return (lax.rem(b + k, nb), u, c)

    def x_dev(k):
        return (lax.rem(x + k, nx) * ny + y, u, c)

    def y_dev(k):
        return (x * ny + lax.rem(y + k, ny), u, c)

    def z_dev(k):
        return (b, lax.rem(u + k, nu), c)

    def remote(src, dst, s, r, dev):
        return pltpu.make_async_remote_copy(
            src_ref=src, dst_ref=dst, send_sem=s, recv_sem=r, device_id=dev, device_id_type=MESH
        )

    def each(lo, hi, body):
        lax.fori_loop(lo, hi, lambda i, z: (body(i), z)[1], 0)

    pairs = (
        (list_in, list_ref),
        (ck_in, ck_ref),
        (cv_in, cv_ref),
        (w_in, w_buf.at[c]),
        (hidden_in, hidden_ref),
        (gain_in, gain_ref),
    )
    loads = tuple(
        pltpu.make_async_copy(src, dst, in_sem.at[i]) for i, (src, dst) in enumerate(pairs)
    )
    for load in loads:
        load.start()
    list_load, k_load, v_load, w_load, hidden_load, gain_load = loads
    cleanup = []

    barrier = pltpu.get_barrier_semaphore()

    def greet(dev):
        pl.semaphore_signal(barrier, inc=1, device_id=dev, device_id_type=MESH)

    each(1, nb, lambda k: greet(bal_dev(k)))
    each(1, nu, lambda k: greet(z_dev(k)))
    greet((b, u, other))

    list_load.wait()
    my_rows = 0
    for j in range(entries):
        my_rows = my_rows + jnp.where(list_ref[j] < blocks, BLOCK, 0)
    lane = iota((1, LANES), 1)
    row = jnp.zeros((1, LANES), jnp.int32) + my_rows
    for j in range(entries):
        row = jnp.where(lane == LANES - entries + j, list_ref[j], row)
    lists[b] = row

    k_load.wait()
    v_load.wait()
    for head in range(2):
        columns = slice(head * HEAD_DIM, (head + 1) * HEAD_DIM)
        kv[x, head, 0] = normalize(ck_ref[:, columns].astype(F32)).astype(BF16)
        kv[x, head, 1] = cv_ref[:, columns]
    w_load.wait()
    hidden_load.wait()

    pl.semaphore_wait(barrier, nb - 1 + nu - 1 + 1)

    def list_copy(k, slot):
        return remote(lists.at[b], lists.at[slot], list_s.at[k], list_r.at[slot], bal_dev(k))

    each(1, nb, lambda k: list_copy(k, b).start())
    cleanup.append(lambda: each(1, nb, lambda k: list_copy(k, b).wait_send()))

    prev_x, next_x = lax.rem(x + nx - 1, nx), lax.rem(x + 1, nx)

    def ring(slot_x, s, way):
        return remote(kv.at[slot_x], kv.at[slot_x], kv_s.at[s], kv_r.at[slot_x], x_dev(way))

    def ring_head(slot_x, head, s, way):
        part = kv.at[slot_x, head]
        return remote(part, part, kv_s.at[s], kv_r.at[nx + head], x_dev(way))

    own_up, own_down = ring(x, 0, 1), ring(x, 1, nx - 1)
    own_up.start()
    own_down.start()
    cleanup.extend((own_up.wait_send, own_down.wait_send))
    w_out = remote(w_buf.at[c], w_buf.at[c], w_s, w_r, (b, u, other))
    w_out.start()
    cleanup.append(w_out.wait_send)

    dest = iota((nb, toks), 0)
    each(1, nb, lambda k: list_copy(k, lax.rem(b + k, nb)).wait_recv())
    table = lists[...].reshape(nb, LANES).astype(F32)
    sub_n, lane_n = iota((nb, nb), 0), iota((nb, nb), 1)
    my_start = jnp.sum(jnp.where(iota((nb, LANES), 0) < b, table, 0.0), axis=0, keepdims=True)
    my_start = my_start.astype(jnp.int32)
    local = jnp.bitwise_and(dest - my_start[:, :toks], nb - 1)
    entry = local // BLOCK
    token = jnp.zeros((nb, toks), jnp.int32)
    for j in range(entries):
        token = jnp.where(entry == j, list_ref[j], token)
    token = token * BLOCK + local % BLOCK
    pick = (token == iota((nb, toks), 1)).astype(F32).astype(BF16)
    for j in range(pieces):
        stage[:, j, :] = dot(pick, hidden_ref[:, j * LANES : (j + 1) * LANES])
    out1[...] = stage[...].astype(BF16)

    def p1_copy(k, slot):
        to = lax.rem(b + k, nb)
        return remote(out1.at[to], in1.at[slot], p1_s.at[k], p1_r.at[slot], bal_dev(k))

    each(1, nb, lambda k: p1_copy(k, b).start())
    cleanup.append(lambda: each(1, nb, lambda k: p1_copy(k, b).wait_send()))
    in1[b] = out1[b]

    counts = table[:, :nb]
    start_row = jnp.sum(jnp.where(sub_n < lane_n, counts, 0.0), axis=0, keepdims=True).astype(jnp.int32)
    count_row = jnp.sum(jnp.where(sub_n == lane_n, counts, 0.0), axis=0, keepdims=True)
    start_col = jnp.sum(jnp.where(lane_n < sub_n, count_row, 0.0), axis=1, keepdims=True).astype(jnp.int32)
    count_row = count_row.astype(jnp.int32)
    count_col = counts[:, :BLOCK].astype(jnp.int32)
    local_row = jnp.bitwise_and(b - start_row, nb - 1)
    slot_row = (start_row + local_row) // nb
    sel = (local_row < count_row) & (slot_row == iota((BLOCK, nb), 0))
    sel = sel.astype(F32).astype(BF16)
    near = (iota((BLOCK, nb), 1) == iota((BLOCK, nb), 0) * ny + y) & (iota((BLOCK, nb), 0) < nx)
    xbuf[u, :, width:] = dot(near.astype(F32).astype(BF16), table.astype(BF16)).astype(BF16)
    each(1, nb, lambda k: p1_copy(k, lax.rem(b + k, nb)).wait_recv())
    stage[...] = in1[...].astype(F32)
    for j in range(pieces):
        xbuf[u, :, j * LANES : (j + 1) * LANES] = dot(sel, stage[:, j, :].astype(BF16)).astype(BF16)

    def z_copy(k, slot):
        return remote(xbuf.at[u], xbuf.at[slot], z_s.at[k], z_r.at[slot], z_dev(k))

    order = []
    for k in range(nu // 2, 0, -1):
        order += [k] if 2 * k == nu else [k, nu - k]
    for k in order:
        z_copy(k, u).start()
    cleanup.append(lambda: each(1, nu, lambda k: z_copy(k, u).wait_send()))

    ring(prev_x, 0, 1).wait_recv()
    ring(next_x, 0, 1).wait_recv()
    on_up, on_down = ring_head(prev_x, 0, 2, 1), ring_head(next_x, 1, 3, nx - 1)
    on_up.start()
    on_down.start()
    cleanup.extend((on_up.wait_send, on_down.wait_send))
    w_out.wait_recv()
    gain_load.wait()

    each(1, nu, lambda k: z_copy(k, lax.rem(u + k, nu)).wait_recv())
    chunk = math.gcd(width, 1024)
    projected = [jnp.zeros((half, 3 * HEAD_DIM), F32)] * 2
    for j in range(0, width, chunk):
        rows = xbuf[:, :, j : j + chunk].astype(F32).reshape(half, chunk).astype(BF16)
        projected = [projected[h] + dot(rows, w_buf[h, j : j + chunk, :]) for h in range(2)]
    for h in range(2):
        mine = slice(h * half, (h + 1) * half)
        query = normalize(projected[h][:, :HEAD_DIM]) * gain_ref[h : h + 1, :]
        qbuf[y, mine, :] = query.astype(BF16)

    def q_copy(k, slot):
        return remote(qbuf.at[y], qbuf.at[slot], q_s.at[k], q_r.at[slot], y_dev(k))

    def kf_copy(k, slot):
        return remote(kvf.at[x], kvf.at[slot], kf_s.at[k], kf_r.at[slot], x_dev(k))

    for k in range(1, ny // 2 + 1):
        for way in [k] if 2 * k == ny else [k, ny - k]:
            q_copy(way, y).start()
    for h in range(2):
        mine = slice(h * half, (h + 1) * half)
        k_fresh = projected[h][:, HEAD_DIM : 2 * HEAD_DIM].astype(BF16).astype(F32)
        kvf[x, 0, mine, :] = normalize(k_fresh).astype(BF16)
        kvf[x, 1, mine, :] = projected[h][:, 2 * HEAD_DIM :].astype(BF16)
    each(1, nx, lambda k: kf_copy(k, x).start())
    cleanup.append(lambda: each(1, ny, lambda k: q_copy(k, y).wait_send()))
    cleanup.append(lambda: each(1, nx, lambda k: kf_copy(k, x).wait_send()))

    far_x = lax.rem(x + nx // 2, nx)
    ring_head(far_x, 0, 2, 1).wait_recv()
    ring_head(far_x, 1, 3, nx - 1).wait_recv()
    span = nx * keys
    owner_hit = (iota((keys, nu), 0) // toks == iota((keys, nu), 1)).astype(F32).astype(BF16)
    block_hit = (iota((keys, LANES), 0) % toks) // BLOCK == iota((keys, LANES), 1)
    ones = jnp.ones((LANES, LANES), BF16)
    lane_u = iota((nu, LANES), 1).astype(F32)
    extra = xbuf[:, :, width:].astype(F32)
    for k in range(nx):
        named = extra[:, k, :]
        hit = jnp.zeros((nu, LANES), F32)
        for j in range(LANES - entries, LANES):
            hit = hit + (named[:, j : j + 1] == lane_u).astype(F32)
        spread = jnp.where(block_hit, dot(owner_hit, hit.astype(BF16)), 0.0).astype(BF16)
        mask = 1.0 - dot(spread, ones)
        rows = pl.ds(k * keys, keys)
        for h in range(2):
            vaug[h, rows, :HEAD_DIM] = (kv[k, h, 1].astype(F32) * mask).astype(BF16)
            vaug[h, rows, HEAD_DIM:] = mask.astype(BF16)

    each(1, nx, lambda k: kf_copy(k, lax.rem(x + k, nx)).wait_recv())
    fresh_keys = nx * half
    for h in range(2):
        mine = slice(h * half, (h + 1) * half)
        vaug[h, span:, :HEAD_DIM] = kvf[:, 1, mine, :].reshape(fresh_keys, HEAD_DIM)
        vaug[h, span:, HEAD_DIM:] = jnp.ones((fresh_keys, HEAD_DIM), BF16)
    factor = 1.0 / math.sqrt(HEAD_DIM)

    def weigh(queries, some_keys):
        return jnp.exp(dot_t(queries, some_keys) * factor).astype(BF16)

    def rs_copy(k, slot):
        to = lax.rem(y + k, ny)
        return remote(rsout.at[to], rsin.at[slot], rs_s.at[k], rs_r.at[slot], y_dev(k))

    def attend(i):
        way_a, way_b = lax.rem(ny - i, ny), i + 1
        slot_a, slot_b = lax.rem(y + way_a, ny), lax.rem(y + way_b, ny)

        @pl.when(i > 0)
        def _():
            q_copy(way_a, slot_a).wait_recv()

        q_copy(way_b, slot_b).wait_recv()
        flat_a = jnp.zeros((1, LANES), F32)
        flat_b = jnp.zeros((1, LANES), F32)
        for h in range(2):
            mine = slice(h * half, (h + 1) * half)
            queries = jnp.concatenate([qbuf[slot_a, mine, :], qbuf[slot_b, mine, :]], axis=0)
            k_last = kvf[:, 0, mine, :].reshape(fresh_keys, HEAD_DIM)
            got = dot(weigh(queries, k_last), vaug[h, span:, :])
            for k in range(nx):
                got = got + dot(weigh(queries, kv[k, h, 0]), vaug[h, k * keys : (k + 1) * keys, :])
            rsout[slot_a, mine, :] = got[:half, :HEAD_DIM].astype(BF16)
            rsout[slot_b, mine, :] = got[half:, :HEAD_DIM].astype(BF16)
            place = iota((half, LANES), 1) == iota((half, LANES), 0) + h * half
            flat_a = flat_a + jnp.sum(jnp.where(place, got[:half, HEAD_DIM:], 0.0), axis=0, keepdims=True)
            flat_b = flat_b + jnp.sum(jnp.where(place, got[half:, HEAD_DIM:], 0.0), axis=0, keepdims=True)
        tail = rsout.shape[1] - 2 * half
        tail_row = iota((tail, LANES), 0)
        for slot, flat in ((slot_a, flat_a), (slot_b, flat_b)):
            coarse = flat.astype(BF16).astype(F32)
            rest = jnp.where(tail_row == 1, flat - coarse, 0.0)
            rsout[slot, 2 * half :, :] = jnp.where(tail_row == 0, coarse, rest).astype(BF16)

        @pl.when(i > 0)
        def _():
            rs_copy(way_a, y).start()

        rs_copy(way_b, y).start()

    each(0, ny // 2, attend)
    cleanup.append(lambda: each(1, ny, lambda k: rs_copy(k, y).wait_send()))
    rsin[y] = rsout[y]

    each(1, ny, lambda k: rs_copy(k, lax.rem(y + k, ny)).wait_recv())
    summed = jnp.sum(rsin[...].astype(F32), axis=0)
    total = summed[2 * half : 2 * half + 1, :] + summed[2 * half + 1 : 2 * half + 2, :]
    square = iota((2 * half, LANES), 0) == iota((2 * half, LANES), 1)
    total = jnp.sum(jnp.where(square, total, 0.0), axis=1, keepdims=True)
    attended = summed[: 2 * half, :] / total
    for h in range(2):
        rows = attended[h * half : (h + 1) * half, :]
        ret_out[:, h] = rows.reshape(nu, BLOCK, HEAD_DIM).astype(BF16)

    def ret_copy(k, slot):
        to = lax.rem(u + k, nu)
        return remote(ret_out.at[to], ret1.at[slot], ret_s.at[k], ret_r.at[slot], z_dev(k))

    each(1, nu, lambda k: ret_copy(k, u).start())
    cleanup.append(lambda: each(1, nu, lambda k: ret_copy(k, u).wait_send()))
    ret1[u] = ret_out[u]
    slot_col = start_col + jnp.bitwise_and(b - start_col, nb - 1)
    give = (slot_col < start_col + count_col) & (slot_col // nb == iota((nb, BLOCK), 1))
    give = give.astype(F32).astype(BF16)
    each(1, nu, lambda k: ret_copy(k, lax.rem(u + k, nu)).wait_recv())
    for h in range(nh):
        stage2[:, h, :] = dot(give, ret1[h // 2, h % 2])
    out2[...] = stage2[...].astype(BF16)

    def back_copy(k, slot):
        to = lax.rem(b + k, nb)
        return remote(out2.at[to], in2.at[slot], back_s.at[k], back_r.at[slot], bal_dev(k))

    each(1, nb, lambda k: back_copy(k, b).start())
    cleanup.append(lambda: each(1, nb, lambda k: back_copy(k, b).wait_send()))
    in2[b] = out2[b]
    spread_rows = iota((nb, nb), 0)
    final = jnp.bitwise_and(my_start[:, :nb] + spread_rows, nb - 1) == lane_n
    final = (final & (spread_rows < my_rows)).astype(F32).astype(BF16)
    each(1, nb, lambda k: back_copy(k, lax.rem(b + k, nb)).wait_recv())
    stage2[...] = in2[...].astype(F32)
    for h in range(nh):
        out_ref[:, h * HEAD_DIM : (h + 1) * HEAD_DIM] = dot(final, stage2[:, h, :].astype(BF16)).astype(BF16)

    for finish in cleanup:
        finish()


def on_device(hidden, w_qkv, q_gain, cache_k, cache_v, fresh_list):
    nb, nu = lax.axis_size("bal"), lax.axis_size("uly")
    nx = SIDE_X
    ny = nb // nx
    toks, width = hidden.shape[1:]
    keys = cache_k.shape[1]
    entries = fresh_list.shape[3]
    half = nu * BLOCK
    nh = 2 * nu
    pieces = width // LANES
    span = nx * (keys + half)
    vmem = pl.BlockSpec(memory_space=pltpu.VMEM)
    dma = pltpu.SemaphoreType.DMA
    out = pl.pallas_call(
        functools.partial(kernel, nx, nu),
        out_shape=jax.ShapeDtypeStruct((entries * BLOCK, nh * HEAD_DIM), BF16),
        in_specs=[
            *[pl.BlockSpec(memory_space=pltpu.HBM)] * 6,
        ],
        out_specs=vmem,
        scratch_shapes=[
            pltpu.SMEM((entries,), jnp.int32),
            pltpu.VMEM((toks, width), BF16),
            pltpu.VMEM((2, *w_qkv.shape), BF16),
            pltpu.VMEM((2, HEAD_DIM), F32),
            pltpu.VMEM((keys, 2 * HEAD_DIM), BF16),
            pltpu.VMEM((keys, 2 * HEAD_DIM), BF16),
            pltpu.VMEM((nb, 1, LANES), jnp.int32),
            pltpu.VMEM((nb, pieces, LANES), F32),
            pltpu.VMEM((nb, pieces, LANES), BF16),
            pltpu.VMEM((nb, pieces, LANES), BF16),
            pltpu.VMEM((nu, BLOCK, width + LANES), BF16),
            pltpu.VMEM((nx, 2, 2, keys, HEAD_DIM), BF16),
            pltpu.VMEM((ny, 2 * half, HEAD_DIM), BF16),
            pltpu.VMEM((nx, 2, 2 * half, HEAD_DIM), BF16),
            pltpu.VMEM((2, span, 2 * HEAD_DIM), BF16),
            pltpu.VMEM((ny, 2 * half + 16, HEAD_DIM), BF16),
            pltpu.VMEM((ny, 2 * half + 16, HEAD_DIM), BF16),
            pltpu.VMEM((nu, 2, BLOCK, HEAD_DIM), BF16),
            pltpu.VMEM((nu, 2, BLOCK, HEAD_DIM), BF16),
            pltpu.VMEM((nb, nh, HEAD_DIM), F32),
            pltpu.VMEM((nb, nh, HEAD_DIM), BF16),
            pltpu.VMEM((nb, nh, HEAD_DIM), BF16),
            dma((6,)),
            dma, dma,
            dma((nb,)), dma((nb,)),
            dma((nb,)), dma((nb,)),
            dma((nu,)), dma((nu,)),
            dma((4,)), dma((nx + 2,)),
            dma((ny,)), dma((ny,)),
            dma((nx,)), dma((nx,)),
            dma((ny,)), dma((ny,)),
            dma((nu,)), dma((nu,)),
            dma((nb,)), dma((nb,)),
        ],
        compiler_params=pltpu.CompilerParams(
            collective_id=0, has_side_effects=True, vmem_limit_bytes=63 * 1024 * 1024
        ),
    )(
        fresh_list.reshape(entries),
        hidden.reshape(toks, width),
        w_qkv,
        q_gain.reshape(2, HEAD_DIM),
        cache_k.reshape(keys, 2 * HEAD_DIM),
        cache_v.reshape(keys, 2 * HEAD_DIM),
    )
    return out.reshape(1, 1, 1, entries * BLOCK, nh * HEAD_DIM)


def solution(mesh):
    in_specs = (
        P("cfg", ("bal", "uly"), None),
        P(None, ("uly", "cfg")),
        P("uly"),
        P("cfg", "bal", "uly"),
        P("cfg", "bal", "uly"),
        P("cfg", "bal", "uly", None),
    )
    out_specs = P("cfg", "bal", "uly", None, None)
    return jax.shard_map(
        on_device, mesh=mesh, in_specs=in_specs, out_specs=out_specs, check_vma=False
    )
```

```python
import functools
import math

import jax
import jax.numpy as jnp
from jax import lax
from jax.experimental import pallas as pl
from jax.experimental.pallas import tpu as pltpu
from jax.sharding import PartitionSpec as P

HEAD_DIM = 128
BLOCK = 8
SIDE_X = 4
LANES = 128
MESH = pl.DeviceIdType.MESH
F32 = jnp.float32
BF16 = jnp.bfloat16


def normalize(values):
    return values * lax.rsqrt(jnp.mean(values * values, axis=-1, keepdims=True) + 1e-06)


def iota(shape, dim):
    return lax.broadcasted_iota(jnp.int32, shape, dim)


def dot(a, b):
    return jnp.dot(a, b, preferred_element_type=F32)


def dot_t(a, b):
    return lax.dot_general(a, b, (((1,), (1,)), ((), ())), preferred_element_type=F32)


def kernel(
    nx, nu, list_in, hidden_in, w_in, gain_in, ck_in, cv_in, out_ref,
    list_ref, hidden_ref, w_buf, gain_ref, ck_ref, cv_ref, lists, named, stage, out1, in1, outx, inx, xbuf, kv, qbuf, kvf,
    vaug, rsout, rsin, ret_out, ret1, stage2, out2, in2,
    in_sem, w_s, w_r, list_s, list_r, name_s, name_r, p1_s, p1_r, px_s, px_r, z_s, z_r, kv_s, kv_r, q_s, q_r, kf_s, kf_r, rs_s, rs_r,
    ret_s, ret_r, back_s, back_r,
):
    b, u, c = lax.axis_index("bal"), lax.axis_index("uly"), lax.axis_index("cfg")
    nb, width = lists.shape[0], hidden_ref.shape[1]
    ny = nb // nx
    x, y = b // ny, b % ny
    toks = hidden_ref.shape[0]
    blocks = toks // BLOCK
    entries = list_ref.shape[0]
    keys = ck_ref.shape[0]
    half = nu * BLOCK
    pieces = width // LANES
    nh = 2 * nu
    other = 1 - c

    def farthest(j, n):
        step = (j + 1) // 2
        return lax.rem(n // 2 + n + jnp.where(lax.rem(j, 2) == 1, step, -step), n)

    def x_of(k):
        return lax.rem(x + farthest(k - 1, nx), nx)

    def y_of(k):
        return lax.rem(y + farthest(k - 1, ny), ny)

    def bal_of(k):
        return x_of(lax.rem(k - 1, nx) + 1) * ny + y_of((k - 1) // nx + 1)

    def bal_dev(k):
        return (bal_of(k), u, c)

    def x_dev(k):
        return (lax.rem(x + k, nx) * ny + y, u, c)

    def y_dev(k):
        return (x * ny + lax.rem(y + k, ny), u, c)

    def z_dev(k):
        return (b, lax.rem(u + k, nu), c)

    def remote(src, dst, s, r, dev):
        return pltpu.make_async_remote_copy(
            src_ref=src, dst_ref=dst, send_sem=s, recv_sem=r, device_id=dev, device_id_type=MESH
        )

    def each(lo, hi, body):
        lax.fori_loop(lo, hi, lambda i, z: (body(i), z)[1], 0)

    pairs = (
        (list_in, list_ref),
        (ck_in, ck_ref),
        (cv_in, cv_ref),
        (w_in, w_buf.at[c]),
        (hidden_in, hidden_ref),
        (gain_in, gain_ref),
    )
    loads = tuple(
        pltpu.make_async_copy(src, dst, in_sem.at[i]) for i, (src, dst) in enumerate(pairs)
    )
    for load in loads:
        load.start()
    list_load, k_load, v_load, w_load, hidden_load, gain_load = loads
    cleanup = []

    barrier = pltpu.get_barrier_semaphore()

    def greet(dev):
        pl.semaphore_signal(barrier, inc=1, device_id=dev, device_id_type=MESH)

    each(1, nb, lambda k: greet(bal_dev(k)))
    each(1, nu, lambda k: greet(z_dev(k)))
    greet((b, u, other))

    list_load.wait()
    my_blocks = 0
    for j in range(entries):
        my_blocks = my_blocks + jnp.where(list_ref[j] < blocks, 1, 0)
    lane = iota((1, LANES), 1)
    row = jnp.zeros((1, LANES), jnp.int32) + my_blocks
    for j in range(entries):
        row = jnp.where(lane == LANES - entries + j, list_ref[j], row)
    lists[b] = row

    hidden_load.wait()
    token = jnp.zeros((nb, toks), jnp.int32)
    for j in range(entries):
        token = jnp.where(iota((nb, toks), 0) % entries == j, list_ref[j], token)
    token = token * BLOCK + iota((nb, toks), 0) // entries
    pick = (token == iota((nb, toks), 1)).astype(F32).astype(BF16)
    for j in range(pieces):
        stage[:, j, :] = dot(pick, hidden_ref[:, j * LANES : (j + 1) * LANES])
    out1[...] = stage[...].astype(BF16).reshape(out1.shape)

    k_load.wait()
    v_load.wait()
    for head in range(2):
        columns = slice(head * HEAD_DIM, (head + 1) * HEAD_DIM)
        kv[x, head, 0] = normalize(ck_ref[:, columns].astype(F32)).astype(BF16)
        kv[x, head, 1] = cv_ref[:, columns]
    w_load.wait()

    pl.semaphore_wait(barrier, nb - 1 + nu - 1 + 1)

    def list_copy(k, slot):
        return remote(lists.at[b], lists.at[slot], list_s.at[k], list_r.at[slot], bal_dev(k))

    each(1, nb, lambda k: list_copy(k, b).start())
    cleanup.append(lambda: each(1, nb, lambda k: list_copy(k, b).wait_send()))

    def p1_copy(k, slot):
        to = y_of(k)
        dev = (x * ny + to, u, c)
        return remote(out1.at[to], in1.at[slot], p1_s.at[k], p1_r.at[slot], dev)

    each(1, ny, lambda k: p1_copy(k, y).start())
    cleanup.append(lambda: each(1, ny, lambda k: p1_copy(k, y).wait_send()))
    in1[y] = out1[y]

    w_out = remote(w_buf.at[c], w_buf.at[c], w_s, w_r, (b, u, other))
    w_out.start()
    cleanup.append(w_out.wait_send)

    each(1, nb, lambda k: list_copy(k, bal_of(k)).wait_recv())
    table = lists[...].reshape(nb, LANES).astype(F32)
    counts = table[:, :nb]
    sub_n, lane_n = iota((nb, nb), 0), iota((nb, nb), 1)
    source = x * ny + lane_n // entries
    rank = jnp.sum(jnp.where(sub_n < source, counts, 0.0), axis=0, keepdims=True).astype(jnp.int32)
    known = jnp.sum(jnp.where(sub_n == source, counts, 0.0), axis=0, keepdims=True).astype(jnp.int32)
    entry = iota((1, nb), 1) % entries
    slots = nb // nx
    wanted = (sub_n % slots) * nx + sub_n // slots
    sel = (rank + entry == wanted) & (entry < known)
    sel = sel.astype(F32).astype(BF16)

    near = (iota((BLOCK, nb), 1) == iota((BLOCK, nb), 0) * ny + y) & (iota((BLOCK, nb), 0) < nx)
    named[u] = dot(near.astype(F32).astype(BF16), table.astype(BF16))

    def name_copy(k, slot):
        return remote(named.at[u], named.at[slot], name_s.at[k], name_r.at[slot], z_dev(k))

    each(1, nu, lambda k: name_copy(k, u).start())
    cleanup.append(lambda: each(1, nu, lambda k: name_copy(k, u).wait_send()))
    each(1, ny, lambda k: p1_copy(k, y_of(k)).wait_recv())
    stage[...] = in1[...].astype(F32).reshape(stage.shape)
    for j in range(pieces):
        part = dot(sel, stage[:, j, :].astype(BF16)).astype(BF16)
        for k in range(nx):
            outx[k, :, j * LANES : (j + 1) * LANES] = part[k * slots : (k + 1) * slots, :]

    def px_copy(k, slot):
        to = x_of(k)
        return remote(outx.at[to], inx.at[slot], px_s.at[k], px_r.at[slot], (to * ny + y, u, c))

    each(1, nx, lambda k: px_copy(k, x).start())
    cleanup.append(lambda: each(1, nx, lambda k: px_copy(k, x).wait_send()))
    inx[x] = outx[x]

    prev_x, next_x, far_x = lax.rem(x + nx - 1, nx), lax.rem(x + 1, nx), lax.rem(x + nx // 2, nx)

    def ring(slot_x, s, way):
        return remote(kv.at[slot_x], kv.at[slot_x], kv_s.at[s], kv_r.at[slot_x], x_dev(way))

    def ring_head(slot_x, head, s, way):
        part = kv.at[slot_x, head]
        return remote(part, part, kv_s.at[s], kv_r.at[nx + head], x_dev(way))

    own_up, own_down = ring(x, 0, 1), ring(x, 1, nx - 1)
    own_up.start()
    own_down.start()
    cleanup.extend((own_up.wait_send, own_down.wait_send))

    each(1, nx, lambda k: px_copy(k, x_of(k)).wait_recv())
    gathered = inx[0].astype(F32)
    for k in range(1, nx):
        gathered = gathered + inx[k].astype(F32)
    xbuf[u] = gathered.astype(BF16)

    def z_copy(k, slot):
        return remote(xbuf.at[u], xbuf.at[slot], z_s.at[k], z_r.at[slot], z_dev(k))

    order = []
    for k in range(nu // 2, 0, -1):
        order += [k] if 2 * k == nu else [k, nu - k]
    for k in order:
        z_copy(k, u).start()
    cleanup.append(lambda: each(1, nu, lambda k: z_copy(k, u).wait_send()))

    span = nx * keys
    owner_hit = (iota((keys, nu), 0) // toks == iota((keys, nu), 1)).astype(F32).astype(BF16)
    block_hit = (iota((keys, LANES), 0) % toks) // BLOCK == iota((keys, LANES), 1)
    ones = jnp.ones((LANES, LANES), BF16)
    lane_u = iota((nu, LANES), 1).astype(F32)

    def weigh_values(k):
        ids = named[:, pl.ds(k, 1), :].reshape(nu, LANES)
        hit = jnp.zeros((nu, LANES), F32)
        for j in range(LANES - entries, LANES):
            hit = hit + (ids[:, j : j + 1] == lane_u).astype(F32)
        spread = jnp.where(block_hit, dot(owner_hit, hit.astype(BF16)), 0.0).astype(BF16)
        mask = 1.0 - dot(spread, ones)
        rows = pl.ds(pl.multiple_of(k * keys, keys), keys)
        for h in range(2):
            vaug[h, rows, :HEAD_DIM] = (kv[k, h, 1].astype(F32) * mask).astype(BF16)
            vaug[h, rows, HEAD_DIM:] = mask.astype(BF16)

    each(1, nu, lambda k: name_copy(k, lax.rem(u + k, nu)).wait_recv())
    weigh_values(x)

    ring(prev_x, 0, 1).wait_recv()
    ring(next_x, 0, 1).wait_recv()
    on_up, on_down = ring_head(prev_x, 0, 2, 1), ring_head(next_x, 1, 3, nx - 1)
    on_up.start()
    on_down.start()
    cleanup.extend((on_up.wait_send, on_down.wait_send))
    weigh_values(prev_x)
    weigh_values(next_x)
    w_out.wait_recv()
    gain_load.wait()

    each(1, nu, lambda k: z_copy(k, lax.rem(u + k, nu)).wait_recv())
    chunk = math.gcd(width, 1024)
    projected = [jnp.zeros((half, 3 * HEAD_DIM), F32)] * 2
    for j in range(0, width, chunk):
        rows = xbuf[:, :, j : j + chunk].astype(F32).reshape(half, chunk).astype(BF16)
        projected = [projected[h] + dot(rows, w_buf[h, j : j + chunk, :]) for h in range(2)]
    for h in range(2):
        mine = slice(h * half, (h + 1) * half)
        query = normalize(projected[h][:, :HEAD_DIM]) * gain_ref[h : h + 1, :]
        qbuf[y, mine, :] = query.astype(BF16)

    def q_copy(k, slot):
        return remote(qbuf.at[y], qbuf.at[slot], q_s.at[k], q_r.at[slot], y_dev(k))

    def kf_copy(k, slot):
        return remote(kvf.at[x], kvf.at[slot], kf_s.at[k], kf_r.at[slot], x_dev(k))

    for k in range(1, ny // 2 + 1):
        for way in [k] if 2 * k == ny else [k, ny - k]:
            q_copy(way, y).start()
    for h in range(2):
        mine = slice(h * half, (h + 1) * half)
        k_fresh = projected[h][:, HEAD_DIM : 2 * HEAD_DIM].astype(BF16).astype(F32)
        kvf[x, 0, mine, :] = normalize(k_fresh).astype(BF16)
        kvf[x, 1, mine, :] = projected[h][:, 2 * HEAD_DIM :].astype(BF16)
    each(1, nx, lambda k: kf_copy(k, x).start())
    cleanup.append(lambda: each(1, ny, lambda k: q_copy(k, y).wait_send()))
    cleanup.append(lambda: each(1, nx, lambda k: kf_copy(k, x).wait_send()))

    ring_head(far_x, 0, 2, 1).wait_recv()
    ring_head(far_x, 1, 3, nx - 1).wait_recv()
    weigh_values(far_x)

    each(1, nx, lambda k: kf_copy(k, lax.rem(x + k, nx)).wait_recv())
    fresh_keys = nx * half
    for h in range(2):
        mine = slice(h * half, (h + 1) * half)
        vaug[h, span:, :HEAD_DIM] = kvf[:, 1, mine, :].reshape(fresh_keys, HEAD_DIM)
        vaug[h, span:, HEAD_DIM:] = jnp.ones((fresh_keys, HEAD_DIM), BF16)
    factor = 1.0 / math.sqrt(HEAD_DIM)

    def weigh(queries, some_keys):
        return jnp.exp(dot_t(queries, some_keys) * factor).astype(BF16)

    def rs_copy(k, slot):
        to = lax.rem(y + k, ny)
        return remote(rsout.at[to], rsin.at[slot], rs_s.at[k], rs_r.at[slot], y_dev(k))

    def attend(i):
        way_a, way_b = lax.rem(ny - i, ny), i + 1
        slot_a, slot_b = lax.rem(y + way_a, ny), lax.rem(y + way_b, ny)

        @pl.when(i > 0)
        def _():
            q_copy(way_a, slot_a).wait_recv()

        q_copy(way_b, slot_b).wait_recv()
        flat_a = jnp.zeros((1, LANES), F32)
        flat_b = jnp.zeros((1, LANES), F32)
        for h in range(2):
            mine = slice(h * half, (h + 1) * half)
            queries = jnp.concatenate([qbuf[slot_a, mine, :], qbuf[slot_b, mine, :]], axis=0)
            k_last = kvf[:, 0, mine, :].reshape(fresh_keys, HEAD_DIM)
            got = dot(weigh(queries, k_last), vaug[h, span:, :])
            for k in range(nx):
                got = got + dot(weigh(queries, kv[k, h, 0]), vaug[h, k * keys : (k + 1) * keys, :])
            rsout[slot_a, mine, :] = got[:half, :HEAD_DIM].astype(BF16)
            rsout[slot_b, mine, :] = got[half:, :HEAD_DIM].astype(BF16)
            place = iota((half, LANES), 1) == iota((half, LANES), 0) + h * half
            flat_a = flat_a + jnp.sum(jnp.where(place, got[:half, HEAD_DIM:], 0.0), axis=0, keepdims=True)
            flat_b = flat_b + jnp.sum(jnp.where(place, got[half:, HEAD_DIM:], 0.0), axis=0, keepdims=True)
        tail = rsout.shape[1] - 2 * half
        tail_row = iota((tail, LANES), 0)
        for slot, flat in ((slot_a, flat_a), (slot_b, flat_b)):
            coarse = flat.astype(BF16).astype(F32)
            rest = jnp.where(tail_row == 1, flat - coarse, 0.0)
            rsout[slot, 2 * half :, :] = jnp.where(tail_row == 0, coarse, rest).astype(BF16)

        @pl.when(i > 0)
        def _():
            rs_copy(way_a, y).start()

        rs_copy(way_b, y).start()

    each(0, ny // 2, attend)
    cleanup.append(lambda: each(1, ny, lambda k: rs_copy(k, y).wait_send()))
    rsin[y] = rsout[y]

    each(1, ny, lambda k: rs_copy(k, lax.rem(y + k, ny)).wait_recv())
    summed = jnp.sum(rsin[...].astype(F32), axis=0)
    total = summed[2 * half : 2 * half + 1, :] + summed[2 * half + 1 : 2 * half + 2, :]
    square = iota((2 * half, LANES), 0) == iota((2 * half, LANES), 1)
    total = jnp.sum(jnp.where(square, total, 0.0), axis=1, keepdims=True)
    attended = summed[: 2 * half, :] / total
    for h in range(2):
        rows = attended[h * half : (h + 1) * half, :]
        ret_out[:, h] = rows.reshape(nu, BLOCK, HEAD_DIM).astype(BF16)

    def ret_copy(k, slot):
        to = lax.rem(u + k, nu)
        return remote(ret_out.at[to], ret1.at[slot], ret_s.at[k], ret_r.at[slot], z_dev(k))

    each(1, nu, lambda k: ret_copy(k, u).start())
    cleanup.append(lambda: each(1, nu, lambda k: ret_copy(k, u).wait_send()))
    ret1[u] = ret_out[u]
    count_row = jnp.sum(jnp.where(sub_n == lane_n, counts, 0.0), axis=0, keepdims=True)
    start_col = jnp.sum(jnp.where(lane_n < sub_n, count_row, 0.0), axis=1, keepdims=True).astype(jnp.int32)
    rank_col = start_col + jnp.bitwise_and(x - start_col, nx - 1)
    give = rank_col < start_col + counts[:, :slots].astype(jnp.int32)
    give = give & (rank_col // nx == iota((nb, slots), 1))
    give = give.astype(F32).astype(BF16)
    each(1, nu, lambda k: ret_copy(k, lax.rem(u + k, nu)).wait_recv())
    for h in range(nh):
        stage2[:, h, :] = dot(give, ret1[h // 2, h % 2])
    out2[...] = stage2[...].astype(BF16)

    def back_copy(k, slot):
        to = bal_of(k)
        return remote(out2.at[to], in2.at[slot], back_s.at[k], back_r.at[slot], (to, u, c))

    each(1, nb, lambda k: back_copy(k, b).start())
    cleanup.append(lambda: each(1, nb, lambda k: back_copy(k, b).wait_send()))
    in2[b] = out2[b]
    my_start = jnp.sum(jnp.where(sub_n < b, counts, 0.0), axis=0, keepdims=True).astype(jnp.int32)
    from_x = jnp.bitwise_and(my_start + sub_n // BLOCK, nx - 1)
    final = (from_x * ny + sub_n % BLOCK == lane_n) & (sub_n // BLOCK < my_blocks)
    final = final.astype(F32).astype(BF16)
    each(1, nb, lambda k: back_copy(k, bal_of(k)).wait_recv())
    stage2[...] = in2[...].astype(F32)
    for h in range(nh):
        out_ref[:, h * HEAD_DIM : (h + 1) * HEAD_DIM] = dot(final, stage2[:, h, :].astype(BF16)).astype(BF16)

    for finish in cleanup:
        finish()


def on_device(hidden, w_qkv, q_gain, cache_k, cache_v, fresh_list):
    nb, nu = lax.axis_size("bal"), lax.axis_size("uly")
    nx = SIDE_X
    ny = nb // nx
    toks, width = hidden.shape[1:]
    keys = cache_k.shape[1]
    entries = fresh_list.shape[3]
    half = nu * BLOCK
    nh = 2 * nu
    pieces = width // LANES
    span = nx * (keys + half)
    vmem = pl.BlockSpec(memory_space=pltpu.VMEM)
    dma = pltpu.SemaphoreType.DMA
    out = pl.pallas_call(
        functools.partial(kernel, nx, nu),
        out_shape=jax.ShapeDtypeStruct((entries * BLOCK, nh * HEAD_DIM), BF16),
        in_specs=[
            *[pl.BlockSpec(memory_space=pltpu.HBM)] * 6,
        ],
        out_specs=vmem,
        scratch_shapes=[
            pltpu.SMEM((entries,), jnp.int32),
            pltpu.VMEM((toks, width), BF16),
            pltpu.VMEM((2, *w_qkv.shape), BF16),
            pltpu.VMEM((2, HEAD_DIM), F32),
            pltpu.VMEM((keys, 2 * HEAD_DIM), BF16),
            pltpu.VMEM((keys, 2 * HEAD_DIM), BF16),
            pltpu.VMEM((nb, 1, LANES), jnp.int32),
            pltpu.VMEM((nu, BLOCK, LANES), F32),
            pltpu.VMEM((nb, pieces, LANES), F32),
            pltpu.VMEM((ny, entries, pieces, LANES), BF16),
            pltpu.VMEM((ny, entries, pieces, LANES), BF16),
            pltpu.VMEM((nx, nb // nx, width), BF16),
            pltpu.VMEM((nx, nb // nx, width), BF16),
            pltpu.VMEM((nu, nb // nx, width), BF16),
            pltpu.VMEM((nx, 2, 2, keys, HEAD_DIM), BF16),
            pltpu.VMEM((ny, 2 * half, HEAD_DIM), BF16),
            pltpu.VMEM((nx, 2, 2 * half, HEAD_DIM), BF16),
            pltpu.VMEM((2, span, 2 * HEAD_DIM), BF16),
            pltpu.VMEM((ny, 2 * half + 16, HEAD_DIM), BF16),
            pltpu.VMEM((ny, 2 * half + 16, HEAD_DIM), BF16),
            pltpu.VMEM((nu, 2, BLOCK, HEAD_DIM), BF16),
            pltpu.VMEM((nu, 2, BLOCK, HEAD_DIM), BF16),
            pltpu.VMEM((nb, nh, HEAD_DIM), F32),
            pltpu.VMEM((nb, nh, HEAD_DIM), BF16),
            pltpu.VMEM((nb, nh, HEAD_DIM), BF16),
            dma((6,)),
            dma, dma,
            dma((nb,)), dma((nb,)),
            dma((nu,)), dma((nu,)),
            dma((ny,)), dma((ny,)),
            dma((nx,)), dma((nx,)),
            dma((nu,)), dma((nu,)),
            dma((4,)), dma((nx + 2,)),
            dma((ny,)), dma((ny,)),
            dma((nx,)), dma((nx,)),
            dma((ny,)), dma((ny,)),
            dma((nu,)), dma((nu,)),
            dma((nb,)), dma((nb,)),
        ],
        compiler_params=pltpu.CompilerParams(
            collective_id=0, has_side_effects=True, vmem_limit_bytes=63 * 1024 * 1024
        ),
    )(
        fresh_list.reshape(entries),
        hidden.reshape(toks, width),
        w_qkv,
        q_gain.reshape(2, HEAD_DIM),
        cache_k.reshape(keys, 2 * HEAD_DIM),
        cache_v.reshape(keys, 2 * HEAD_DIM),
    )
    return out.reshape(1, 1, 1, entries * BLOCK, nh * HEAD_DIM)


def solution(mesh):
    in_specs = (
        P("cfg", ("bal", "uly"), None),
        P(None, ("uly", "cfg")),
        P("uly"),
        P("cfg", "bal", "uly"),
        P("cfg", "bal", "uly"),
        P("cfg", "bal", "uly", None),
    )
    out_specs = P("cfg", "bal", "uly", None, None)
    return jax.shard_map(
        on_device, mesh=mesh, in_specs=in_specs, out_specs=out_specs, check_vma=False
    )
```

```python
import functools
import math

import jax
import jax.numpy as jnp
from jax import lax
from jax.experimental import pallas as pl
from jax.experimental.pallas import tpu as pltpu
from jax.sharding import PartitionSpec as P

HEAD_DIM = 128
BLOCK = 8
SIDE_X = 4
LANES = 128
MESH = pl.DeviceIdType.MESH
F32 = jnp.float32
BF16 = jnp.bfloat16


def normalize(values):
    return values * lax.rsqrt(jnp.mean(values * values, axis=-1, keepdims=True) + 1e-06)


def iota(shape, dim):
    return lax.broadcasted_iota(jnp.int32, shape, dim)


def dot(a, b):
    return jnp.dot(a, b, preferred_element_type=F32)


def dot_t(a, b):
    return lax.dot_general(a, b, (((1,), (1,)), ((), ())), preferred_element_type=F32)


def kernel(
    nx, nu, list_in, hidden_in, w_in, gain_in, ck_in, cv_in, out_ref,
    list_ref, hidden_ref, w_buf, gain_ref, ck_ref, cv_ref, lists, named, stage, out1, in1, outx, inx, xbuf, kv, qbuf, kvf,
    vaug, rsout, rsin, ret_out, ret1, stage2, out2, in2,
    in_sem, w_s, w_r, list_s, list_r, name_s, name_r, p1_s, p1_r, px_s, px_r, z_s, z_r, kv_s, kv_r, q_s, q_r, kf_s, kf_r, rs_s, rs_r,
    ret_s, ret_r, back_s, back_r,
):
    b, u, c = lax.axis_index("bal"), lax.axis_index("uly"), lax.axis_index("cfg")
    nb, width = lists.shape[0], hidden_ref.shape[1]
    ny = nb // nx
    x, y = b // ny, b % ny
    toks = hidden_ref.shape[0]
    blocks = toks // BLOCK
    entries = list_ref.shape[0]
    keys = ck_ref.shape[0]
    half = nu * BLOCK
    pieces = width // LANES
    nh = 2 * nu
    other = 1 - c

    def farthest(j, n):
        step = (j + 1) // 2
        return lax.rem(n // 2 + n + jnp.where(lax.rem(j, 2) == 1, step, -step), n)

    def x_of(k):
        return lax.rem(x + farthest(k - 1, nx), nx)

    def y_of(k):
        return lax.rem(y + farthest(k - 1, ny), ny)

    def bal_of(k):
        return x_of(lax.rem(k - 1, nx) + 1) * ny + y_of((k - 1) // nx + 1)

    def bal_dev(k):
        return (bal_of(k), u, c)

    def x_dev(k):
        return (lax.rem(x + k, nx) * ny + y, u, c)

    def y_dev(k):
        return (x * ny + lax.rem(y + k, ny), u, c)

    def z_dev(k):
        return (b, lax.rem(u + k, nu), c)

    def remote(src, dst, s, r, dev):
        return pltpu.make_async_remote_copy(
            src_ref=src, dst_ref=dst, send_sem=s, recv_sem=r, device_id=dev, device_id_type=MESH
        )

    def each(lo, hi, body):
        lax.fori_loop(lo, hi, lambda i, z: (body(i), z)[1], 0)

    pairs = (
        (list_in, list_ref),
        (ck_in, ck_ref),
        (cv_in, cv_ref),
        (w_in, w_buf.at[c]),
        (hidden_in, hidden_ref),
        (gain_in, gain_ref),
    )
    loads = tuple(
        pltpu.make_async_copy(src, dst, in_sem.at[i]) for i, (src, dst) in enumerate(pairs)
    )
    for load in loads:
        load.start()
    list_load, k_load, v_load, w_load, hidden_load, gain_load = loads
    cleanup = []

    barrier = pltpu.get_barrier_semaphore()

    def greet(dev):
        pl.semaphore_signal(barrier, inc=1, device_id=dev, device_id_type=MESH)

    each(1, nb, lambda k: greet(bal_dev(k)))
    each(1, nu, lambda k: greet(z_dev(k)))
    greet((b, u, other))

    list_load.wait()
    my_blocks = 0
    for j in range(entries):
        my_blocks = my_blocks + jnp.where(list_ref[j] < blocks, 1, 0)
    lane = iota((1, LANES), 1)
    row = jnp.zeros((1, LANES), jnp.int32) + my_blocks
    for j in range(entries):
        row = jnp.where(lane == LANES - entries + j, list_ref[j], row)
    lists[b] = row

    hidden_load.wait()
    token = jnp.zeros((nb, toks), jnp.int32)
    for j in range(entries):
        token = jnp.where(iota((nb, toks), 0) % entries == j, list_ref[j], token)
    token = token * BLOCK + iota((nb, toks), 0) // entries
    pick = (token == iota((nb, toks), 1)).astype(F32).astype(BF16)
    for j in range(pieces):
        stage[:, j, :] = dot(pick, hidden_ref[:, j * LANES : (j + 1) * LANES])
    out1[...] = stage[...].astype(BF16).reshape(out1.shape)

    k_load.wait()
    v_load.wait()
    for head in range(2):
        columns = slice(head * HEAD_DIM, (head + 1) * HEAD_DIM)
        kv[x, head, 0] = normalize(ck_ref[:, columns].astype(F32)).astype(BF16)
        kv[x, head, 1] = cv_ref[:, columns]
    w_load.wait()

    pl.semaphore_wait(barrier, nb - 1 + nu - 1 + 1)

    def list_copy(k, slot):
        return remote(lists.at[b], lists.at[slot], list_s.at[k], list_r.at[slot], bal_dev(k))

    each(1, nb, lambda k: list_copy(k, b).start())
    cleanup.append(lambda: each(1, nb, lambda k: list_copy(k, b).wait_send()))

    def p1_copy(k, slot):
        to = y_of(k)
        dev = (x * ny + to, u, c)
        return remote(out1.at[to], in1.at[slot], p1_s.at[k], p1_r.at[slot], dev)

    each(1, ny, lambda k: p1_copy(k, y).start())
    cleanup.append(lambda: each(1, ny, lambda k: p1_copy(k, y).wait_send()))
    in1[y] = out1[y]

    w_out = remote(w_buf.at[c], w_buf.at[c], w_s, w_r, (b, u, other))
    w_out.start()
    cleanup.append(w_out.wait_send)

    prev_x, next_x, far_x = lax.rem(x + nx - 1, nx), lax.rem(x + 1, nx), lax.rem(x + nx // 2, nx)

    def ring(slot_x, head, s, way):
        part = kv.at[slot_x, head]
        return remote(part, part, kv_s.at[s], kv_r.at[slot_x, head], x_dev(way))

    def ring_start(head):
        up, down = ring(x, head, 2 * head, 1), ring(x, head, 2 * head + 1, nx - 1)
        up.start()
        down.start()
        cleanup.extend((up.wait_send, down.wait_send))

    ring_start(0)

    each(1, nb, lambda k: list_copy(k, bal_of(k)).wait_recv())
    table = lists[...].reshape(nb, LANES).astype(F32)
    counts = table[:, :nb]
    sub_n, lane_n = iota((nb, nb), 0), iota((nb, nb), 1)
    source = x * ny + lane_n // entries
    rank = jnp.sum(jnp.where(sub_n < source, counts, 0.0), axis=0, keepdims=True).astype(jnp.int32)
    known = jnp.sum(jnp.where(sub_n == source, counts, 0.0), axis=0, keepdims=True).astype(jnp.int32)
    entry = iota((1, nb), 1) % entries
    slots = nb // nx
    wanted = (sub_n % slots) * nx + sub_n // slots
    sel = (rank + entry == wanted) & (entry < known)
    sel = sel.astype(F32).astype(BF16)

    near = (iota((BLOCK, nb), 1) == iota((BLOCK, nb), 0) * ny + y) & (iota((BLOCK, nb), 0) < nx)
    named[u] = dot(near.astype(F32).astype(BF16), table.astype(BF16))

    def name_copy(k, slot):
        return remote(named.at[u], named.at[slot], name_s.at[k], name_r.at[slot], z_dev(k))

    each(1, nu, lambda k: name_copy(k, u).start())
    cleanup.append(lambda: each(1, nu, lambda k: name_copy(k, u).wait_send()))
    each(1, ny, lambda k: p1_copy(k, y_of(k)).wait_recv())
    stage[...] = in1[...].astype(F32).reshape(stage.shape)
    for j in range(pieces):
        part = dot(sel, stage[:, j, :].astype(BF16)).astype(BF16)
        for k in range(nx):
            outx[k, :, j * LANES : (j + 1) * LANES] = part[k * slots : (k + 1) * slots, :]

    def px_copy(k, slot):
        to = x_of(k)
        return remote(outx.at[to], inx.at[slot], px_s.at[k], px_r.at[slot], (to * ny + y, u, c))

    each(1, nx, lambda k: px_copy(k, x).start())
    cleanup.append(lambda: each(1, nx, lambda k: px_copy(k, x).wait_send()))
    inx[x] = outx[x]

    ring_start(1)

    each(1, nx, lambda k: px_copy(k, x_of(k)).wait_recv())
    gathered = inx[0].astype(F32)
    for k in range(1, nx):
        gathered = gathered + inx[k].astype(F32)
    xbuf[u] = gathered.astype(BF16)

    def z_copy(k, slot):
        return remote(xbuf.at[u], xbuf.at[slot], z_s.at[k], z_r.at[slot], z_dev(k))

    order = []
    for k in range(nu // 2, 0, -1):
        order += [k] if 2 * k == nu else [k, nu - k]
    for k in order:
        z_copy(k, u).start()
    cleanup.append(lambda: each(1, nu, lambda k: z_copy(k, u).wait_send()))

    span = nx * keys
    owner_hit = (iota((keys, nu), 0) // toks == iota((keys, nu), 1)).astype(F32).astype(BF16)
    block_hit = (iota((keys, LANES), 0) % toks) // BLOCK == iota((keys, LANES), 1)
    ones = jnp.ones((LANES, LANES), BF16)
    lane_u = iota((nu, LANES), 1).astype(F32)

    def weigh_values(k):
        ids = named[:, pl.ds(k, 1), :].reshape(nu, LANES)
        hit = jnp.zeros((nu, LANES), F32)
        for j in range(LANES - entries, LANES):
            hit = hit + (ids[:, j : j + 1] == lane_u).astype(F32)
        spread = jnp.where(block_hit, dot(owner_hit, hit.astype(BF16)), 0.0).astype(BF16)
        mask = 1.0 - dot(spread, ones)
        rows = pl.ds(pl.multiple_of(k * keys, keys), keys)
        for h in range(2):
            vaug[h, rows, :HEAD_DIM] = (kv[k, h, 1].astype(F32) * mask).astype(BF16)
            vaug[h, rows, HEAD_DIM:] = mask.astype(BF16)

    each(1, nu, lambda k: name_copy(k, lax.rem(u + k, nu)).wait_recv())
    weigh_values(x)

    on_up, on_down = ring(prev_x, 0, 4, 1), ring(next_x, 1, 5, nx - 1)
    ring(prev_x, 0, 0, 1).wait_recv()
    on_up.start()
    ring(next_x, 1, 2, 1).wait_recv()
    on_down.start()
    cleanup.extend((on_up.wait_send, on_down.wait_send))
    ring(prev_x, 1, 2, 1).wait_recv()
    ring(next_x, 0, 0, 1).wait_recv()
    weigh_values(prev_x)
    weigh_values(next_x)
    w_out.wait_recv()
    gain_load.wait()

    each(1, nu, lambda k: z_copy(k, lax.rem(u + k, nu)).wait_recv())
    chunk = math.gcd(width, 1024)
    projected = [jnp.zeros((half, 3 * HEAD_DIM), F32)] * 2
    for j in range(0, width, chunk):
        rows = xbuf[:, :, j : j + chunk].astype(F32).reshape(half, chunk).astype(BF16)
        projected = [projected[h] + dot(rows, w_buf[h, j : j + chunk, :]) for h in range(2)]
    for h in range(2):
        mine = slice(h * half, (h + 1) * half)
        query = normalize(projected[h][:, :HEAD_DIM]) * gain_ref[h : h + 1, :]
        qbuf[y, mine, :] = query.astype(BF16)

    def q_copy(k, slot):
        return remote(qbuf.at[y], qbuf.at[slot], q_s.at[k], q_r.at[slot], y_dev(k))

    def kf_copy(k, slot):
        return remote(kvf.at[x], kvf.at[slot], kf_s.at[k], kf_r.at[slot], x_dev(k))

    for k in range(1, ny // 2 + 1):
        for way in [k] if 2 * k == ny else [k, ny - k]:
            q_copy(way, y).start()
    for h in range(2):
        mine = slice(h * half, (h + 1) * half)
        k_fresh = projected[h][:, HEAD_DIM : 2 * HEAD_DIM].astype(BF16).astype(F32)
        kvf[x, 0, mine, :] = normalize(k_fresh).astype(BF16)
        kvf[x, 1, mine, :] = projected[h][:, 2 * HEAD_DIM :].astype(BF16)
    each(1, nx, lambda k: kf_copy(k, x).start())
    cleanup.append(lambda: each(1, ny, lambda k: q_copy(k, y).wait_send()))
    cleanup.append(lambda: each(1, nx, lambda k: kf_copy(k, x).wait_send()))

    ring(far_x, 0, 4, 1).wait_recv()
    ring(far_x, 1, 5, nx - 1).wait_recv()
    weigh_values(far_x)

    each(1, nx, lambda k: kf_copy(k, lax.rem(x + k, nx)).wait_recv())
    fresh_keys = nx * half
    for h in range(2):
        mine = slice(h * half, (h + 1) * half)
        vaug[h, span:, :HEAD_DIM] = kvf[:, 1, mine, :].reshape(fresh_keys, HEAD_DIM)
        vaug[h, span:, HEAD_DIM:] = jnp.ones((fresh_keys, HEAD_DIM), BF16)
    factor = 1.0 / math.sqrt(HEAD_DIM)

    def weigh(queries, some_keys):
        return jnp.exp(dot_t(queries, some_keys) * factor).astype(BF16)

    def rs_copy(k, slot):
        to = lax.rem(y + k, ny)
        return remote(rsout.at[to], rsin.at[slot], rs_s.at[k], rs_r.at[slot], y_dev(k))

    def attend(i):
        way_a, way_b = lax.rem(ny - i, ny), i + 1
        slot_a, slot_b = lax.rem(y + way_a, ny), lax.rem(y + way_b, ny)

        @pl.when(i > 0)
        def _():
            q_copy(way_a, slot_a).wait_recv()

        q_copy(way_b, slot_b).wait_recv()
        flat_a = jnp.zeros((1, LANES), F32)
        flat_b = jnp.zeros((1, LANES), F32)
        for h in range(2):
            mine = slice(h * half, (h + 1) * half)
            queries = jnp.concatenate([qbuf[slot_a, mine, :], qbuf[slot_b, mine, :]], axis=0)
            k_last = kvf[:, 0, mine, :].reshape(fresh_keys, HEAD_DIM)
            got = dot(weigh(queries, k_last), vaug[h, span:, :])
            for k in range(nx):
                got = got + dot(weigh(queries, kv[k, h, 0]), vaug[h, k * keys : (k + 1) * keys, :])
            rsout[slot_a, mine, :] = got[:half, :HEAD_DIM].astype(BF16)
            rsout[slot_b, mine, :] = got[half:, :HEAD_DIM].astype(BF16)
            place = iota((half, LANES), 1) == iota((half, LANES), 0) + h * half
            flat_a = flat_a + jnp.sum(jnp.where(place, got[:half, HEAD_DIM:], 0.0), axis=0, keepdims=True)
            flat_b = flat_b + jnp.sum(jnp.where(place, got[half:, HEAD_DIM:], 0.0), axis=0, keepdims=True)
        tail = rsout.shape[1] - 2 * half
        tail_row = iota((tail, LANES), 0)
        for slot, flat in ((slot_a, flat_a), (slot_b, flat_b)):
            coarse = flat.astype(BF16).astype(F32)
            rest = jnp.where(tail_row == 1, flat - coarse, 0.0)
            rsout[slot, 2 * half :, :] = jnp.where(tail_row == 0, coarse, rest).astype(BF16)

        @pl.when(i > 0)
        def _():
            rs_copy(way_a, y).start()

        rs_copy(way_b, y).start()

    each(0, ny // 2, attend)
    cleanup.append(lambda: each(1, ny, lambda k: rs_copy(k, y).wait_send()))
    rsin[y] = rsout[y]

    each(1, ny, lambda k: rs_copy(k, lax.rem(y + k, ny)).wait_recv())
    summed = jnp.sum(rsin[...].astype(F32), axis=0)
    total = summed[2 * half : 2 * half + 1, :] + summed[2 * half + 1 : 2 * half + 2, :]
    square = iota((2 * half, LANES), 0) == iota((2 * half, LANES), 1)
    total = jnp.sum(jnp.where(square, total, 0.0), axis=1, keepdims=True)
    attended = summed[: 2 * half, :] / total
    for h in range(2):
        rows = attended[h * half : (h + 1) * half, :]
        ret_out[:, h] = rows.reshape(nu, BLOCK, HEAD_DIM).astype(BF16)

    def ret_copy(k, slot):
        to = lax.rem(u + k, nu)
        return remote(ret_out.at[to], ret1.at[slot], ret_s.at[k], ret_r.at[slot], z_dev(k))

    each(1, nu, lambda k: ret_copy(k, u).start())
    cleanup.append(lambda: each(1, nu, lambda k: ret_copy(k, u).wait_send()))
    ret1[u] = ret_out[u]
    count_row = jnp.sum(jnp.where(sub_n == lane_n, counts, 0.0), axis=0, keepdims=True)
    start_col = jnp.sum(jnp.where(lane_n < sub_n, count_row, 0.0), axis=1, keepdims=True).astype(jnp.int32)
    rank_col = start_col + jnp.bitwise_and(x - start_col, nx - 1)
    give = rank_col < start_col + counts[:, :slots].astype(jnp.int32)
    give = give & (rank_col // nx == iota((nb, slots), 1))
    give = give.astype(F32).astype(BF16)
    each(1, nu, lambda k: ret_copy(k, lax.rem(u + k, nu)).wait_recv())
    for h in range(nh):
        stage2[:, h, :] = dot(give, ret1[h // 2, h % 2])
    out2[...] = stage2[...].astype(BF16)

    def back_copy(k, slot):
        to = bal_of(k)
        return remote(out2.at[to], in2.at[slot], back_s.at[k], back_r.at[slot], (to, u, c))

    each(1, nb, lambda k: back_copy(k, b).start())
    cleanup.append(lambda: each(1, nb, lambda k: back_copy(k, b).wait_send()))
    in2[b] = out2[b]
    my_start = jnp.sum(jnp.where(sub_n < b, counts, 0.0), axis=0, keepdims=True).astype(jnp.int32)
    from_x = jnp.bitwise_and(my_start + sub_n // BLOCK, nx - 1)
    final = (from_x * ny + sub_n % BLOCK == lane_n) & (sub_n // BLOCK < my_blocks)
    final = final.astype(F32).astype(BF16)
    each(1, nb, lambda k: back_copy(k, bal_of(k)).wait_recv())
    stage2[...] = in2[...].astype(F32)
    for h in range(nh):
        out_ref[:, h * HEAD_DIM : (h + 1) * HEAD_DIM] = dot(final, stage2[:, h, :].astype(BF16)).astype(BF16)

    for finish in cleanup:
        finish()


def on_device(hidden, w_qkv, q_gain, cache_k, cache_v, fresh_list):
    nb, nu = lax.axis_size("bal"), lax.axis_size("uly")
    nx = SIDE_X
    ny = nb // nx
    toks, width = hidden.shape[1:]
    keys = cache_k.shape[1]
    entries = fresh_list.shape[3]
    half = nu * BLOCK
    nh = 2 * nu
    pieces = width // LANES
    span = nx * (keys + half)
    vmem = pl.BlockSpec(memory_space=pltpu.VMEM)
    dma = pltpu.SemaphoreType.DMA
    out = pl.pallas_call(
        functools.partial(kernel, nx, nu),
        out_shape=jax.ShapeDtypeStruct((entries * BLOCK, nh * HEAD_DIM), BF16),
        in_specs=[
            *[pl.BlockSpec(memory_space=pltpu.HBM)] * 6,
        ],
        out_specs=vmem,
        scratch_shapes=[
            pltpu.SMEM((entries,), jnp.int32),
            pltpu.VMEM((toks, width), BF16),
            pltpu.VMEM((2, *w_qkv.shape), BF16),
            pltpu.VMEM((2, HEAD_DIM), F32),
            pltpu.VMEM((keys, 2 * HEAD_DIM), BF16),
            pltpu.VMEM((keys, 2 * HEAD_DIM), BF16),
            pltpu.VMEM((nb, 1, LANES), jnp.int32),
            pltpu.VMEM((nu, BLOCK, LANES), F32),
            pltpu.VMEM((nb, pieces, LANES), F32),
            pltpu.VMEM((ny, entries, pieces, LANES), BF16),
            pltpu.VMEM((ny, entries, pieces, LANES), BF16),
            pltpu.VMEM((nx, nb // nx, width), BF16),
            pltpu.VMEM((nx, nb // nx, width), BF16),
            pltpu.VMEM((nu, nb // nx, width), BF16),
            pltpu.VMEM((nx, 2, 2, keys, HEAD_DIM), BF16),
            pltpu.VMEM((ny, 2 * half, HEAD_DIM), BF16),
            pltpu.VMEM((nx, 2, 2 * half, HEAD_DIM), BF16),
            pltpu.VMEM((2, span, 2 * HEAD_DIM), BF16),
            pltpu.VMEM((ny, 2 * half + 16, HEAD_DIM), BF16),
            pltpu.VMEM((ny, 2 * half + 16, HEAD_DIM), BF16),
            pltpu.VMEM((nu, 2, BLOCK, HEAD_DIM), BF16),
            pltpu.VMEM((nu, 2, BLOCK, HEAD_DIM), BF16),
            pltpu.VMEM((nb, nh, HEAD_DIM), F32),
            pltpu.VMEM((nb, nh, HEAD_DIM), BF16),
            pltpu.VMEM((nb, nh, HEAD_DIM), BF16),
            dma((6,)),
            dma, dma,
            dma((nb,)), dma((nb,)),
            dma((nu,)), dma((nu,)),
            dma((ny,)), dma((ny,)),
            dma((nx,)), dma((nx,)),
            dma((nu,)), dma((nu,)),
            dma((6,)), dma((nx, 2)),
            dma((ny,)), dma((ny,)),
            dma((nx,)), dma((nx,)),
            dma((ny,)), dma((ny,)),
            dma((nu,)), dma((nu,)),
            dma((nb,)), dma((nb,)),
        ],
        compiler_params=pltpu.CompilerParams(
            collective_id=0, has_side_effects=True, vmem_limit_bytes=63 * 1024 * 1024
        ),
    )(
        fresh_list.reshape(entries),
        hidden.reshape(toks, width),
        w_qkv,
        q_gain.reshape(2, HEAD_DIM),
        cache_k.reshape(keys, 2 * HEAD_DIM),
        cache_v.reshape(keys, 2 * HEAD_DIM),
    )
    return out.reshape(1, 1, 1, entries * BLOCK, nh * HEAD_DIM)


def solution(mesh):
    in_specs = (
        P("cfg", ("bal", "uly"), None),
        P(None, ("uly", "cfg")),
        P("uly"),
        P("cfg", "bal", "uly"),
        P("cfg", "bal", "uly"),
        P("cfg", "bal", "uly", None),
    )
    out_specs = P("cfg", "bal", "uly", None, None)
    return jax.shard_map(
        on_device, mesh=mesh, in_specs=in_specs, out_specs=out_specs, check_vma=False
    )
```

```python
import functools
import math

import jax
import jax.numpy as jnp
from jax import lax
from jax.experimental import pallas as pl
from jax.experimental.pallas import tpu as pltpu
from jax.sharding import PartitionSpec as P

HEAD_DIM = 128
BLOCK = 8
SIDE_X = 4
LANES = 128
MESH = pl.DeviceIdType.MESH
F32 = jnp.float32
BF16 = jnp.bfloat16


def normalize(values):
    return values * lax.rsqrt(jnp.mean(values * values, axis=-1, keepdims=True) + 1e-06)


def iota(shape, dim):
    return lax.broadcasted_iota(jnp.int32, shape, dim)


def dot(a, b):
    return jnp.dot(a, b, preferred_element_type=F32)


def dot_t(a, b):
    return lax.dot_general(a, b, (((1,), (1,)), ((), ())), preferred_element_type=F32)


def kernel(
    nx, nu, list_in, hidden_in, w_in, gain_in, ck_in, cv_in, out_ref,
    list_ref, hidden_ref, w_buf, gain_ref, ck_ref, cv_ref, lists, named, stage, out1, in1, outx, inx, xbuf, kv, qbuf, kvf,
    vaug, rsout, rsin, ret_out, ret1, stage2, out2, in2,
    in_sem, w_s, w_r, list_s, list_r, name_s, name_r, p1_s, p1_r, px_s, px_r, z_s, z_r, opp_s, opp_r, kv_s, kv_r, q_s, q_r, kf_s, kf_r, rs_s, rs_r,
    ret_s, ret_r, back_s, back_r,
):
    b, u, c = lax.axis_index("bal"), lax.axis_index("uly"), lax.axis_index("cfg")
    nb, width = lists.shape[0], hidden_ref.shape[1]
    ny = nb // nx
    x, y = b // ny, b % ny
    toks = hidden_ref.shape[0]
    blocks = toks // BLOCK
    entries = list_ref.shape[0]
    keys = ck_ref.shape[0]
    half = nu * BLOCK
    pieces = width // LANES
    nh = 2 * nu
    other = 1 - c

    def farthest(j, n):
        step = (j + 1) // 2
        return lax.rem(n // 2 + n + jnp.where(lax.rem(j, 2) == 1, step, -step), n)

    def x_of(k):
        return lax.rem(x + farthest(k - 1, nx), nx)

    def y_of(k):
        return lax.rem(y + farthest(k - 1, ny), ny)

    def bal_of(k):
        return x_of(lax.rem(k - 1, nx) + 1) * ny + y_of((k - 1) // nx + 1)

    def bal_dev(k):
        return (bal_of(k), u, c)

    def x_dev(k):
        return (lax.rem(x + k, nx) * ny + y, u, c)

    def y_dev(k):
        return (x * ny + lax.rem(y + k, ny), u, c)

    def z_dev(k):
        return (b, lax.rem(u + k, nu), c)

    def remote(src, dst, s, r, dev):
        return pltpu.make_async_remote_copy(
            src_ref=src, dst_ref=dst, send_sem=s, recv_sem=r, device_id=dev, device_id_type=MESH
        )

    def each(lo, hi, body):
        lax.fori_loop(lo, hi, lambda i, z: (body(i), z)[1], 0)

    pairs = (
        (list_in, list_ref),
        (ck_in, ck_ref),
        (cv_in, cv_ref),
        (w_in, w_buf.at[c]),
        (hidden_in, hidden_ref),
        (gain_in, gain_ref),
    )
    loads = tuple(
        pltpu.make_async_copy(src, dst, in_sem.at[i]) for i, (src, dst) in enumerate(pairs)
    )
    for load in loads:
        load.start()
    list_load, k_load, v_load, w_load, hidden_load, gain_load = loads
    cleanup = []

    barrier = pltpu.get_barrier_semaphore()

    def greet(dev):
        pl.semaphore_signal(barrier, inc=1, device_id=dev, device_id_type=MESH)

    each(1, nb, lambda k: greet(bal_dev(k)))
    each(1, nu, lambda k: greet(z_dev(k)))
    greet((b, u, other))

    list_load.wait()
    my_blocks = 0
    for j in range(entries):
        my_blocks = my_blocks + jnp.where(list_ref[j] < blocks, 1, 0)
    lane = iota((1, LANES), 1)
    row = jnp.zeros((1, LANES), jnp.int32) + my_blocks
    for j in range(entries):
        row = jnp.where(lane == LANES - entries + j, list_ref[j], row)
    lists[b] = row

    hidden_load.wait()
    token = jnp.zeros((nb, toks), jnp.int32)
    for j in range(entries):
        token = jnp.where(iota((nb, toks), 0) % entries == j, list_ref[j], token)
    token = token * BLOCK + iota((nb, toks), 0) // entries
    pick = (token == iota((nb, toks), 1)).astype(F32).astype(BF16)
    for j in range(pieces):
        stage[:, j, :] = dot(pick, hidden_ref[:, j * LANES : (j + 1) * LANES])
    out1[...] = stage[...].astype(BF16).reshape(out1.shape)

    k_load.wait()
    v_load.wait()
    for head in range(2):
        columns = slice(head * HEAD_DIM, (head + 1) * HEAD_DIM)
        kv[x, head, 0] = normalize(ck_ref[:, columns].astype(F32)).astype(BF16)
        kv[x, head, 1] = cv_ref[:, columns]
    w_load.wait()

    pl.semaphore_wait(barrier, nb - 1 + nu - 1 + 1)

    def list_copy(k, slot):
        return remote(lists.at[b], lists.at[slot], list_s.at[k], list_r.at[slot], bal_dev(k))

    each(1, nb, lambda k: list_copy(k, b).start())
    cleanup.append(lambda: each(1, nb, lambda k: list_copy(k, b).wait_send()))

    def p1_copy(k, slot):
        to = y_of(k)
        dev = (x * ny + to, u, c)
        return remote(out1.at[to], in1.at[slot], p1_s.at[k], p1_r.at[slot], dev)

    each(1, ny, lambda k: p1_copy(k, y).start())
    cleanup.append(lambda: each(1, ny, lambda k: p1_copy(k, y).wait_send()))
    in1[y] = out1[y]

    w_out = remote(w_buf.at[c], w_buf.at[c], w_s, w_r, (b, u, other))
    w_out.start()
    cleanup.append(w_out.wait_send)

    prev_x, next_x, far_x = lax.rem(x + nx - 1, nx), lax.rem(x + 1, nx), lax.rem(x + nx // 2, nx)

    def ring(slot_x, head, s, way):
        part = kv.at[slot_x, head]
        return remote(part, part, kv_s.at[s], kv_r.at[slot_x, head], x_dev(way))

    def ring_start(head):
        up, down = ring(x, head, 2 * head, 1), ring(x, head, 2 * head + 1, nx - 1)
        up.start()
        down.start()
        cleanup.extend((up.wait_send, down.wait_send))

    ring_start(0)

    each(1, nb, lambda k: list_copy(k, bal_of(k)).wait_recv())
    table = lists[...].reshape(nb, LANES).astype(F32)
    counts = table[:, :nb]
    sub_n, lane_n = iota((nb, nb), 0), iota((nb, nb), 1)
    source = x * ny + lane_n // entries
    rank = jnp.sum(jnp.where(sub_n < source, counts, 0.0), axis=0, keepdims=True).astype(jnp.int32)
    known = jnp.sum(jnp.where(sub_n == source, counts, 0.0), axis=0, keepdims=True).astype(jnp.int32)
    entry = iota((1, nb), 1) % entries
    slots = nb // nx
    wanted = (sub_n % slots) * nx + sub_n // slots
    sel = (rank + entry == wanted) & (entry < known)
    sel = sel.astype(F32).astype(BF16)

    near = (iota((BLOCK, nb), 1) == iota((BLOCK, nb), 0) * ny + y) & (iota((BLOCK, nb), 0) < nx)
    named[u] = dot(near.astype(F32).astype(BF16), table.astype(BF16))

    def name_copy(k, slot):
        return remote(named.at[u], named.at[slot], name_s.at[k], name_r.at[slot], z_dev(k))

    each(1, nu, lambda k: name_copy(k, u).start())
    cleanup.append(lambda: each(1, nu, lambda k: name_copy(k, u).wait_send()))
    each(1, ny, lambda k: p1_copy(k, y_of(k)).wait_recv())
    stage[...] = in1[...].astype(F32).reshape(stage.shape)
    for j in range(pieces):
        part = dot(sel, stage[:, j, :].astype(BF16)).astype(BF16)
        for k in range(nx):
            outx[k, :, j * LANES : (j + 1) * LANES] = part[k * slots : (k + 1) * slots, :]

    def px_copy(k, slot):
        to = x_of(k)
        return remote(outx.at[to], inx.at[slot], px_s.at[k], px_r.at[slot], (to * ny + y, u, c))

    each(1, nx, lambda k: px_copy(k, x).start())
    cleanup.append(lambda: each(1, nx, lambda k: px_copy(k, x).wait_send()))
    inx[x] = outx[x]

    ring_start(1)

    each(1, nx, lambda k: px_copy(k, x_of(k)).wait_recv())
    gathered = inx[0].astype(F32)
    for k in range(1, nx):
        gathered = gathered + inx[k].astype(F32)
    xbuf[u] = gathered.astype(BF16)

    def z_copy(k, slot):
        return remote(xbuf.at[u], xbuf.at[slot], z_s.at[k], z_r.at[slot], z_dev(k))

    far = nu // 2
    order = [far - 1, far + 1, 2, nu - 2, 1, nu - 1]
    for k in order:
        z_copy(k, u).start()
        cleanup.append(z_copy(k, u).wait_send)

    def opposite_copy(side, slot):
        part = xbuf.at[slot, :, pl.ds(side * (width // 2), width // 2)]
        return remote(part, part, opp_s.at[side], opp_r.at[side], z_dev(1 if side == 0 else nu - 1))

    span = nx * keys
    owner_hit = (iota((keys, nu), 0) // toks == iota((keys, nu), 1)).astype(F32).astype(BF16)
    block_hit = (iota((keys, LANES), 0) % toks) // BLOCK == iota((keys, LANES), 1)
    ones = jnp.ones((LANES, LANES), BF16)
    lane_u = iota((nu, LANES), 1).astype(F32)

    def weigh_values(k):
        ids = named[:, pl.ds(k, 1), :].reshape(nu, LANES)
        hit = jnp.zeros((nu, LANES), F32)
        for j in range(LANES - entries, LANES):
            hit = hit + (ids[:, j : j + 1] == lane_u).astype(F32)
        spread = jnp.where(block_hit, dot(owner_hit, hit.astype(BF16)), 0.0).astype(BF16)
        mask = 1.0 - dot(spread, ones)
        rows = pl.ds(pl.multiple_of(k * keys, keys), keys)
        for h in range(2):
            vaug[h, rows, :HEAD_DIM] = (kv[k, h, 1].astype(F32) * mask).astype(BF16)
            vaug[h, rows, HEAD_DIM:] = mask.astype(BF16)

    each(1, nu, lambda k: name_copy(k, lax.rem(u + k, nu)).wait_recv())
    weigh_values(x)

    on_up, on_down = ring(prev_x, 0, 4, 1), ring(next_x, 1, 5, nx - 1)
    cleanup.extend((on_up.wait_send, on_down.wait_send))
    ring(prev_x, 0, 0, 1).wait_recv()
    on_up.start()
    for side, k in enumerate((far + 1, far - 1)):
        slot = lax.rem(u + k, nu)
        z_copy(k, slot).wait_recv()
        opposite_copy(side, slot).start()
        cleanup.append(opposite_copy(side, slot).wait_send)
    ring(next_x, 1, 2, 1).wait_recv()
    on_down.start()
    ring(prev_x, 1, 2, 1).wait_recv()
    ring(next_x, 0, 0, 1).wait_recv()
    weigh_values(prev_x)
    weigh_values(next_x)
    w_out.wait_recv()
    gain_load.wait()

    for k in order[2:]:
        z_copy(k, lax.rem(u + k, nu)).wait_recv()
    for side in range(2):
        opposite_copy(side, lax.rem(u + far, nu)).wait_recv()
    chunk = math.gcd(width, 1024)
    projected = [jnp.zeros((half, 3 * HEAD_DIM), F32)] * 2
    for j in range(0, width, chunk):
        rows = xbuf[:, :, j : j + chunk].astype(F32).reshape(half, chunk).astype(BF16)
        projected = [projected[h] + dot(rows, w_buf[h, j : j + chunk, :]) for h in range(2)]
    for h in range(2):
        mine = slice(h * half, (h + 1) * half)
        query = normalize(projected[h][:, :HEAD_DIM]) * gain_ref[h : h + 1, :]
        qbuf[y, mine, :] = query.astype(BF16)

    def q_copy(k, slot):
        return remote(qbuf.at[y], qbuf.at[slot], q_s.at[k], q_r.at[slot], y_dev(k))

    def kf_copy(k, slot):
        return remote(kvf.at[x], kvf.at[slot], kf_s.at[k], kf_r.at[slot], x_dev(k))

    for k in range(ny // 2, 0, -1):
        for way in [k] if 2 * k == ny else [k, ny - k]:
            q_copy(way, y).start()
    for h in range(2):
        mine = slice(h * half, (h + 1) * half)
        k_fresh = projected[h][:, HEAD_DIM : 2 * HEAD_DIM].astype(BF16).astype(F32)
        kvf[x, 0, mine, :] = normalize(k_fresh).astype(BF16)
        kvf[x, 1, mine, :] = projected[h][:, 2 * HEAD_DIM :].astype(BF16)
    each(1, nx, lambda k: kf_copy(k, x).start())
    cleanup.append(lambda: each(1, ny, lambda k: q_copy(k, y).wait_send()))
    cleanup.append(lambda: each(1, nx, lambda k: kf_copy(k, x).wait_send()))

    ring(far_x, 0, 4, 1).wait_recv()
    ring(far_x, 1, 5, nx - 1).wait_recv()
    weigh_values(far_x)

    each(1, nx, lambda k: kf_copy(k, lax.rem(x + k, nx)).wait_recv())
    fresh_keys = nx * half
    for h in range(2):
        mine = slice(h * half, (h + 1) * half)
        vaug[h, span:, :HEAD_DIM] = kvf[:, 1, mine, :].reshape(fresh_keys, HEAD_DIM)
        vaug[h, span:, HEAD_DIM:] = jnp.ones((fresh_keys, HEAD_DIM), BF16)
    factor = 1.0 / math.sqrt(HEAD_DIM)

    def weigh(queries, some_keys):
        return jnp.exp(dot_t(queries, some_keys) * factor).astype(BF16)

    def rs_copy(k, slot):
        to = lax.rem(y + k, ny)
        return remote(rsout.at[to], rsin.at[slot], rs_s.at[k], rs_r.at[slot], y_dev(k))

    def attend(i):
        step = ny // 2 - 1 - i
        last = step == ny // 2 - 1
        way_a, way_b = step + 1, jnp.where(last, 0, ny - 1 - step)
        slot_a, slot_b = lax.rem(y + way_a, ny), lax.rem(y + way_b, ny)

        q_copy(way_a, slot_a).wait_recv()

        @pl.when(jnp.logical_not(last))
        def _():
            q_copy(way_b, slot_b).wait_recv()

        flat_a = jnp.zeros((1, LANES), F32)
        flat_b = jnp.zeros((1, LANES), F32)
        for h in range(2):
            mine = slice(h * half, (h + 1) * half)
            queries = jnp.concatenate([qbuf[slot_a, mine, :], qbuf[slot_b, mine, :]], axis=0)
            k_last = kvf[:, 0, mine, :].reshape(fresh_keys, HEAD_DIM)
            got = dot(weigh(queries, k_last), vaug[h, span:, :])
            for k in range(nx):
                got = got + dot(weigh(queries, kv[k, h, 0]), vaug[h, k * keys : (k + 1) * keys, :])
            rsout[slot_a, mine, :] = got[:half, :HEAD_DIM].astype(BF16)
            rsout[slot_b, mine, :] = got[half:, :HEAD_DIM].astype(BF16)
            place = iota((half, LANES), 1) == iota((half, LANES), 0) + h * half
            flat_a = flat_a + jnp.sum(jnp.where(place, got[:half, HEAD_DIM:], 0.0), axis=0, keepdims=True)
            flat_b = flat_b + jnp.sum(jnp.where(place, got[half:, HEAD_DIM:], 0.0), axis=0, keepdims=True)
        tail = rsout.shape[1] - 2 * half
        tail_row = iota((tail, LANES), 0)
        for slot, flat in ((slot_a, flat_a), (slot_b, flat_b)):
            coarse = flat.astype(BF16).astype(F32)
            rest = jnp.where(tail_row == 1, flat - coarse, 0.0)
            rsout[slot, 2 * half :, :] = jnp.where(tail_row == 0, coarse, rest).astype(BF16)

        rs_copy(way_a, y).start()

        @pl.when(jnp.logical_not(last))
        def _():
            rs_copy(way_b, y).start()

    each(0, ny // 2, attend)
    cleanup.append(lambda: each(1, ny, lambda k: rs_copy(k, y).wait_send()))

    summed = rsout[y].astype(F32)
    for k in range(1, ny // 2 + 1):
        for way in [k] if 2 * k == ny else [k, ny - k]:
            slot = lax.rem(y + way, ny)
            rs_copy(way, slot).wait_recv()
            summed = summed + rsin[slot].astype(F32)
    total = summed[2 * half : 2 * half + 1, :] + summed[2 * half + 1 : 2 * half + 2, :]
    square = iota((2 * half, LANES), 0) == iota((2 * half, LANES), 1)
    total = jnp.sum(jnp.where(square, total, 0.0), axis=1, keepdims=True)
    attended = summed[: 2 * half, :] / total
    for h in range(2):
        rows = attended[h * half : (h + 1) * half, :]
        ret_out[:, h] = rows.reshape(nu, BLOCK, HEAD_DIM).astype(BF16)

    def ret_copy(k, slot):
        to = lax.rem(u + k, nu)
        return remote(ret_out.at[to], ret1.at[slot], ret_s.at[k], ret_r.at[slot], z_dev(k))

    each(1, nu, lambda k: ret_copy(k, u).start())
    cleanup.append(lambda: each(1, nu, lambda k: ret_copy(k, u).wait_send()))
    ret1[u] = ret_out[u]
    count_row = jnp.sum(jnp.where(sub_n == lane_n, counts, 0.0), axis=0, keepdims=True)
    start_col = jnp.sum(jnp.where(lane_n < sub_n, count_row, 0.0), axis=1, keepdims=True).astype(jnp.int32)
    rank_col = start_col + jnp.bitwise_and(x - start_col, nx - 1)
    give = rank_col < start_col + counts[:, :slots].astype(jnp.int32)
    give = give & (rank_col // nx == iota((nb, slots), 1))
    give = give.astype(F32).astype(BF16)
    each(1, nu, lambda k: ret_copy(k, lax.rem(u + k, nu)).wait_recv())
    for h in range(nh):
        stage2[:, h, :] = dot(give, ret1[h // 2, h % 2])
    out2[...] = stage2[...].astype(BF16)

    def back_copy(k, slot):
        to = bal_of(k)
        return remote(out2.at[to], in2.at[slot], back_s.at[k], back_r.at[slot], (to, u, c))

    each(1, nb, lambda k: back_copy(k, b).start())
    cleanup.append(lambda: each(1, nb, lambda k: back_copy(k, b).wait_send()))
    in2[b] = out2[b]
    my_start = jnp.sum(jnp.where(sub_n < b, counts, 0.0), axis=0, keepdims=True).astype(jnp.int32)
    from_x = jnp.bitwise_and(my_start + sub_n // BLOCK, nx - 1)
    final = (from_x * ny + sub_n % BLOCK == lane_n) & (sub_n // BLOCK < my_blocks)
    final = final.astype(F32).astype(BF16)
    each(1, nb, lambda k: back_copy(k, bal_of(k)).wait_recv())
    stage2[...] = in2[...].astype(F32)
    for h in range(nh):
        out_ref[:, h * HEAD_DIM : (h + 1) * HEAD_DIM] = dot(final, stage2[:, h, :].astype(BF16)).astype(BF16)

    for finish in cleanup:
        finish()


def on_device(hidden, w_qkv, q_gain, cache_k, cache_v, fresh_list):
    nb, nu = lax.axis_size("bal"), lax.axis_size("uly")
    nx = SIDE_X
    ny = nb // nx
    toks, width = hidden.shape[1:]
    keys = cache_k.shape[1]
    entries = fresh_list.shape[3]
    half = nu * BLOCK
    nh = 2 * nu
    pieces = width // LANES
    span = nx * (keys + half)
    vmem = pl.BlockSpec(memory_space=pltpu.VMEM)
    dma = pltpu.SemaphoreType.DMA
    out = pl.pallas_call(
        functools.partial(kernel, nx, nu),
        out_shape=jax.ShapeDtypeStruct((entries * BLOCK, nh * HEAD_DIM), BF16),
        in_specs=[
            *[pl.BlockSpec(memory_space=pltpu.HBM)] * 6,
        ],
        out_specs=vmem,
        scratch_shapes=[
            pltpu.SMEM((entries,), jnp.int32),
            pltpu.VMEM((toks, width), BF16),
            pltpu.VMEM((2, *w_qkv.shape), BF16),
            pltpu.VMEM((2, HEAD_DIM), F32),
            pltpu.VMEM((keys, 2 * HEAD_DIM), BF16),
            pltpu.VMEM((keys, 2 * HEAD_DIM), BF16),
            pltpu.VMEM((nb, 1, LANES), jnp.int32),
            pltpu.VMEM((nu, BLOCK, LANES), F32),
            pltpu.VMEM((nb, pieces, LANES), F32),
            pltpu.VMEM((ny, entries, pieces, LANES), BF16),
            pltpu.VMEM((ny, entries, pieces, LANES), BF16),
            pltpu.VMEM((nx, nb // nx, width), BF16),
            pltpu.VMEM((nx, nb // nx, width), BF16),
            pltpu.VMEM((nu, nb // nx, width), BF16),
            pltpu.VMEM((nx, 2, 2, keys, HEAD_DIM), BF16),
            pltpu.VMEM((ny, 2 * half, HEAD_DIM), BF16),
            pltpu.VMEM((nx, 2, 2 * half, HEAD_DIM), BF16),
            pltpu.VMEM((2, span, 2 * HEAD_DIM), BF16),
            pltpu.VMEM((ny, 2 * half + 16, HEAD_DIM), BF16),
            pltpu.VMEM((ny, 2 * half + 16, HEAD_DIM), BF16),
            pltpu.VMEM((nu, 2, BLOCK, HEAD_DIM), BF16),
            pltpu.VMEM((nu, 2, BLOCK, HEAD_DIM), BF16),
            pltpu.VMEM((nb, nh, HEAD_DIM), F32),
            pltpu.VMEM((nb, nh, HEAD_DIM), BF16),
            pltpu.VMEM((nb, nh, HEAD_DIM), BF16),
            dma((6,)),
            dma, dma,
            dma((nb,)), dma((nb,)),
            dma((nu,)), dma((nu,)),
            dma((ny,)), dma((ny,)),
            dma((nx,)), dma((nx,)),
            dma((nu,)), dma((nu,)),
            dma((2,)), dma((2,)),
            dma((6,)), dma((nx, 2)),
            dma((ny,)), dma((ny,)),
            dma((nx,)), dma((nx,)),
            dma((ny,)), dma((ny,)),
            dma((nu,)), dma((nu,)),
            dma((nb,)), dma((nb,)),
        ],
        compiler_params=pltpu.CompilerParams(
            collective_id=0, has_side_effects=True, vmem_limit_bytes=63 * 1024 * 1024
        ),
    )(
        fresh_list.reshape(entries),
        hidden.reshape(toks, width),
        w_qkv,
        q_gain.reshape(2, HEAD_DIM),
        cache_k.reshape(keys, 2 * HEAD_DIM),
        cache_v.reshape(keys, 2 * HEAD_DIM),
    )
    return out.reshape(1, 1, 1, entries * BLOCK, nh * HEAD_DIM)


def solution(mesh):
    in_specs = (
        P("cfg", ("bal", "uly"), None),
        P(None, ("uly", "cfg")),
        P("uly"),
        P("cfg", "bal", "uly"),
        P("cfg", "bal", "uly"),
        P("cfg", "bal", "uly", None),
    )
    out_specs = P("cfg", "bal", "uly", None, None)
    return jax.shard_map(
        on_device, mesh=mesh, in_specs=in_specs, out_specs=out_specs, check_vma=False
    )
```

```python
import functools
import math

import jax
import jax.numpy as jnp
from jax import lax
from jax.experimental import pallas as pl
from jax.experimental.pallas import tpu as pltpu
from jax.sharding import PartitionSpec as P

HEAD_DIM = 128
BLOCK = 8
SIDE_X = 4
LANES = 128
MESH = pl.DeviceIdType.MESH
F32 = jnp.float32
BF16 = jnp.bfloat16


def normalize(values):
    return values * lax.rsqrt(jnp.mean(values * values, axis=-1, keepdims=True) + 1e-06)


def iota(shape, dim):
    return lax.broadcasted_iota(jnp.int32, shape, dim)


def dot(a, b):
    return jnp.dot(a, b, preferred_element_type=F32)


def dot_t(a, b):
    return lax.dot_general(a, b, (((1,), (1,)), ((), ())), preferred_element_type=F32)


def kernel(
    nx, nu, list_in, hidden_in, w_in, gain_in, ck_in, cv_in, out_ref,
    list_ref, hidden_ref, w_buf, gain_ref, ck_ref, cv_ref, lists, named, stage, out1, in1, outx, inx, xbuf, kv, qbuf, kvf,
    vaug, rsout, rsin, ret_out, ret1, stage2, out2, in2,
    in_sem, w_s, w_r, list_s, list_r, name_s, name_r, p1_s, p1_r, px_s, px_r, z_s, z_r, opp_s, opp_r, kv_s, kv_r, q_s, q_r, kf_s, kf_r, rs_s, rs_r,
    ret_s, ret_r, back_s, back_r,
):
    b, u, c = lax.axis_index("bal"), lax.axis_index("uly"), lax.axis_index("cfg")
    nb, width = lists.shape[0], hidden_ref.shape[1]
    ny = nb // nx
    x, y = b // ny, b % ny
    toks = hidden_ref.shape[0]
    blocks = toks // BLOCK
    entries = list_ref.shape[0]
    keys = ck_ref.shape[0]
    half = nu * BLOCK
    pieces = width // LANES
    nh = 2 * nu
    other = 1 - c

    def farthest(j, n):
        step = (j + 1) // 2
        return lax.rem(n // 2 + n + jnp.where(lax.rem(j, 2) == 1, step, -step), n)

    def x_of(k):
        return lax.rem(x + farthest(k - 1, nx), nx)

    def y_of(k):
        return lax.rem(y + farthest(k - 1, ny), ny)

    def bal_of(k):
        return x_of(lax.rem(k - 1, nx) + 1) * ny + y_of((k - 1) // nx + 1)

    def bal_dev(k):
        return (bal_of(k), u, c)

    def x_dev(k):
        return (lax.rem(x + k, nx) * ny + y, u, c)

    def y_dev(k):
        return (x * ny + lax.rem(y + k, ny), u, c)

    def z_dev(k):
        return (b, lax.rem(u + k, nu), c)

    def z_of(k):
        return lax.rem(u + farthest(k - 1, nu), nu)

    def remote(src, dst, s, r, dev):
        return pltpu.make_async_remote_copy(
            src_ref=src, dst_ref=dst, send_sem=s, recv_sem=r, device_id=dev, device_id_type=MESH
        )

    def each(lo, hi, body):
        lax.fori_loop(lo, hi, lambda i, z: (body(i), z)[1], 0)

    pairs = (
        (list_in, list_ref),
        (ck_in, ck_ref),
        (cv_in, cv_ref),
        (w_in, w_buf.at[c]),
        (hidden_in, hidden_ref),
        (gain_in, gain_ref),
    )
    loads = tuple(
        pltpu.make_async_copy(src, dst, in_sem.at[i]) for i, (src, dst) in enumerate(pairs)
    )
    for load in loads:
        load.start()
    list_load, k_load, v_load, w_load, hidden_load, gain_load = loads
    cleanup = []

    barrier = pltpu.get_barrier_semaphore()

    def greet(dev):
        pl.semaphore_signal(barrier, inc=1, device_id=dev, device_id_type=MESH)

    each(1, nb, lambda k: greet(bal_dev(k)))
    each(1, nu, lambda k: greet(z_dev(k)))
    greet((b, u, other))

    list_load.wait()
    my_blocks = 0
    for j in range(entries):
        my_blocks = my_blocks + jnp.where(list_ref[j] < blocks, 1, 0)
    lane = iota((1, LANES), 1)
    row = jnp.zeros((1, LANES), jnp.int32) + my_blocks
    for j in range(entries):
        row = jnp.where(lane == LANES - entries + j, list_ref[j], row)
    lists[b] = row

    hidden_load.wait()
    token = jnp.zeros((nb, toks), jnp.int32)
    for j in range(entries):
        token = jnp.where(iota((nb, toks), 0) % entries == j, list_ref[j], token)
    token = token * BLOCK + iota((nb, toks), 0) // entries
    pick = (token == iota((nb, toks), 1)).astype(F32).astype(BF16)
    for j in range(pieces):
        stage[:, j, :] = dot(pick, hidden_ref[:, j * LANES : (j + 1) * LANES])
    out1[...] = stage[...].astype(BF16).reshape(out1.shape)

    k_load.wait()
    v_load.wait()
    for head in range(2):
        columns = slice(head * HEAD_DIM, (head + 1) * HEAD_DIM)
        kv[x, head, 0] = normalize(ck_ref[:, columns].astype(F32)).astype(BF16)
        kv[x, head, 1] = cv_ref[:, columns]
    w_load.wait()

    pl.semaphore_wait(barrier, nb - 1 + nu - 1 + 1)

    def list_copy(k, slot):
        return remote(lists.at[b], lists.at[slot], list_s.at[k], list_r.at[slot], bal_dev(k))

    each(1, nb, lambda k: list_copy(k, b).start())
    cleanup.append(lambda: each(1, nb, lambda k: list_copy(k, b).wait_send()))

    def p1_copy(k, slot):
        to = y_of(k)
        dev = (x * ny + to, u, c)
        return remote(out1.at[to], in1.at[slot], p1_s.at[k], p1_r.at[slot], dev)

    each(1, ny, lambda k: p1_copy(k, y).start())
    cleanup.append(lambda: each(1, ny, lambda k: p1_copy(k, y).wait_send()))
    in1[y] = out1[y]

    w_out = remote(w_buf.at[c], w_buf.at[c], w_s, w_r, (b, u, other))
    w_out.start()
    cleanup.append(w_out.wait_send)

    prev_x, next_x, far_x = lax.rem(x + nx - 1, nx), lax.rem(x + 1, nx), lax.rem(x + nx // 2, nx)

    def ring(slot_x, head, s, way):
        part = kv.at[slot_x, head]
        return remote(part, part, kv_s.at[s], kv_r.at[slot_x, head], x_dev(way))

    def ring_start(head):
        up, down = ring(x, head, 2 * head, 1), ring(x, head, 2 * head + 1, nx - 1)
        up.start()
        down.start()
        cleanup.extend((up.wait_send, down.wait_send))

    ring_start(0)

    each(1, nb, lambda k: list_copy(k, bal_of(k)).wait_recv())
    table = lists[...].reshape(nb, LANES).astype(F32)
    counts = table[:, :nb]
    sub_n, lane_n = iota((nb, nb), 0), iota((nb, nb), 1)
    source = x * ny + lane_n // entries
    rank = jnp.sum(jnp.where(sub_n < source, counts, 0.0), axis=0, keepdims=True).astype(jnp.int32)
    known = jnp.sum(jnp.where(sub_n == source, counts, 0.0), axis=0, keepdims=True).astype(jnp.int32)
    entry = iota((1, nb), 1) % entries
    slots = nb // nx
    wanted = (sub_n % slots) * nx + sub_n // slots
    sel = (rank + entry == wanted) & (entry < known)
    sel = sel.astype(F32).astype(BF16)

    each(1, ny, lambda k: p1_copy(k, y_of(k)).wait_recv())
    stage[...] = in1[...].astype(F32).reshape(stage.shape)
    for j in range(pieces):
        part = dot(sel, stage[:, j, :].astype(BF16)).astype(BF16)
        for k in range(nx):
            outx[k, :, j * LANES : (j + 1) * LANES] = part[k * slots : (k + 1) * slots, :]

    def px_copy(k, slot):
        to = x_of(k)
        return remote(outx.at[to], inx.at[slot], px_s.at[k], px_r.at[slot], (to * ny + y, u, c))

    each(1, nx, lambda k: px_copy(k, x).start())
    cleanup.append(lambda: each(1, nx, lambda k: px_copy(k, x).wait_send()))
    inx[x] = outx[x]

    near = (iota((BLOCK, nb), 1) == iota((BLOCK, nb), 0) * ny + y) & (iota((BLOCK, nb), 0) < nx)
    named[u] = dot(near.astype(F32).astype(BF16), table.astype(BF16))

    def name_copy(k, slot):
        return remote(named.at[u], named.at[slot], name_s.at[k], name_r.at[slot], z_dev(k))

    each(1, nu, lambda k: name_copy(k, u).start())
    cleanup.append(lambda: each(1, nu, lambda k: name_copy(k, u).wait_send()))
    ring_start(1)

    each(1, nx, lambda k: px_copy(k, x_of(k)).wait_recv())
    gathered = inx[0].astype(F32)
    for k in range(1, nx):
        gathered = gathered + inx[k].astype(F32)
    xbuf[u] = gathered.astype(BF16)

    def z_copy(k, slot):
        return remote(xbuf.at[u], xbuf.at[slot], z_s.at[k], z_r.at[slot], z_dev(k))

    far = nu // 2
    order = [far - 1, far + 1, 2, nu - 2, 1, nu - 1]
    for k in order:
        z_copy(k, u).start()
        cleanup.append(z_copy(k, u).wait_send)

    def opposite_copy(side, slot):
        part = xbuf.at[slot, :, pl.ds(side * (width // 2), width // 2)]
        return remote(part, part, opp_s.at[side], opp_r.at[side], z_dev(1 if side == 0 else nu - 1))

    span = nx * keys
    owner_hit = (iota((keys, nu), 0) // toks == iota((keys, nu), 1)).astype(F32).astype(BF16)
    block_hit = (iota((keys, LANES), 0) % toks) // BLOCK == iota((keys, LANES), 1)
    ones = jnp.ones((LANES, LANES), BF16)
    lane_u = iota((nu, LANES), 1).astype(F32)

    def weigh_values(k):
        ids = named[:, pl.ds(k, 1), :].reshape(nu, LANES)
        hit = jnp.zeros((nu, LANES), F32)
        for j in range(LANES - entries, LANES):
            hit = hit + (ids[:, j : j + 1] == lane_u).astype(F32)
        spread = jnp.where(block_hit, dot(owner_hit, hit.astype(BF16)), 0.0).astype(BF16)
        mask = 1.0 - dot(spread, ones)
        rows = pl.ds(pl.multiple_of(k * keys, keys), keys)
        for h in range(2):
            vaug[h, rows, :HEAD_DIM] = (kv[k, h, 1].astype(F32) * mask).astype(BF16)
            vaug[h, rows, HEAD_DIM:] = mask.astype(BF16)

    each(1, nu, lambda k: name_copy(k, lax.rem(u + k, nu)).wait_recv())
    weigh_values(x)

    on_up, on_down = ring(prev_x, 0, 4, 1), ring(next_x, 1, 5, nx - 1)
    cleanup.extend((on_up.wait_send, on_down.wait_send))
    ring(prev_x, 0, 0, 1).wait_recv()
    on_up.start()
    for side, k in enumerate((far + 1, far - 1)):
        slot = lax.rem(u + k, nu)
        z_copy(k, slot).wait_recv()
        opposite_copy(side, slot).start()
        cleanup.append(opposite_copy(side, slot).wait_send)
    ring(next_x, 1, 2, 1).wait_recv()
    on_down.start()
    ring(prev_x, 1, 2, 1).wait_recv()
    ring(next_x, 0, 0, 1).wait_recv()
    weigh_values(prev_x)
    weigh_values(next_x)
    w_out.wait_recv()
    gain_load.wait()

    for k in order[2:]:
        z_copy(k, lax.rem(u + k, nu)).wait_recv()
    for side in range(2):
        opposite_copy(side, lax.rem(u + far, nu)).wait_recv()
    chunk = math.gcd(width, 1024)
    starts = range(0, width, chunk)
    rows = [xbuf[:, :, j : j + chunk].astype(F32).reshape(half, chunk).astype(BF16) for j in starts]

    def project(h, columns):
        total = dot(rows[0], w_buf[h, :chunk, columns])
        for i, j in enumerate(starts):
            if i > 0:
                total = total + dot(rows[i], w_buf[h, j : j + chunk, columns])
        return total

    for h in range(2):
        query = normalize(project(h, slice(0, HEAD_DIM))) * gain_ref[h : h + 1, :]
        qbuf[y, h * half : (h + 1) * half, :] = query.astype(BF16)

    def q_copy(k, slot):
        return remote(qbuf.at[y], qbuf.at[slot], q_s.at[k], q_r.at[slot], y_dev(k))

    def kf_copy(k, slot):
        return remote(kvf.at[x], kvf.at[slot], kf_s.at[k], kf_r.at[slot], (x_of(k) * ny + y, u, c))

    for k in range(ny // 2, 0, -1):
        for way in [k] if 2 * k == ny else [k, ny - k]:
            q_copy(way, y).start()
    for h in range(2):
        mine = slice(h * half, (h + 1) * half)
        both = project(h, slice(HEAD_DIM, 3 * HEAD_DIM))
        k_fresh = both[:, :HEAD_DIM].astype(BF16).astype(F32)
        kvf[x, 0, mine, :] = normalize(k_fresh).astype(BF16)
        kvf[x, 1, mine, :] = both[:, HEAD_DIM:].astype(BF16)
    each(1, nx, lambda k: kf_copy(k, x).start())
    cleanup.append(lambda: each(1, ny, lambda k: q_copy(k, y).wait_send()))
    cleanup.append(lambda: each(1, nx, lambda k: kf_copy(k, x).wait_send()))

    ring(far_x, 0, 4, 1).wait_recv()
    ring(far_x, 1, 5, nx - 1).wait_recv()
    weigh_values(far_x)

    each(1, nx, lambda k: kf_copy(k, x_of(k)).wait_recv())
    fresh_keys = nx * half
    for h in range(2):
        mine = slice(h * half, (h + 1) * half)
        vaug[h, span:, :HEAD_DIM] = kvf[:, 1, mine, :].reshape(fresh_keys, HEAD_DIM)
        vaug[h, span:, HEAD_DIM:] = jnp.ones((fresh_keys, HEAD_DIM), BF16)
    factor = 1.0 / math.sqrt(HEAD_DIM)

    def weigh(queries, some_keys):
        return jnp.exp(dot_t(queries, some_keys) * factor).astype(BF16)

    def rs_copy(k, slot):
        to = lax.rem(y + k, ny)
        return remote(rsout.at[to], rsin.at[slot], rs_s.at[k], rs_r.at[slot], y_dev(k))

    def attend(i):
        step = ny // 2 - 1 - i
        last = step == ny // 2 - 1
        way_a, way_b = step + 1, jnp.where(last, 0, ny - 1 - step)
        slot_a, slot_b = lax.rem(y + way_a, ny), lax.rem(y + way_b, ny)

        q_copy(way_a, slot_a).wait_recv()

        @pl.when(jnp.logical_not(last))
        def _():
            q_copy(way_b, slot_b).wait_recv()

        flat_a = jnp.zeros((1, LANES), F32)
        flat_b = jnp.zeros((1, LANES), F32)
        for h in range(2):
            mine = slice(h * half, (h + 1) * half)
            queries = jnp.concatenate([qbuf[slot_a, mine, :], qbuf[slot_b, mine, :]], axis=0)
            k_last = kvf[:, 0, mine, :].reshape(fresh_keys, HEAD_DIM)
            got = dot(weigh(queries, k_last), vaug[h, span:, :])
            for k in range(nx):
                got = got + dot(weigh(queries, kv[k, h, 0]), vaug[h, k * keys : (k + 1) * keys, :])
            rsout[slot_a, mine, :] = got[:half, :HEAD_DIM].astype(BF16)
            rsout[slot_b, mine, :] = got[half:, :HEAD_DIM].astype(BF16)
            place = iota((half, LANES), 1) == iota((half, LANES), 0) + h * half
            flat_a = flat_a + jnp.sum(jnp.where(place, got[:half, HEAD_DIM:], 0.0), axis=0, keepdims=True)
            flat_b = flat_b + jnp.sum(jnp.where(place, got[half:, HEAD_DIM:], 0.0), axis=0, keepdims=True)
        tail = rsout.shape[1] - 2 * half
        tail_row = iota((tail, LANES), 0)
        for slot, flat in ((slot_a, flat_a), (slot_b, flat_b)):
            coarse = flat.astype(BF16).astype(F32)
            rest = jnp.where(tail_row == 1, flat - coarse, 0.0)
            rsout[slot, 2 * half :, :] = jnp.where(tail_row == 0, coarse, rest).astype(BF16)

        rs_copy(way_a, y).start()

        @pl.when(jnp.logical_not(last))
        def _():
            rs_copy(way_b, y).start()

    each(0, ny // 2, attend)
    cleanup.append(lambda: each(1, ny, lambda k: rs_copy(k, y).wait_send()))

    summed = rsout[y].astype(F32)
    for k in range(1, ny // 2 + 1):
        for way in [k] if 2 * k == ny else [k, ny - k]:
            slot = lax.rem(y + way, ny)
            rs_copy(way, slot).wait_recv()
            summed = summed + rsin[slot].astype(F32)
    total = summed[2 * half : 2 * half + 1, :] + summed[2 * half + 1 : 2 * half + 2, :]
    square = iota((2 * half, LANES), 0) == iota((2 * half, LANES), 1)
    total = jnp.sum(jnp.where(square, total, 0.0), axis=1, keepdims=True)
    attended = summed[: 2 * half, :] / total
    for h in range(2):
        rows = attended[h * half : (h + 1) * half, :]
        ret_out[:, h] = rows.reshape(nu, BLOCK, HEAD_DIM).astype(BF16)

    def ret_copy(k, slot):
        to = z_of(k)
        return remote(ret_out.at[to], ret1.at[slot], ret_s.at[k], ret_r.at[slot], (b, to, c))

    each(1, nu, lambda k: ret_copy(k, u).start())
    cleanup.append(lambda: each(1, nu, lambda k: ret_copy(k, u).wait_send()))
    ret1[u] = ret_out[u]
    count_row = jnp.sum(jnp.where(sub_n == lane_n, counts, 0.0), axis=0, keepdims=True)
    start_col = jnp.sum(jnp.where(lane_n < sub_n, count_row, 0.0), axis=1, keepdims=True).astype(jnp.int32)
    rank_col = start_col + jnp.bitwise_and(x - start_col, nx - 1)
    give = rank_col < start_col + counts[:, :slots].astype(jnp.int32)
    give = give & (rank_col // nx == iota((nb, slots), 1))
    give = give.astype(F32).astype(BF16)
    each(1, nu, lambda k: ret_copy(k, z_of(k)).wait_recv())
    for h in range(nh):
        stage2[:, h, :] = dot(give, ret1[h // 2, h % 2])
    out2[...] = stage2[...].astype(BF16)

    def back_copy(k, slot):
        to = bal_of(k)
        return remote(out2.at[to], in2.at[slot], back_s.at[k], back_r.at[slot], (to, u, c))

    each(1, nb, lambda k: back_copy(k, b).start())
    cleanup.append(lambda: each(1, nb, lambda k: back_copy(k, b).wait_send()))
    in2[b] = out2[b]
    my_start = jnp.sum(jnp.where(sub_n < b, counts, 0.0), axis=0, keepdims=True).astype(jnp.int32)
    from_x = jnp.bitwise_and(my_start + sub_n // BLOCK, nx - 1)
    final = (from_x * ny + sub_n % BLOCK == lane_n) & (sub_n // BLOCK < my_blocks)
    final = final.astype(F32).astype(BF16)
    each(1, nb, lambda k: back_copy(k, bal_of(k)).wait_recv())
    stage2[...] = in2[...].astype(F32)
    for h in range(nh):
        out_ref[:, h * HEAD_DIM : (h + 1) * HEAD_DIM] = dot(final, stage2[:, h, :].astype(BF16)).astype(BF16)

    for finish in cleanup:
        finish()


def on_device(hidden, w_qkv, q_gain, cache_k, cache_v, fresh_list):
    nb, nu = lax.axis_size("bal"), lax.axis_size("uly")
    nx = SIDE_X
    ny = nb // nx
    toks, width = hidden.shape[1:]
    keys = cache_k.shape[1]
    entries = fresh_list.shape[3]
    half = nu * BLOCK
    nh = 2 * nu
    pieces = width // LANES
    span = nx * (keys + half)
    vmem = pl.BlockSpec(memory_space=pltpu.VMEM)
    dma = pltpu.SemaphoreType.DMA
    out = pl.pallas_call(
        functools.partial(kernel, nx, nu),
        out_shape=jax.ShapeDtypeStruct((entries * BLOCK, nh * HEAD_DIM), BF16),
        in_specs=[
            *[pl.BlockSpec(memory_space=pltpu.HBM)] * 6,
        ],
        out_specs=vmem,
        scratch_shapes=[
            pltpu.SMEM((entries,), jnp.int32),
            pltpu.VMEM((toks, width), BF16),
            pltpu.VMEM((2, *w_qkv.shape), BF16),
            pltpu.VMEM((2, HEAD_DIM), F32),
            pltpu.VMEM((keys, 2 * HEAD_DIM), BF16),
            pltpu.VMEM((keys, 2 * HEAD_DIM), BF16),
            pltpu.VMEM((nb, 1, LANES), jnp.int32),
            pltpu.VMEM((nu, BLOCK, LANES), F32),
            pltpu.VMEM((nb, pieces, LANES), F32),
            pltpu.VMEM((ny, entries, pieces, LANES), BF16),
            pltpu.VMEM((ny, entries, pieces, LANES), BF16),
            pltpu.VMEM((nx, nb // nx, width), BF16),
            pltpu.VMEM((nx, nb // nx, width), BF16),
            pltpu.VMEM((nu, nb // nx, width), BF16),
            pltpu.VMEM((nx, 2, 2, keys, HEAD_DIM), BF16),
            pltpu.VMEM((ny, 2 * half, HEAD_DIM), BF16),
            pltpu.VMEM((nx, 2, 2 * half, HEAD_DIM), BF16),
            pltpu.VMEM((2, span, 2 * HEAD_DIM), BF16),
            pltpu.VMEM((ny, 2 * half + 8, HEAD_DIM), BF16),
            pltpu.VMEM((ny, 2 * half + 8, HEAD_DIM), BF16),
            pltpu.VMEM((nu, 2, BLOCK, HEAD_DIM), BF16),
            pltpu.VMEM((nu, 2, BLOCK, HEAD_DIM), BF16),
            pltpu.VMEM((nb, nh, HEAD_DIM), F32),
            pltpu.VMEM((nb, nh, HEAD_DIM), BF16),
            pltpu.VMEM((nb, nh, HEAD_DIM), BF16),
            dma((6,)),
            dma, dma,
            dma((nb,)), dma((nb,)),
            dma((nu,)), dma((nu,)),
            dma((ny,)), dma((ny,)),
            dma((nx,)), dma((nx,)),
            dma((nu,)), dma((nu,)),
            dma((2,)), dma((2,)),
            dma((6,)), dma((nx, 2)),
            dma((ny,)), dma((ny,)),
            dma((nx,)), dma((nx,)),
            dma((ny,)), dma((ny,)),
            dma((nu,)), dma((nu,)),
            dma((nb,)), dma((nb,)),
        ],
        compiler_params=pltpu.CompilerParams(
            collective_id=0, has_side_effects=True, vmem_limit_bytes=63 * 1024 * 1024
        ),
    )(
        fresh_list.reshape(entries),
        hidden.reshape(toks, width),
        w_qkv,
        q_gain.reshape(2, HEAD_DIM),
        cache_k.reshape(keys, 2 * HEAD_DIM),
        cache_v.reshape(keys, 2 * HEAD_DIM),
    )
    return out.reshape(1, 1, 1, entries * BLOCK, nh * HEAD_DIM)


def solution(mesh):
    in_specs = (
        P("cfg", ("bal", "uly"), None),
        P(None, ("uly", "cfg")),
        P("uly"),
        P("cfg", "bal", "uly"),
        P("cfg", "bal", "uly"),
        P("cfg", "bal", "uly", None),
    )
    out_specs = P("cfg", "bal", "uly", None, None)
    return jax.shard_map(
        on_device, mesh=mesh, in_specs=in_specs, out_specs=out_specs, check_vma=False
    )
```

```python
import functools
import math

import jax
import jax.numpy as jnp
from jax import lax
from jax.experimental import pallas as pl
from jax.experimental.pallas import tpu as pltpu
from jax.sharding import PartitionSpec as P

HEAD_DIM = 128
BLOCK = 8
SIDE_X = 4
LANES = 128
MESH = pl.DeviceIdType.MESH
F32 = jnp.float32
BF16 = jnp.bfloat16


def normalize(values):
    return values * lax.rsqrt(jnp.mean(values * values, axis=-1, keepdims=True) + 1e-06)


def iota(shape, dim):
    return lax.broadcasted_iota(jnp.int32, shape, dim)


def dot(a, b):
    return jnp.dot(a, b, preferred_element_type=F32)


def dot_t(a, b):
    return lax.dot_general(a, b, (((1,), (1,)), ((), ())), preferred_element_type=F32)


def kernel(
    nx, nu, list_in, hidden_in, w_in, gain_in, ck_in, cv_in, out_ref,
    list_ref, hidden_ref, w_buf, gain_ref, ck_ref, cv_ref, lists, named, stage, out1, in1, outx, inx, xbuf, kv, qbuf, kvf,
    vaug, rsout, rsin, ret_out, ret1, stage2, out2, in2,
    in_sem, w_s, w_r, list_s, list_r, name_s, name_r, p1_s, p1_r, px_s, px_r, z_s, z_r, opp_s, opp_r, kv_s, kv_r, q_s, q_r, kf_s, kf_r, rs_s, rs_r,
    ret_s, ret_r, back_s, back_r,
):
    b, u, c = lax.axis_index("bal"), lax.axis_index("uly"), lax.axis_index("cfg")
    nb, width = lists.shape[0], hidden_ref.shape[1]
    ny = nb // nx
    x, y = b // ny, b % ny
    toks = hidden_ref.shape[0]
    blocks = toks // BLOCK
    entries = list_ref.shape[0]
    keys = ck_ref.shape[0]
    half = nu * BLOCK
    pieces = width // LANES
    nh = 2 * nu
    other = 1 - c

    def farthest(j, n):
        step = (j + 1) // 2
        return lax.rem(n // 2 + n + jnp.where(lax.rem(j, 2) == 1, step, -step), n)

    def x_of(k):
        return lax.rem(x + farthest(k - 1, nx), nx)

    def y_of(k):
        return lax.rem(y + farthest(k - 1, ny), ny)

    def bal_of(k):
        return x_of(lax.rem(k - 1, nx) + 1) * ny + y_of((k - 1) // nx + 1)

    def bal_dev(k):
        return (bal_of(k), u, c)

    def ways(n):
        return [(n // 2 + (j + 1) // 2 * (1 if j % 2 == 1 else -1)) % n for j in range(n)]

    x_list = [lax.rem(x + way, nx) for way in ways(nx)]
    y_list = [lax.rem(y + way, ny) for way in ways(ny)]
    bal_list = [x_list[j % nx] * ny + y_list[j // nx] for j in range(nb)]

    z_list = [lax.rem(u + way, nu) for way in ways(nu)]

    def x_dev(k):
        return (lax.rem(x + k, nx) * ny + y, u, c)

    def y_dev(k):
        return (x * ny + lax.rem(y + k, ny), u, c)

    def z_dev(k):
        return (b, lax.rem(u + k, nu), c)

    def remote(src, dst, s, r, dev):
        return pltpu.make_async_remote_copy(
            src_ref=src, dst_ref=dst, send_sem=s, recv_sem=r, device_id=dev, device_id_type=MESH
        )

    def each(lo, hi, body):
        lax.fori_loop(lo, hi, lambda i, z: (body(i), z)[1], 0)

    pairs = (
        (list_in, list_ref),
        (ck_in, ck_ref),
        (cv_in, cv_ref),
        (w_in, w_buf.at[c]),
        (hidden_in, hidden_ref),
        (gain_in, gain_ref),
    )
    loads = tuple(
        pltpu.make_async_copy(src, dst, in_sem.at[i]) for i, (src, dst) in enumerate(pairs)
    )
    for load in loads:
        load.start()
    list_load, k_load, v_load, w_load, hidden_load, gain_load = loads
    cleanup = []

    barrier = pltpu.get_barrier_semaphore()

    def greet(dev):
        pl.semaphore_signal(barrier, inc=1, device_id=dev, device_id_type=MESH)

    each(1, nb, lambda k: greet(bal_dev(k)))
    each(1, nu, lambda k: greet(z_dev(k)))
    greet((b, u, other))

    list_load.wait()
    my_blocks = 0
    for j in range(entries):
        my_blocks = my_blocks + jnp.where(list_ref[j] < blocks, 1, 0)
    lane = iota((1, LANES), 1)
    row = jnp.zeros((1, LANES), jnp.int32) + my_blocks
    for j in range(entries):
        row = jnp.where(lane == LANES - entries + j, list_ref[j], row)
    lists[b] = row

    hidden_load.wait()
    token = jnp.zeros((nb, toks), jnp.int32)
    for j in range(entries):
        token = jnp.where(iota((nb, toks), 0) % entries == j, list_ref[j], token)
    token = token * BLOCK + iota((nb, toks), 0) // entries
    pick = (token == iota((nb, toks), 1)).astype(F32).astype(BF16)
    for j in range(pieces):
        stage[:, j, :] = dot(pick, hidden_ref[:, j * LANES : (j + 1) * LANES])
    out1[...] = stage[...].astype(BF16).reshape(out1.shape)

    k_load.wait()
    v_load.wait()
    for head in range(2):
        columns = slice(head * HEAD_DIM, (head + 1) * HEAD_DIM)
        kv[x, head, 0] = normalize(ck_ref[:, columns].astype(F32)).astype(BF16)
        kv[x, head, 1] = cv_ref[:, columns]
    w_load.wait()

    pl.semaphore_wait(barrier, nb - 1 + nu - 1 + 1)

    def list_copy(k, slot, to):
        return remote(lists.at[b], lists.at[slot], list_s.at[k], list_r.at[slot], (to, u, c))

    for k in range(1, nb):
        list_copy(k, b, bal_list[k - 1]).start()
    cleanup.append(lambda: each(1, nb, lambda k: list_copy(k, b, bal_of(k)).wait_send()))

    def p1_copy(k, slot):
        to = y_list[k - 1]
        dev = (x * ny + to, u, c)
        return remote(out1.at[to], in1.at[slot], p1_s.at[k], p1_r.at[slot], dev)

    for k in range(1, ny):
        p1_copy(k, y).start()
        cleanup.append(p1_copy(k, y).wait_send)
    in1[y] = out1[y]

    w_out = remote(w_buf.at[c], w_buf.at[c], w_s, w_r, (b, u, other))
    w_out.start()
    cleanup.append(w_out.wait_send)

    prev_x, next_x, far_x = lax.rem(x + nx - 1, nx), lax.rem(x + 1, nx), lax.rem(x + nx // 2, nx)

    def ring(slot_x, head, s, way):
        part = kv.at[slot_x, head]
        return remote(part, part, kv_s.at[s], kv_r.at[slot_x, head], x_dev(way))

    def ring_start(head):
        up, down = ring(x, head, 2 * head, 1), ring(x, head, 2 * head + 1, nx - 1)
        up.start()
        down.start()
        cleanup.extend((up.wait_send, down.wait_send))

    ring_start(0)


    def list_arrival(k):
        slot = lax.rem(b + k, nb)
        list_copy(k, slot, slot).wait_recv()

    each(1, nb, list_arrival)
    table = lists[...].reshape(nb, LANES).astype(F32)
    counts = table[:, :nb]
    sub_n, lane_n = iota((nb, nb), 0), iota((nb, nb), 1)
    source = x * ny + lane_n // entries
    rank = jnp.sum(jnp.where(sub_n < source, counts, 0.0), axis=0, keepdims=True).astype(jnp.int32)
    known = jnp.sum(jnp.where(sub_n == source, counts, 0.0), axis=0, keepdims=True).astype(jnp.int32)
    entry = iota((1, nb), 1) % entries
    slots = nb // nx
    wanted = (sub_n % slots) * nx + sub_n // slots
    sel = (rank + entry == wanted) & (entry < known)
    sel = sel.astype(F32).astype(BF16)

    for k in range(1, ny):
        p1_copy(k, y_list[k - 1]).wait_recv()
    stage[...] = in1[...].astype(F32).reshape(stage.shape)
    for j in range(pieces):
        part = dot(sel, stage[:, j, :].astype(BF16)).astype(BF16)
        for k in range(nx):
            outx[k, :, j * LANES : (j + 1) * LANES] = part[k * slots : (k + 1) * slots, :]

    def px_copy(k, slot):
        to = x_list[k - 1]
        return remote(outx.at[to], inx.at[slot], px_s.at[k], px_r.at[slot], (to * ny + y, u, c))

    for k in range(1, nx):
        px_copy(k, x).start()
        cleanup.append(px_copy(k, x).wait_send)
    inx[x] = outx[x]

    near = (iota((BLOCK, nb), 1) == iota((BLOCK, nb), 0) * ny + y) & (iota((BLOCK, nb), 0) < nx)
    named[u] = dot(near.astype(F32).astype(BF16), table.astype(BF16))

    def name_copy(k, slot):
        return remote(named.at[u], named.at[slot], name_s.at[k], name_r.at[slot], z_dev(k))

    each(1, nu, lambda k: name_copy(k, u).start())
    cleanup.append(lambda: each(1, nu, lambda k: name_copy(k, u).wait_send()))
    ring_start(1)

    for k in range(1, nx):
        px_copy(k, x_list[k - 1]).wait_recv()
    gathered = inx[0].astype(F32)
    for k in range(1, nx):
        gathered = gathered + inx[k].astype(F32)
    xbuf[u] = gathered.astype(BF16)

    def z_copy(k, slot):
        return remote(xbuf.at[u], xbuf.at[slot], z_s.at[k], z_r.at[slot], z_dev(k))

    far = nu // 2
    order = [far - 1, far + 1, 2, nu - 2, 1, nu - 1]
    for k in order:
        z_copy(k, u).start()
        cleanup.append(z_copy(k, u).wait_send)

    def opposite_copy(side, slot):
        part = xbuf.at[slot, :, pl.ds(side * (width // 2), width // 2)]
        return remote(part, part, opp_s.at[side], opp_r.at[side], z_dev(1 if side == 0 else nu - 1))

    span = nx * keys
    owner_hit = (iota((keys, nu), 0) // toks == iota((keys, nu), 1)).astype(F32).astype(BF16)
    block_hit = (iota((keys, LANES), 0) % toks) // BLOCK == iota((keys, LANES), 1)
    ones = jnp.ones((LANES, LANES), BF16)
    lane_u = iota((nu, LANES), 1).astype(F32)

    def weigh_values(k):
        ids = named[:, pl.ds(k, 1), :].reshape(nu, LANES)
        hit = jnp.zeros((nu, LANES), F32)
        for j in range(LANES - entries, LANES):
            hit = hit + (ids[:, j : j + 1] == lane_u).astype(F32)
        spread = jnp.where(block_hit, dot(owner_hit, hit.astype(BF16)), 0.0).astype(BF16)
        mask = 1.0 - dot(spread, ones)
        rows = pl.ds(pl.multiple_of(k * keys, keys), keys)
        for h in range(2):
            vaug[h, rows, :HEAD_DIM] = (kv[k, h, 1].astype(F32) * mask).astype(BF16)
            vaug[h, rows, HEAD_DIM:] = mask.astype(BF16)

    each(1, nu, lambda k: name_copy(k, lax.rem(u + k, nu)).wait_recv())
    weigh_values(x)

    on_up, on_down = ring(prev_x, 0, 4, 1), ring(next_x, 1, 5, nx - 1)
    cleanup.extend((on_up.wait_send, on_down.wait_send))
    ring(prev_x, 0, 0, 1).wait_recv()
    on_up.start()
    for side, k in enumerate((far + 1, far - 1)):
        slot = lax.rem(u + k, nu)
        z_copy(k, slot).wait_recv()
        opposite_copy(side, slot).start()
        cleanup.append(opposite_copy(side, slot).wait_send)
    ring(next_x, 1, 2, 1).wait_recv()
    on_down.start()
    ring(prev_x, 1, 2, 1).wait_recv()
    ring(next_x, 0, 0, 1).wait_recv()
    weigh_values(prev_x)
    weigh_values(next_x)
    w_out.wait_recv()
    gain_load.wait()

    for k in order[2:]:
        z_copy(k, lax.rem(u + k, nu)).wait_recv()
    for side in range(2):
        opposite_copy(side, lax.rem(u + far, nu)).wait_recv()
    chunk = math.gcd(width, 1024)
    starts = range(0, width, chunk)
    rows = [xbuf[:, :, j : j + chunk].astype(F32).reshape(half, chunk).astype(BF16) for j in starts]

    def project(h, columns):
        total = dot(rows[0], w_buf[h, :chunk, columns])
        for i, j in enumerate(starts):
            if i > 0:
                total = total + dot(rows[i], w_buf[h, j : j + chunk, columns])
        return total

    for h in range(2):
        query = normalize(project(h, slice(0, HEAD_DIM))) * gain_ref[h : h + 1, :]
        qbuf[y, h * half : (h + 1) * half, :] = query.astype(BF16)

    def q_copy(k, slot):
        return remote(qbuf.at[y], qbuf.at[slot], q_s.at[k], q_r.at[slot], y_dev(k))

    def kf_copy(k, slot):
        return remote(kvf.at[x], kvf.at[slot], kf_s.at[k], kf_r.at[slot], (x_of(k) * ny + y, u, c))

    for k in range(ny // 2, 0, -1):
        for way in [k] if 2 * k == ny else [k, ny - k]:
            q_copy(way, y).start()
    for h in range(2):
        mine = slice(h * half, (h + 1) * half)
        both = project(h, slice(HEAD_DIM, 3 * HEAD_DIM))
        k_fresh = both[:, :HEAD_DIM].astype(BF16).astype(F32)
        kvf[x, 0, mine, :] = normalize(k_fresh).astype(BF16)
        kvf[x, 1, mine, :] = both[:, HEAD_DIM:].astype(BF16)
    each(1, nx, lambda k: kf_copy(k, x).start())
    cleanup.append(lambda: each(1, ny, lambda k: q_copy(k, y).wait_send()))
    cleanup.append(lambda: each(1, nx, lambda k: kf_copy(k, x).wait_send()))

    ring(far_x, 0, 4, 1).wait_recv()
    ring(far_x, 1, 5, nx - 1).wait_recv()
    weigh_values(far_x)

    each(1, nx, lambda k: kf_copy(k, x_of(k)).wait_recv())
    fresh_keys = nx * half
    for h in range(2):
        mine = slice(h * half, (h + 1) * half)
        vaug[h, span:, :HEAD_DIM] = kvf[:, 1, mine, :].reshape(fresh_keys, HEAD_DIM)
        vaug[h, span:, HEAD_DIM:] = jnp.ones((fresh_keys, HEAD_DIM), BF16)
    factor = 1.0 / math.sqrt(HEAD_DIM)

    def weigh(queries, some_keys):
        return jnp.exp(dot_t(queries, some_keys) * factor).astype(BF16)

    def rs_copy(k, slot):
        to = lax.rem(y + k, ny)
        return remote(rsout.at[to], rsin.at[slot], rs_s.at[k], rs_r.at[slot], y_dev(k))

    def attend(i):
        step = ny // 2 - 1 - i
        last = step == ny // 2 - 1
        way_a, way_b = step + 1, jnp.where(last, 0, ny - 1 - step)
        slot_a, slot_b = lax.rem(y + way_a, ny), lax.rem(y + way_b, ny)

        q_copy(way_a, slot_a).wait_recv()

        @pl.when(jnp.logical_not(last))
        def _():
            q_copy(way_b, slot_b).wait_recv()

        flat_a = jnp.zeros((1, LANES), F32)
        flat_b = jnp.zeros((1, LANES), F32)
        for h in range(2):
            mine = slice(h * half, (h + 1) * half)
            queries = jnp.concatenate([qbuf[slot_a, mine, :], qbuf[slot_b, mine, :]], axis=0)
            k_last = kvf[:, 0, mine, :].reshape(fresh_keys, HEAD_DIM)
            got = dot(weigh(queries, k_last), vaug[h, span:, :])
            for k in range(nx):
                got = got + dot(weigh(queries, kv[k, h, 0]), vaug[h, k * keys : (k + 1) * keys, :])
            rsout[slot_a, mine, :] = got[:half, :HEAD_DIM].astype(BF16)
            rsout[slot_b, mine, :] = got[half:, :HEAD_DIM].astype(BF16)
            place = iota((half, LANES), 1) == iota((half, LANES), 0) + h * half
            flat_a = flat_a + jnp.sum(jnp.where(place, got[:half, HEAD_DIM:], 0.0), axis=0, keepdims=True)
            flat_b = flat_b + jnp.sum(jnp.where(place, got[half:, HEAD_DIM:], 0.0), axis=0, keepdims=True)
        tail = rsout.shape[1] - 2 * half
        tail_row = iota((tail, LANES), 0)
        for slot, flat in ((slot_a, flat_a), (slot_b, flat_b)):
            coarse = flat.astype(BF16).astype(F32)
            rest = jnp.where(tail_row == 1, flat - coarse, 0.0)
            rsout[slot, 2 * half :, :] = jnp.where(tail_row == 0, coarse, rest).astype(BF16)

        rs_copy(way_a, y).start()

        @pl.when(jnp.logical_not(last))
        def _():
            rs_copy(way_b, y).start()

    each(0, ny // 2, attend)
    cleanup.append(lambda: each(1, ny, lambda k: rs_copy(k, y).wait_send()))

    count_row = jnp.sum(jnp.where(sub_n == lane_n, counts, 0.0), axis=0, keepdims=True)
    start_col = jnp.sum(jnp.where(lane_n < sub_n, count_row, 0.0), axis=1, keepdims=True).astype(jnp.int32)
    rank_col = start_col + jnp.bitwise_and(x - start_col, nx - 1)
    give = rank_col < start_col + counts[:, :slots].astype(jnp.int32)
    give = give & (rank_col // nx == iota((nb, slots), 1))
    give = give.astype(F32).astype(BF16)
    my_start = jnp.sum(jnp.where(sub_n < b, counts, 0.0), axis=0, keepdims=True).astype(jnp.int32)
    from_x = jnp.bitwise_and(my_start + sub_n // BLOCK, nx - 1)
    final = (from_x * ny + sub_n % BLOCK == lane_n) & (sub_n // BLOCK < my_blocks)
    final = final.astype(F32).astype(BF16)
    summed = rsout[y].astype(F32)
    for k in range(1, ny // 2 + 1):
        for way in [k] if 2 * k == ny else [k, ny - k]:
            slot = lax.rem(y + way, ny)
            rs_copy(way, slot).wait_recv()
            summed = summed + rsin[slot].astype(F32)
    total = summed[2 * half : 2 * half + 1, :] + summed[2 * half + 1 : 2 * half + 2, :]
    square = iota((2 * half, LANES), 0) == iota((2 * half, LANES), 1)
    total = jnp.sum(jnp.where(square, total, 0.0), axis=1, keepdims=True)
    attended = summed[: 2 * half, :] / total
    for h in range(2):
        rows = attended[h * half : (h + 1) * half, :]
        ret_out[:, h] = rows.reshape(nu, BLOCK, HEAD_DIM).astype(BF16)

    def ret_copy(k, slot):
        to = z_list[k - 1]
        return remote(ret_out.at[to], ret1.at[slot], ret_s.at[k], ret_r.at[slot], (b, to, c))

    for k in range(1, nu):
        ret_copy(k, u).start()
        cleanup.append(ret_copy(k, u).wait_send)
    ret1[u] = ret_out[u]
    for k in range(1, nu):
        ret_copy(k, z_list[k - 1]).wait_recv()
    for h in range(nh):
        stage2[:, h, :] = dot(give, ret1[h // 2, h % 2])
    out2[...] = stage2[...].astype(BF16)

    def back_copy(k, slot, to):
        return remote(out2.at[to], in2.at[slot], back_s.at[k], back_r.at[slot], (to, u, c))

    for k in range(1, nb):
        back_copy(k, b, bal_list[k - 1]).start()
    in2[b] = out2[b]
    for finish in cleanup:
        finish()

    def back_arrival(k):
        slot = lax.rem(b + k, nb)
        back_copy(k, slot, slot).wait_recv()

    each(1, nb, back_arrival)
    stage2[...] = in2[...].astype(F32)
    for h in range(nh):
        out_ref[:, h * HEAD_DIM : (h + 1) * HEAD_DIM] = dot(final, stage2[:, h, :].astype(BF16)).astype(BF16)

    each(1, nb, lambda k: back_copy(k, b, bal_of(k)).wait_send())


def on_device(hidden, w_qkv, q_gain, cache_k, cache_v, fresh_list):
    nb, nu = lax.axis_size("bal"), lax.axis_size("uly")
    nx = SIDE_X
    ny = nb // nx
    toks, width = hidden.shape[1:]
    keys = cache_k.shape[1]
    entries = fresh_list.shape[3]
    half = nu * BLOCK
    nh = 2 * nu
    pieces = width // LANES
    span = nx * (keys + half)
    vmem = pl.BlockSpec(memory_space=pltpu.VMEM)
    dma = pltpu.SemaphoreType.DMA
    out = pl.pallas_call(
        functools.partial(kernel, nx, nu),
        out_shape=jax.ShapeDtypeStruct((entries * BLOCK, nh * HEAD_DIM), BF16),
        in_specs=[
            *[pl.BlockSpec(memory_space=pltpu.HBM)] * 6,
        ],
        out_specs=vmem,
        scratch_shapes=[
            pltpu.SMEM((entries,), jnp.int32),
            pltpu.VMEM((toks, width), BF16),
            pltpu.VMEM((2, *w_qkv.shape), BF16),
            pltpu.VMEM((2, HEAD_DIM), F32),
            pltpu.VMEM((keys, 2 * HEAD_DIM), BF16),
            pltpu.VMEM((keys, 2 * HEAD_DIM), BF16),
            pltpu.VMEM((nb, 1, LANES), jnp.int32),
            pltpu.VMEM((nu, BLOCK, LANES), F32),
            pltpu.VMEM((nb, pieces, LANES), F32),
            pltpu.VMEM((ny, entries, pieces, LANES), BF16),
            pltpu.VMEM((ny, entries, pieces, LANES), BF16),
            pltpu.VMEM((nx, nb // nx, width), BF16),
            pltpu.VMEM((nx, nb // nx, width), BF16),
            pltpu.VMEM((nu, nb // nx, width), BF16),
            pltpu.VMEM((nx, 2, 2, keys, HEAD_DIM), BF16),
            pltpu.VMEM((ny, 2 * half, HEAD_DIM), BF16),
            pltpu.VMEM((nx, 2, 2 * half, HEAD_DIM), BF16),
            pltpu.VMEM((2, span, 2 * HEAD_DIM), BF16),
            pltpu.VMEM((ny, 2 * half + 8, HEAD_DIM), BF16),
            pltpu.VMEM((ny, 2 * half + 8, HEAD_DIM), BF16),
            pltpu.VMEM((nu, 2, BLOCK, HEAD_DIM), BF16),
            pltpu.VMEM((nu, 2, BLOCK, HEAD_DIM), BF16),
            pltpu.VMEM((nb, nh, HEAD_DIM), F32),
            pltpu.VMEM((nb, nh, HEAD_DIM), BF16),
            pltpu.VMEM((nb, nh, HEAD_DIM), BF16),
            dma((6,)),
            dma, dma,
            dma((nb,)), dma((nb,)),
            dma((nu,)), dma((nu,)),
            dma((ny,)), dma((ny,)),
            dma((nx,)), dma((nx,)),
            dma((nu,)), dma((nu,)),
            dma((2,)), dma((2,)),
            dma((6,)), dma((nx, 2)),
            dma((ny,)), dma((ny,)),
            dma((nx,)), dma((nx,)),
            dma((ny,)), dma((ny,)),
            dma((nu,)), dma((nu,)),
            dma((nb,)), dma((nb,)),
        ],
        compiler_params=pltpu.CompilerParams(
            collective_id=0, has_side_effects=True, vmem_limit_bytes=63 * 1024 * 1024
        ),
    )(
        fresh_list.reshape(entries),
        hidden.reshape(toks, width),
        w_qkv,
        q_gain.reshape(2, HEAD_DIM),
        cache_k.reshape(keys, 2 * HEAD_DIM),
        cache_v.reshape(keys, 2 * HEAD_DIM),
    )
    return out.reshape(1, 1, 1, entries * BLOCK, nh * HEAD_DIM)


def solution(mesh):
    in_specs = (
        P("cfg", ("bal", "uly"), None),
        P(None, ("uly", "cfg")),
        P("uly"),
        P("cfg", "bal", "uly"),
        P("cfg", "bal", "uly"),
        P("cfg", "bal", "uly", None),
    )
    out_specs = P("cfg", "bal", "uly", None, None)
    return jax.shard_map(
        on_device, mesh=mesh, in_specs=in_specs, out_specs=out_specs, check_vma=False
    )
```

```python
import functools
import math

import jax
import jax.numpy as jnp
from jax import lax
from jax.experimental import pallas as pl
from jax.experimental.pallas import tpu as pltpu
from jax.sharding import PartitionSpec as P

HEAD_DIM = 128
BLOCK = 8
SIDE_X = 4
LANES = 128
MESH = pl.DeviceIdType.MESH
F32 = jnp.float32
BF16 = jnp.bfloat16


def normalize(values):
    return values * lax.rsqrt(jnp.mean(values * values, axis=-1, keepdims=True) + 1e-06)


def iota(shape, dim):
    return lax.broadcasted_iota(jnp.int32, shape, dim)


def dot(a, b):
    return jnp.dot(a, b, preferred_element_type=F32)


def dot_t(a, b):
    return lax.dot_general(a, b, (((1,), (1,)), ((), ())), preferred_element_type=F32)


def kernel(
    nx, nu, list_in, hidden_in, w_in, gain_in, ck_in, cv_in, out_ref,
    list_ref, hidden_ref, w_buf, gain_ref, ck_ref, cv_ref, lists, named, stage, out1, in1, outx, inx, xbuf, kv, qbuf, kvf,
    vaug, rsout, rsin, ret_out, ret1, stage2, out2, in2,
    in_sem, w_s, w_r, list_s, list_r, name_s, name_r, p1_s, p1_r, px_s, px_r, z_s, z_r, opp_s, opp_r, kv_s, kv_r, q_s, q_r, kf_s, kf_r, rs_s, rs_r,
    ret_s, ret_r, back_s, back_r,
):
    b, u, c = lax.axis_index("bal"), lax.axis_index("uly"), lax.axis_index("cfg")
    nb, width = lists.shape[0], hidden_ref.shape[1]
    ny = nb // nx
    x, y = b // ny, b % ny
    toks = hidden_ref.shape[0]
    blocks = toks // BLOCK
    entries = list_ref.shape[0]
    keys = ck_ref.shape[0]
    half = nu * BLOCK
    pieces = width // LANES
    nh = 2 * nu
    other = 1 - c

    def farthest(j, n):
        step = (j + 1) // 2
        return lax.rem(n // 2 + n + jnp.where(lax.rem(j, 2) == 1, step, -step), n)

    def x_of(k):
        return lax.rem(x + farthest(k - 1, nx), nx)

    def y_of(k):
        return lax.rem(y + farthest(k - 1, ny), ny)

    def bal_of(k):
        return x_of(lax.rem(k - 1, nx) + 1) * ny + y_of((k - 1) // nx + 1)

    def ways(n):
        return [(n // 2 + (j + 1) // 2 * (1 if j % 2 == 1 else -1)) % n for j in range(n)]

    x_list = [lax.rem(x + way, nx) for way in ways(nx)]
    y_list = [lax.rem(y + way, ny) for way in ways(ny)]
    bal_list = [x_list[j % nx] * ny + y_list[j // nx] for j in range(nb)]

    z_list = [lax.rem(u + way, nu) for way in ways(nu)]

    def x_dev(k):
        return (lax.rem(x + k, nx) * ny + y, u, c)

    def y_dev(k):
        return (x * ny + lax.rem(y + k, ny), u, c)

    def z_dev(k):
        return (b, lax.rem(u + k, nu), c)

    def remote(src, dst, s, r, dev):
        return pltpu.make_async_remote_copy(
            src_ref=src, dst_ref=dst, send_sem=s, recv_sem=r, device_id=dev, device_id_type=MESH
        )

    def each(lo, hi, body):
        lax.fori_loop(lo, hi, lambda i, z: (body(i), z)[1], 0)

    pairs = (
        (list_in, list_ref),
        (ck_in, ck_ref),
        (cv_in, cv_ref),
        (w_in, w_buf.at[c]),
        (hidden_in, hidden_ref),
        (gain_in, gain_ref),
    )
    loads = tuple(
        pltpu.make_async_copy(src, dst, in_sem.at[i]) for i, (src, dst) in enumerate(pairs)
    )
    for load in loads:
        load.start()
    list_load, k_load, v_load, w_load, hidden_load, gain_load = loads
    cleanup = []

    barrier = pltpu.get_barrier_semaphore()

    def greet(dev):
        pl.semaphore_signal(barrier, inc=1, device_id=dev, device_id_type=MESH)

    for k in range(1, nb):
        greet((bal_list[k - 1], u, c))
    for k in range(1, nu):
        greet((b, z_list[k - 1], c))
    greet((b, u, other))

    list_load.wait()
    my_blocks = 0
    for j in range(entries):
        my_blocks = my_blocks + jnp.where(list_ref[j] < blocks, 1, 0)
    lane = iota((1, LANES), 1)
    row = jnp.zeros((1, LANES), jnp.int32) + my_blocks
    for j in range(entries):
        row = jnp.where(lane == LANES - entries + j, list_ref[j], row)
    lists[b] = row

    hidden_load.wait()
    token = jnp.zeros((nb, toks), jnp.int32)
    for j in range(entries):
        token = jnp.where(iota((nb, toks), 0) % entries == j, list_ref[j], token)
    token = token * BLOCK + iota((nb, toks), 0) // entries
    pick = (token == iota((nb, toks), 1)).astype(F32).astype(BF16)
    for j in range(pieces):
        stage[:, j, :] = dot(pick, hidden_ref[:, j * LANES : (j + 1) * LANES])
    out1[...] = stage[...].astype(BF16).reshape(out1.shape)

    k_load.wait()
    v_load.wait()
    for head in range(2):
        columns = slice(head * HEAD_DIM, (head + 1) * HEAD_DIM)
        kv[x, head, 0] = normalize(ck_ref[:, columns].astype(F32)).astype(BF16)
        kv[x, head, 1] = cv_ref[:, columns]

    pl.semaphore_wait(barrier, nb - 1 + nu - 1 + 1)

    def list_copy(k, slot, to):
        return remote(lists.at[b], lists.at[slot], list_s.at[k], list_r.at[slot], (to, u, c))

    for k in range(1, nb):
        list_copy(k, b, bal_list[k - 1]).start()
    cleanup.append(lambda: each(1, nb, lambda k: list_copy(k, b, bal_of(k)).wait_send()))

    def p1_copy(k, slot):
        to = y_list[k - 1]
        dev = (x * ny + to, u, c)
        return remote(out1.at[to], in1.at[slot], p1_s.at[k], p1_r.at[slot], dev)

    for k in range(1, ny):
        p1_copy(k, y).start()
        cleanup.append(p1_copy(k, y).wait_send)
    in1[y] = out1[y]

    prev_x, next_x, far_x = lax.rem(x + nx - 1, nx), lax.rem(x + 1, nx), lax.rem(x + nx // 2, nx)

    def ring(slot_x, head, s, way):
        part = kv.at[slot_x, head]
        return remote(part, part, kv_s.at[s], kv_r.at[slot_x, head], x_dev(way))

    def ring_start(head):
        up, down = ring(x, head, 2 * head, 1), ring(x, head, 2 * head + 1, nx - 1)
        up.start()
        down.start()
        cleanup.extend((up.wait_send, down.wait_send))

    ring_start(0)

    w_load.wait()
    w_out = remote(w_buf.at[c], w_buf.at[c], w_s, w_r, (b, u, other))
    w_out.start()
    cleanup.append(w_out.wait_send)


    def list_arrival(k):
        slot = lax.rem(b + k, nb)
        list_copy(k, slot, slot).wait_recv()

    each(1, nb, list_arrival)
    table = lists[...].reshape(nb, LANES).astype(F32)
    counts = table[:, :nb]
    sub_n, lane_n = iota((nb, nb), 0), iota((nb, nb), 1)
    source = x * ny + lane_n // entries
    rank = jnp.sum(jnp.where(sub_n < source, counts, 0.0), axis=0, keepdims=True).astype(jnp.int32)
    known = jnp.sum(jnp.where(sub_n == source, counts, 0.0), axis=0, keepdims=True).astype(jnp.int32)
    entry = iota((1, nb), 1) % entries
    slots = nb // nx
    wanted = (sub_n % slots) * nx + sub_n // slots
    sel = (rank + entry == wanted) & (entry < known)
    sel = sel.astype(F32).astype(BF16)

    for k in range(1, ny):
        p1_copy(k, y_list[k - 1]).wait_recv()
    stage[...] = in1[...].astype(F32).reshape(stage.shape)
    for j in range(pieces):
        part = dot(sel, stage[:, j, :].astype(BF16)).astype(BF16)
        for k in range(nx):
            outx[k, :, j * LANES : (j + 1) * LANES] = part[k * slots : (k + 1) * slots, :]

    def px_copy(k, slot):
        to = x_list[k - 1]
        return remote(outx.at[to], inx.at[slot], px_s.at[k], px_r.at[slot], (to * ny + y, u, c))

    for k in range(1, nx):
        px_copy(k, x).start()
        cleanup.append(px_copy(k, x).wait_send)
    inx[x] = outx[x]

    near = (iota((BLOCK, nb), 1) == iota((BLOCK, nb), 0) * ny + y) & (iota((BLOCK, nb), 0) < nx)
    named[u] = dot(near.astype(F32).astype(BF16), table.astype(BF16))

    def name_copy(k, slot):
        return remote(named.at[u], named.at[slot], name_s.at[k], name_r.at[slot], z_dev(k))

    each(1, nu, lambda k: name_copy(k, u).start())
    cleanup.append(lambda: each(1, nu, lambda k: name_copy(k, u).wait_send()))
    ring_start(1)

    for k in range(1, nx):
        px_copy(k, x_list[k - 1]).wait_recv()
    gathered = inx[0].astype(F32)
    for k in range(1, nx):
        gathered = gathered + inx[k].astype(F32)
    xbuf[u] = gathered.astype(BF16)

    def z_copy(k, slot):
        return remote(xbuf.at[u], xbuf.at[slot], z_s.at[k], z_r.at[slot], z_dev(k))

    far = nu // 2
    order = [far - 1, far + 1, 2, nu - 2, 1, nu - 1]
    for k in order:
        z_copy(k, u).start()
        cleanup.append(z_copy(k, u).wait_send)

    def opposite_copy(side, slot):
        part = xbuf.at[slot, :, pl.ds(side * (width // 2), width // 2)]
        return remote(part, part, opp_s.at[side], opp_r.at[side], z_dev(1 if side == 0 else nu - 1))

    span = nx * keys
    owner_hit = (iota((keys, nu), 0) // toks == iota((keys, nu), 1)).astype(F32).astype(BF16)
    block_hit = (iota((keys, LANES), 0) % toks) // BLOCK == iota((keys, LANES), 1)
    ones = jnp.ones((LANES, LANES), BF16)
    lane_u = iota((nu, LANES), 1).astype(F32)

    def weigh_values(k):
        ids = named[:, pl.ds(k, 1), :].reshape(nu, LANES)
        hit = jnp.zeros((nu, LANES), F32)
        for j in range(LANES - entries, LANES):
            hit = hit + (ids[:, j : j + 1] == lane_u).astype(F32)
        spread = jnp.where(block_hit, dot(owner_hit, hit.astype(BF16)), 0.0).astype(BF16)
        mask = 1.0 - dot(spread, ones)
        rows = pl.ds(pl.multiple_of(k * keys, keys), keys)
        for h in range(2):
            vaug[h, rows, :HEAD_DIM] = (kv[k, h, 1].astype(F32) * mask).astype(BF16)
            vaug[h, rows, HEAD_DIM:] = mask.astype(BF16)

    each(1, nu, lambda k: name_copy(k, lax.rem(u + k, nu)).wait_recv())
    weigh_values(x)

    on_up, on_down = ring(prev_x, 0, 4, 1), ring(next_x, 1, 5, nx - 1)
    cleanup.extend((on_up.wait_send, on_down.wait_send))
    ring(prev_x, 0, 0, 1).wait_recv()
    on_up.start()
    for side, k in enumerate((far + 1, far - 1)):
        slot = lax.rem(u + k, nu)
        z_copy(k, slot).wait_recv()
        opposite_copy(side, slot).start()
        cleanup.append(opposite_copy(side, slot).wait_send)
    ring(next_x, 1, 2, 1).wait_recv()
    on_down.start()
    ring(prev_x, 1, 2, 1).wait_recv()
    ring(next_x, 0, 0, 1).wait_recv()
    weigh_values(prev_x)
    weigh_values(next_x)
    w_out.wait_recv()
    gain_load.wait()

    for k in order[2:]:
        z_copy(k, lax.rem(u + k, nu)).wait_recv()
    for side in range(2):
        opposite_copy(side, lax.rem(u + far, nu)).wait_recv()
    chunk = math.gcd(width, 1024)
    starts = range(0, width, chunk)
    rows = [xbuf[:, :, j : j + chunk].astype(F32).reshape(half, chunk).astype(BF16) for j in starts]

    def project(h, columns):
        total = dot(rows[0], w_buf[h, :chunk, columns])
        for i, j in enumerate(starts):
            if i > 0:
                total = total + dot(rows[i], w_buf[h, j : j + chunk, columns])
        return total

    for h in range(2):
        query = normalize(project(h, slice(0, HEAD_DIM))) * gain_ref[h : h + 1, :]
        qbuf[y, h * half : (h + 1) * half, :] = query.astype(BF16)

    def q_copy(k, slot):
        return remote(qbuf.at[y], qbuf.at[slot], q_s.at[k], q_r.at[slot], y_dev(k))

    def kf_copy(k, slot):
        return remote(kvf.at[x], kvf.at[slot], kf_s.at[k], kf_r.at[slot], (x_of(k) * ny + y, u, c))

    for k in range(ny // 2, 0, -1):
        for way in [k] if 2 * k == ny else [k, ny - k]:
            q_copy(way, y).start()
    for h in range(2):
        mine = slice(h * half, (h + 1) * half)
        both = project(h, slice(HEAD_DIM, 3 * HEAD_DIM))
        k_fresh = both[:, :HEAD_DIM].astype(BF16).astype(F32)
        kvf[x, 0, mine, :] = normalize(k_fresh).astype(BF16)
        kvf[x, 1, mine, :] = both[:, HEAD_DIM:].astype(BF16)
    each(1, nx, lambda k: kf_copy(k, x).start())
    cleanup.append(lambda: each(1, ny, lambda k: q_copy(k, y).wait_send()))
    cleanup.append(lambda: each(1, nx, lambda k: kf_copy(k, x).wait_send()))

    ring(far_x, 0, 4, 1).wait_recv()
    ring(far_x, 1, 5, nx - 1).wait_recv()
    weigh_values(far_x)

    each(1, nx, lambda k: kf_copy(k, x_of(k)).wait_recv())
    fresh_keys = nx * half
    for h in range(2):
        mine = slice(h * half, (h + 1) * half)
        vaug[h, span:, :HEAD_DIM] = kvf[:, 1, mine, :].reshape(fresh_keys, HEAD_DIM)
        vaug[h, span:, HEAD_DIM:] = jnp.ones((fresh_keys, HEAD_DIM), BF16)
    factor = 1.0 / math.sqrt(HEAD_DIM)

    def weigh(queries, some_keys):
        return jnp.exp(dot_t(queries, some_keys) * factor).astype(BF16)

    def rs_copy(k, slot):
        to = lax.rem(y + k, ny)
        return remote(rsout.at[to], rsin.at[slot], rs_s.at[k], rs_r.at[slot], y_dev(k))

    def attend(i):
        step = ny // 2 - 1 - i
        last = step == ny // 2 - 1
        way_a, way_b = step + 1, jnp.where(last, 0, ny - 1 - step)
        slot_a, slot_b = lax.rem(y + way_a, ny), lax.rem(y + way_b, ny)

        q_copy(way_a, slot_a).wait_recv()

        @pl.when(jnp.logical_not(last))
        def _():
            q_copy(way_b, slot_b).wait_recv()

        flat_a = jnp.zeros((1, LANES), F32)
        flat_b = jnp.zeros((1, LANES), F32)
        for h in range(2):
            mine = slice(h * half, (h + 1) * half)
            queries = jnp.concatenate([qbuf[slot_a, mine, :], qbuf[slot_b, mine, :]], axis=0)
            k_last = kvf[:, 0, mine, :].reshape(fresh_keys, HEAD_DIM)
            got = dot(weigh(queries, k_last), vaug[h, span:, :])
            for k in range(nx):
                got = got + dot(weigh(queries, kv[k, h, 0]), vaug[h, k * keys : (k + 1) * keys, :])
            rsout[slot_a, mine, :] = got[:half, :HEAD_DIM].astype(BF16)
            rsout[slot_b, mine, :] = got[half:, :HEAD_DIM].astype(BF16)
            place = iota((half, LANES), 1) == iota((half, LANES), 0) + h * half
            flat_a = flat_a + jnp.sum(jnp.where(place, got[:half, HEAD_DIM:], 0.0), axis=0, keepdims=True)
            flat_b = flat_b + jnp.sum(jnp.where(place, got[half:, HEAD_DIM:], 0.0), axis=0, keepdims=True)
        tail = rsout.shape[1] - 2 * half
        tail_row = iota((tail, LANES), 0)
        for slot, flat in ((slot_a, flat_a), (slot_b, flat_b)):
            coarse = flat.astype(BF16).astype(F32)
            rest = jnp.where(tail_row == 1, flat - coarse, 0.0)
            rsout[slot, 2 * half :, :] = jnp.where(tail_row == 0, coarse, rest).astype(BF16)

        rs_copy(way_a, y).start()

        @pl.when(jnp.logical_not(last))
        def _():
            rs_copy(way_b, y).start()

    each(0, ny // 2, attend)
    cleanup.append(lambda: each(1, ny, lambda k: rs_copy(k, y).wait_send()))

    count_row = jnp.sum(jnp.where(sub_n == lane_n, counts, 0.0), axis=0, keepdims=True)
    start_col = jnp.sum(jnp.where(lane_n < sub_n, count_row, 0.0), axis=1, keepdims=True).astype(jnp.int32)
    rank_col = start_col + jnp.bitwise_and(x - start_col, nx - 1)
    give = rank_col < start_col + counts[:, :slots].astype(jnp.int32)
    give = give & (rank_col // nx == iota((nb, slots), 1))
    give = give.astype(F32).astype(BF16)
    my_start = jnp.sum(jnp.where(sub_n < b, counts, 0.0), axis=0, keepdims=True).astype(jnp.int32)
    from_x = jnp.bitwise_and(my_start + sub_n // BLOCK, nx - 1)
    final = (from_x * ny + sub_n % BLOCK == lane_n) & (sub_n // BLOCK < my_blocks)
    final = final.astype(F32).astype(BF16)
    summed = rsout[y].astype(F32)
    for k in range(1, ny // 2 + 1):
        for way in [k] if 2 * k == ny else [k, ny - k]:
            slot = lax.rem(y + way, ny)
            rs_copy(way, slot).wait_recv()
            summed = summed + rsin[slot].astype(F32)
    total = summed[2 * half : 2 * half + 1, :] + summed[2 * half + 1 : 2 * half + 2, :]
    square = iota((2 * half, LANES), 0) == iota((2 * half, LANES), 1)
    total = jnp.sum(jnp.where(square, total, 0.0), axis=1, keepdims=True)
    attended = summed[: 2 * half, :] / total
    for h in range(2):
        rows = attended[h * half : (h + 1) * half, :]
        ret_out[:, h] = rows.reshape(nu, BLOCK, HEAD_DIM).astype(BF16)

    def ret_copy(k, slot):
        to = z_list[k - 1]
        return remote(ret_out.at[to], ret1.at[slot], ret_s.at[k], ret_r.at[slot], (b, to, c))

    for k in range(1, nu):
        ret_copy(k, u).start()
        cleanup.append(ret_copy(k, u).wait_send)
    ret1[u] = ret_out[u]
    for k in range(1, nu):
        ret_copy(k, z_list[k - 1]).wait_recv()
    for h in range(nh):
        stage2[:, h, :] = dot(give, ret1[h // 2, h % 2])
    out2[...] = stage2[...].astype(BF16)

    def back_copy(k, slot, to):
        return remote(out2.at[to], in2.at[slot], back_s.at[k], back_r.at[slot], (to, u, c))

    for k in range(1, nb):
        back_copy(k, b, bal_list[k - 1]).start()
    in2[b] = out2[b]
    for finish in cleanup:
        finish()

    def back_arrival(k):
        slot = lax.rem(b + k, nb)
        back_copy(k, slot, slot).wait_recv()

    each(1, nb, back_arrival)
    stage2[...] = in2[...].astype(F32)
    for h in range(nh):
        out_ref[:, h * HEAD_DIM : (h + 1) * HEAD_DIM] = dot(final, stage2[:, h, :].astype(BF16)).astype(BF16)

    each(1, nb, lambda k: back_copy(k, b, bal_of(k)).wait_send())


def on_device(hidden, w_qkv, q_gain, cache_k, cache_v, fresh_list):
    nb, nu = lax.axis_size("bal"), lax.axis_size("uly")
    nx = SIDE_X
    ny = nb // nx
    toks, width = hidden.shape[1:]
    keys = cache_k.shape[1]
    entries = fresh_list.shape[3]
    half = nu * BLOCK
    nh = 2 * nu
    pieces = width // LANES
    span = nx * (keys + half)
    vmem = pl.BlockSpec(memory_space=pltpu.VMEM)
    dma = pltpu.SemaphoreType.DMA
    out = pl.pallas_call(
        functools.partial(kernel, nx, nu),
        out_shape=jax.ShapeDtypeStruct((entries * BLOCK, nh * HEAD_DIM), BF16),
        in_specs=[
            *[pl.BlockSpec(memory_space=pltpu.HBM)] * 6,
        ],
        out_specs=vmem,
        scratch_shapes=[
            pltpu.SMEM((entries,), jnp.int32),
            pltpu.VMEM((toks, width), BF16),
            pltpu.VMEM((2, *w_qkv.shape), BF16),
            pltpu.VMEM((2, HEAD_DIM), F32),
            pltpu.VMEM((keys, 2 * HEAD_DIM), BF16),
            pltpu.VMEM((keys, 2 * HEAD_DIM), BF16),
            pltpu.VMEM((nb, 1, LANES), jnp.int32),
            pltpu.VMEM((nu, BLOCK, LANES), F32),
            pltpu.VMEM((nb, pieces, LANES), F32),
            pltpu.VMEM((ny, entries, pieces, LANES), BF16),
            pltpu.VMEM((ny, entries, pieces, LANES), BF16),
            pltpu.VMEM((nx, nb // nx, width), BF16),
            pltpu.VMEM((nx, nb // nx, width), BF16),
            pltpu.VMEM((nu, nb // nx, width), BF16),
            pltpu.VMEM((nx, 2, 2, keys, HEAD_DIM), BF16),
            pltpu.VMEM((ny, 2 * half, HEAD_DIM), BF16),
            pltpu.VMEM((nx, 2, 2 * half, HEAD_DIM), BF16),
            pltpu.VMEM((2, span, 2 * HEAD_DIM), BF16),
            pltpu.VMEM((ny, 2 * half + 8, HEAD_DIM), BF16),
            pltpu.VMEM((ny, 2 * half + 8, HEAD_DIM), BF16),
            pltpu.VMEM((nu, 2, BLOCK, HEAD_DIM), BF16),
            pltpu.VMEM((nu, 2, BLOCK, HEAD_DIM), BF16),
            pltpu.VMEM((nb, nh, HEAD_DIM), F32),
            pltpu.VMEM((nb, nh, HEAD_DIM), BF16),
            pltpu.VMEM((nb, nh, HEAD_DIM), BF16),
            dma((6,)),
            dma, dma,
            dma((nb,)), dma((nb,)),
            dma((nu,)), dma((nu,)),
            dma((ny,)), dma((ny,)),
            dma((nx,)), dma((nx,)),
            dma((nu,)), dma((nu,)),
            dma((2,)), dma((2,)),
            dma((6,)), dma((nx, 2)),
            dma((ny,)), dma((ny,)),
            dma((nx,)), dma((nx,)),
            dma((ny,)), dma((ny,)),
            dma((nu,)), dma((nu,)),
            dma((nb,)), dma((nb,)),
        ],
        compiler_params=pltpu.CompilerParams(
            collective_id=0, has_side_effects=True, vmem_limit_bytes=63 * 1024 * 1024
        ),
    )(
        fresh_list.reshape(entries),
        hidden.reshape(toks, width),
        w_qkv,
        q_gain.reshape(2, HEAD_DIM),
        cache_k.reshape(keys, 2 * HEAD_DIM),
        cache_v.reshape(keys, 2 * HEAD_DIM),
    )
    return out.reshape(1, 1, 1, entries * BLOCK, nh * HEAD_DIM)


def solution(mesh):
    in_specs = (
        P("cfg", ("bal", "uly"), None),
        P(None, ("uly", "cfg")),
        P("uly"),
        P("cfg", "bal", "uly"),
        P("cfg", "bal", "uly"),
        P("cfg", "bal", "uly", None),
    )
    out_specs = P("cfg", "bal", "uly", None, None)
    return jax.shard_map(
        on_device, mesh=mesh, in_specs=in_specs, out_specs=out_specs, check_vma=False
    )
```

```python
import functools
import math

import jax
import jax.numpy as jnp
from jax import lax
from jax.experimental import pallas as pl
from jax.experimental.pallas import tpu as pltpu
from jax.sharding import PartitionSpec as P

HEAD_DIM = 128
BLOCK = 8
SIDE_X = 4
LANES = 128
MESH = pl.DeviceIdType.MESH
F32 = jnp.float32
BF16 = jnp.bfloat16


def normalize(values):
    return values * lax.rsqrt(jnp.mean(values * values, axis=-1, keepdims=True) + 1e-06)


def iota(shape, dim):
    return lax.broadcasted_iota(jnp.int32, shape, dim)


def dot(a, b):
    return jnp.dot(a, b, preferred_element_type=F32)


def dot_t(a, b):
    return lax.dot_general(a, b, (((1,), (1,)), ((), ())), preferred_element_type=F32)


def kernel(
    nx, nu, list_in, hidden_in, w_in, gain_in, ck_in, cv_in, out_ref,
    list_ref, hidden_ref, w_buf, gain_ref, ck_ref, cv_ref, lists, named, stage, out1, in1, outx, inx, xbuf, kv, qbuf, kvf,
    vaug, rsout, rsin, ret_out, ret1, stage2, out2, in2,
    in_sem, w_s, w_r, list_s, list_r, name_s, name_r, p1_s, p1_r, px_s, px_r, z_s, z_r, opp_s, opp_r, kv_s, kv_r, q_s, q_r, kf_s, kf_r, rs_s, rs_r,
    ret_s, ret_r, back_s, back_r,
):
    b, u, c = lax.axis_index("bal"), lax.axis_index("uly"), lax.axis_index("cfg")
    nb, width = lists.shape[0], hidden_ref.shape[1]
    ny = nb // nx
    x, y = b // ny, b % ny
    toks = hidden_ref.shape[0]
    blocks = toks // BLOCK
    entries = list_ref.shape[0]
    keys = ck_ref.shape[0]
    half = nu * BLOCK
    pieces = width // LANES
    nh = 2 * nu
    other = 1 - c

    def farthest(j, n):
        step = (j + 1) // 2
        return lax.rem(n // 2 + n + jnp.where(lax.rem(j, 2) == 1, step, -step), n)

    def x_of(k):
        return lax.rem(x + farthest(k - 1, nx), nx)

    def y_of(k):
        return lax.rem(y + farthest(k - 1, ny), ny)

    def bal_of(k):
        return x_of(lax.rem(k - 1, nx) + 1) * ny + y_of((k - 1) // nx + 1)

    def ways(n):
        return [(n // 2 + (j + 1) // 2 * (1 if j % 2 == 1 else -1)) % n for j in range(n)]

    x_list = [lax.rem(x + way, nx) for way in ways(nx)]
    y_list = [lax.rem(y + way, ny) for way in ways(ny)]
    bal_list = [x_list[j % nx] * ny + y_list[j // nx] for j in range(nb)]

    z_list = [lax.rem(u + way, nu) for way in ways(nu)]

    def x_dev(k):
        return (lax.rem(x + k, nx) * ny + y, u, c)

    def y_dev(k):
        return (x * ny + lax.rem(y + k, ny), u, c)

    def z_dev(k):
        return (b, lax.rem(u + k, nu), c)

    def remote(src, dst, s, r, dev):
        return pltpu.make_async_remote_copy(
            src_ref=src, dst_ref=dst, send_sem=s, recv_sem=r, device_id=dev, device_id_type=MESH
        )

    def each(lo, hi, body):
        lax.fori_loop(lo, hi, lambda i, z: (body(i), z)[1], 0)

    pairs = (
        (list_in, list_ref),
        (ck_in, ck_ref),
        (cv_in, cv_ref),
        (w_in, w_buf.at[c]),
        (hidden_in, hidden_ref),
        (gain_in, gain_ref),
    )
    loads = tuple(
        pltpu.make_async_copy(src, dst, in_sem.at[i]) for i, (src, dst) in enumerate(pairs)
    )
    for load in loads:
        load.start()
    list_load, k_load, v_load, w_load, hidden_load, gain_load = loads
    cleanup = []

    barrier = pltpu.get_barrier_semaphore()

    def greet(dev):
        pl.semaphore_signal(barrier, inc=1, device_id=dev, device_id_type=MESH)

    for k in range(1, nb):
        greet((bal_list[k - 1], u, c))
    for k in range(1, nu):
        greet((b, z_list[k - 1], c))
    greet((b, u, other))

    list_load.wait()
    my_blocks = 0
    for j in range(entries):
        my_blocks = my_blocks + jnp.where(list_ref[j] < blocks, 1, 0)
    lane = iota((1, LANES), 1)
    row = jnp.zeros((1, LANES), jnp.int32) + my_blocks
    for j in range(entries):
        row = jnp.where(lane == LANES - entries + j, list_ref[j], row)
    lists[b] = row

    hidden_load.wait()
    token = jnp.zeros((nb, toks), jnp.int32)
    for j in range(entries):
        token = jnp.where(iota((nb, toks), 0) % entries == j, list_ref[j], token)
    token = token * BLOCK + iota((nb, toks), 0) // entries
    pick = (token == iota((nb, toks), 1)).astype(F32).astype(BF16)
    for j in range(pieces):
        stage[:, j, :] = dot(pick, hidden_ref[:, j * LANES : (j + 1) * LANES])
    out1[...] = stage[...].astype(BF16).reshape(out1.shape)

    k_load.wait()
    v_load.wait()
    for head in range(2):
        columns = slice(head * HEAD_DIM, (head + 1) * HEAD_DIM)
        kv[x, head, 0] = normalize(ck_ref[:, columns].astype(F32)).astype(BF16)
        kv[x, head, 1] = cv_ref[:, columns]

    pl.semaphore_wait(barrier, nb - 1 + nu - 1 + 1)

    def list_copy(k, slot, to):
        return remote(lists.at[b], lists.at[slot], list_s.at[k], list_r.at[slot], (to, u, c))

    for k in range(1, nb):
        list_copy(k, b, bal_list[k - 1]).start()
    cleanup.append(lambda: each(1, nb, lambda k: list_copy(k, b, bal_of(k)).wait_send()))

    def p1_copy(k, slot):
        to = y_list[k - 1]
        dev = (x * ny + to, u, c)
        return remote(out1.at[to], in1.at[slot], p1_s.at[k], p1_r.at[slot], dev)

    for k in range(1, ny):
        p1_copy(k, y).start()
        cleanup.append(p1_copy(k, y).wait_send)
    in1[y] = out1[y]

    prev_x, next_x, far_x = lax.rem(x + nx - 1, nx), lax.rem(x + 1, nx), lax.rem(x + nx // 2, nx)

    def ring(slot_x, head, s, way):
        part = kv.at[slot_x, head]
        return remote(part, part, kv_s.at[s], kv_r.at[slot_x, head], x_dev(way))

    def ring_start(head):
        up, down = ring(x, head, 2 * head, 1), ring(x, head, 2 * head + 1, nx - 1)
        up.start()
        down.start()
        cleanup.extend((up.wait_send, down.wait_send))

    ring_start(0)

    w_load.wait()
    w_out = remote(w_buf.at[c], w_buf.at[c], w_s, w_r, (b, u, other))
    w_out.start()
    cleanup.append(w_out.wait_send)


    def list_arrival(k):
        slot = lax.rem(b + k, nb)
        list_copy(k, slot, slot).wait_recv()

    for k in range(1, ny):
        p1_copy(k, y_list[k - 1]).wait_recv()
    stage[...] = in1[...].astype(F32).reshape(stage.shape)
    each(1, nb, list_arrival)
    table = lists[...].reshape(nb, LANES).astype(F32)
    counts = table[:, :nb]
    sub_n, lane_n = iota((nb, nb), 0), iota((nb, nb), 1)
    source = x * ny + lane_n // entries
    rank = jnp.sum(jnp.where(sub_n < source, counts, 0.0), axis=0, keepdims=True).astype(jnp.int32)
    known = jnp.sum(jnp.where(sub_n == source, counts, 0.0), axis=0, keepdims=True).astype(jnp.int32)
    entry = iota((1, nb), 1) % entries
    slots = nb // nx
    wanted = (sub_n % slots) * nx + sub_n // slots
    sel = (rank + entry == wanted) & (entry < known)
    sel = sel.astype(F32).astype(BF16)

    for j in range(pieces):
        part = dot(sel, stage[:, j, :].astype(BF16)).astype(BF16)
        for k in range(nx):
            outx[k, :, j * LANES : (j + 1) * LANES] = part[k * slots : (k + 1) * slots, :]

    def px_copy(k, slot):
        to = x_list[k - 1]
        return remote(outx.at[to], inx.at[slot], px_s.at[k], px_r.at[slot], (to * ny + y, u, c))

    for k in range(1, nx):
        px_copy(k, x).start()
        cleanup.append(px_copy(k, x).wait_send)
    inx[x] = outx[x]

    near = (iota((BLOCK, nb), 1) == iota((BLOCK, nb), 0) * ny + y) & (iota((BLOCK, nb), 0) < nx)
    named[u] = dot(near.astype(F32).astype(BF16), table.astype(BF16))

    def name_copy(k, slot):
        return remote(named.at[u], named.at[slot], name_s.at[k], name_r.at[slot], z_dev(k))

    each(1, nu, lambda k: name_copy(k, u).start())
    cleanup.append(lambda: each(1, nu, lambda k: name_copy(k, u).wait_send()))
    ring_start(1)

    for k in range(1, nx):
        px_copy(k, x_list[k - 1]).wait_recv()
    gathered = inx[0].astype(F32)
    for k in range(1, nx):
        gathered = gathered + inx[k].astype(F32)
    xbuf[u] = gathered.astype(BF16)

    def z_copy(k, slot):
        return remote(xbuf.at[u], xbuf.at[slot], z_s.at[k], z_r.at[slot], z_dev(k))

    far = nu // 2
    order = [far - 1, far + 1, 2, nu - 2, 1, nu - 1]
    for k in order:
        z_copy(k, u).start()
        cleanup.append(z_copy(k, u).wait_send)

    def opposite_copy(side, slot):
        part = xbuf.at[slot, :, pl.ds(side * (width // 2), width // 2)]
        return remote(part, part, opp_s.at[side], opp_r.at[side], z_dev(1 if side == 0 else nu - 1))

    span = nx * keys
    owner_hit = (iota((keys, nu), 0) // toks == iota((keys, nu), 1)).astype(F32).astype(BF16)
    block_hit = (iota((keys, LANES), 0) % toks) // BLOCK == iota((keys, LANES), 1)
    ones = jnp.ones((LANES, LANES), BF16)
    lane_u = iota((nu, LANES), 1).astype(F32)

    def weigh_values(k):
        ids = named[:, pl.ds(k, 1), :].reshape(nu, LANES)
        hit = jnp.zeros((nu, LANES), F32)
        for j in range(LANES - entries, LANES):
            hit = hit + (ids[:, j : j + 1] == lane_u).astype(F32)
        spread = jnp.where(block_hit, dot(owner_hit, hit.astype(BF16)), 0.0).astype(BF16)
        mask = 1.0 - dot(spread, ones)
        rows = pl.ds(pl.multiple_of(k * keys, keys), keys)
        for h in range(2):
            vaug[h, rows, :HEAD_DIM] = (kv[k, h, 1].astype(F32) * mask).astype(BF16)
            vaug[h, rows, HEAD_DIM:] = mask.astype(BF16)

    each(1, nu, lambda k: name_copy(k, lax.rem(u + k, nu)).wait_recv())
    weigh_values(x)

    on_up, on_down = ring(prev_x, 0, 4, 1), ring(next_x, 1, 5, nx - 1)
    cleanup.extend((on_up.wait_send, on_down.wait_send))
    ring(prev_x, 0, 0, 1).wait_recv()
    on_up.start()
    for side, k in enumerate((far + 1, far - 1)):
        slot = lax.rem(u + k, nu)
        z_copy(k, slot).wait_recv()
        opposite_copy(side, slot).start()
        cleanup.append(opposite_copy(side, slot).wait_send)
    ring(next_x, 1, 2, 1).wait_recv()
    on_down.start()
    ring(prev_x, 1, 2, 1).wait_recv()
    ring(next_x, 0, 0, 1).wait_recv()
    weigh_values(prev_x)
    weigh_values(next_x)
    w_out.wait_recv()
    gain_load.wait()

    for k in order[2:]:
        z_copy(k, lax.rem(u + k, nu)).wait_recv()
    for side in range(2):
        opposite_copy(side, lax.rem(u + far, nu)).wait_recv()
    chunk = math.gcd(width, 1024)
    starts = range(0, width, chunk)
    rows = [xbuf[:, :, j : j + chunk].astype(F32).reshape(half, chunk).astype(BF16) for j in starts]

    def project(h, columns):
        total = dot(rows[0], w_buf[h, :chunk, columns])
        for i, j in enumerate(starts):
            if i > 0:
                total = total + dot(rows[i], w_buf[h, j : j + chunk, columns])
        return total

    for h in range(2):
        query = normalize(project(h, slice(0, HEAD_DIM))) * gain_ref[h : h + 1, :]
        qbuf[y, h * half : (h + 1) * half, :] = query.astype(BF16)

    def q_copy(k, slot):
        return remote(qbuf.at[y], qbuf.at[slot], q_s.at[k], q_r.at[slot], y_dev(k))

    def kf_copy(k, slot):
        return remote(kvf.at[x], kvf.at[slot], kf_s.at[k], kf_r.at[slot], (x_of(k) * ny + y, u, c))

    for k in range(ny // 2, 0, -1):
        for way in [k] if 2 * k == ny else [k, ny - k]:
            q_copy(way, y).start()
    for h in range(2):
        mine = slice(h * half, (h + 1) * half)
        both = project(h, slice(HEAD_DIM, 3 * HEAD_DIM))
        k_fresh = both[:, :HEAD_DIM].astype(BF16).astype(F32)
        kvf[x, 0, mine, :] = normalize(k_fresh).astype(BF16)
        kvf[x, 1, mine, :] = both[:, HEAD_DIM:].astype(BF16)
    each(1, nx, lambda k: kf_copy(k, x).start())
    cleanup.append(lambda: each(1, ny, lambda k: q_copy(k, y).wait_send()))
    cleanup.append(lambda: each(1, nx, lambda k: kf_copy(k, x).wait_send()))

    ring(far_x, 0, 4, 1).wait_recv()
    ring(far_x, 1, 5, nx - 1).wait_recv()
    weigh_values(far_x)

    each(1, nx, lambda k: kf_copy(k, x_of(k)).wait_recv())
    fresh_keys = nx * half
    for h in range(2):
        mine = slice(h * half, (h + 1) * half)
        vaug[h, span:, :HEAD_DIM] = kvf[:, 1, mine, :].reshape(fresh_keys, HEAD_DIM)
        vaug[h, span:, HEAD_DIM:] = jnp.ones((fresh_keys, HEAD_DIM), BF16)
    factor = 1.0 / math.sqrt(HEAD_DIM)

    def weigh(queries, some_keys):
        return jnp.exp(dot_t(queries, some_keys) * factor).astype(BF16)

    def rs_copy(k, slot):
        to = lax.rem(y + k, ny)
        return remote(rsout.at[to], rsin.at[slot], rs_s.at[k], rs_r.at[slot], y_dev(k))

    def attend(i):
        step = ny // 2 - 1 - i
        last = step == ny // 2 - 1
        way_a, way_b = step + 1, jnp.where(last, 0, ny - 1 - step)
        slot_a, slot_b = lax.rem(y + way_a, ny), lax.rem(y + way_b, ny)

        q_copy(way_a, slot_a).wait_recv()

        @pl.when(jnp.logical_not(last))
        def _():
            q_copy(way_b, slot_b).wait_recv()

        flat_a = jnp.zeros((1, LANES), F32)
        flat_b = jnp.zeros((1, LANES), F32)
        for h in range(2):
            mine = slice(h * half, (h + 1) * half)
            queries = jnp.concatenate([qbuf[slot_a, mine, :], qbuf[slot_b, mine, :]], axis=0)
            k_last = kvf[:, 0, mine, :].reshape(fresh_keys, HEAD_DIM)
            got = dot(weigh(queries, k_last), vaug[h, span:, :])
            for k in range(nx):
                got = got + dot(weigh(queries, kv[k, h, 0]), vaug[h, k * keys : (k + 1) * keys, :])
            rsout[slot_a, mine, :] = got[:half, :HEAD_DIM].astype(BF16)
            rsout[slot_b, mine, :] = got[half:, :HEAD_DIM].astype(BF16)
            place = iota((half, LANES), 1) == iota((half, LANES), 0) + h * half
            flat_a = flat_a + jnp.sum(jnp.where(place, got[:half, HEAD_DIM:], 0.0), axis=0, keepdims=True)
            flat_b = flat_b + jnp.sum(jnp.where(place, got[half:, HEAD_DIM:], 0.0), axis=0, keepdims=True)
        tail = rsout.shape[1] - 2 * half
        tail_row = iota((tail, LANES), 0)
        for slot, flat in ((slot_a, flat_a), (slot_b, flat_b)):
            coarse = flat.astype(BF16).astype(F32)
            rest = jnp.where(tail_row == 1, flat - coarse, 0.0)
            rsout[slot, 2 * half :, :] = jnp.where(tail_row == 0, coarse, rest).astype(BF16)

        rs_copy(way_a, y).start()

        @pl.when(jnp.logical_not(last))
        def _():
            rs_copy(way_b, y).start()

    each(0, ny // 2, attend)
    cleanup.append(lambda: each(1, ny, lambda k: rs_copy(k, y).wait_send()))

    count_row = jnp.sum(jnp.where(sub_n == lane_n, counts, 0.0), axis=0, keepdims=True)
    start_col = jnp.sum(jnp.where(lane_n < sub_n, count_row, 0.0), axis=1, keepdims=True).astype(jnp.int32)
    rank_col = start_col + jnp.bitwise_and(x - start_col, nx - 1)
    give = rank_col < start_col + counts[:, :slots].astype(jnp.int32)
    give = give & (rank_col // nx == iota((nb, slots), 1))
    give = give.astype(F32).astype(BF16)
    my_start = jnp.sum(jnp.where(sub_n < b, counts, 0.0), axis=0, keepdims=True).astype(jnp.int32)
    from_x = jnp.bitwise_and(my_start + sub_n // BLOCK, nx - 1)
    final = (from_x * ny + sub_n % BLOCK == lane_n) & (sub_n // BLOCK < my_blocks)
    final = final.astype(F32).astype(BF16)
    summed = rsout[y].astype(F32)
    for k in range(1, ny // 2 + 1):
        for way in [k] if 2 * k == ny else [k, ny - k]:
            slot = lax.rem(y + way, ny)
            rs_copy(way, slot).wait_recv()
            summed = summed + rsin[slot].astype(F32)
    total = summed[2 * half : 2 * half + 1, :] + summed[2 * half + 1 : 2 * half + 2, :]
    square = iota((2 * half, LANES), 0) == iota((2 * half, LANES), 1)
    total = jnp.sum(jnp.where(square, total, 0.0), axis=1, keepdims=True)
    attended = summed[: 2 * half, :] / total
    for h in range(2):
        rows = attended[h * half : (h + 1) * half, :]
        ret_out[:, h] = rows.reshape(nu, BLOCK, HEAD_DIM).astype(BF16)

    def ret_copy(k, slot):
        to = z_list[k - 1]
        return remote(ret_out.at[to], ret1.at[slot], ret_s.at[k], ret_r.at[slot], (b, to, c))

    for k in range(1, nu):
        ret_copy(k, u).start()
        cleanup.append(ret_copy(k, u).wait_send)
    ret1[u] = ret_out[u]
    for k in range(1, nu):
        ret_copy(k, z_list[k - 1]).wait_recv()
    for h in range(nh):
        stage2[:, h, :] = dot(give, ret1[h // 2, h % 2])
    out2[...] = stage2[...].astype(BF16)

    def back_copy(k, slot, to):
        return remote(out2.at[to], in2.at[slot], back_s.at[k], back_r.at[slot], (to, u, c))

    for k in range(1, nb):
        back_copy(k, b, bal_list[k - 1]).start()
    in2[b] = out2[b]
    for finish in cleanup:
        finish()

    def back_arrival(k):
        slot = lax.rem(b + k, nb)
        back_copy(k, slot, slot).wait_recv()

    each(1, nb, back_arrival)
    stage2[...] = in2[...].astype(F32)
    for h in range(nh):
        out_ref[:, h * HEAD_DIM : (h + 1) * HEAD_DIM] = dot(final, stage2[:, h, :].astype(BF16)).astype(BF16)

    each(1, nb, lambda k: back_copy(k, b, bal_of(k)).wait_send())


def on_device(hidden, w_qkv, q_gain, cache_k, cache_v, fresh_list):
    nb, nu = lax.axis_size("bal"), lax.axis_size("uly")
    nx = SIDE_X
    ny = nb // nx
    toks, width = hidden.shape[1:]
    keys = cache_k.shape[1]
    entries = fresh_list.shape[3]
    half = nu * BLOCK
    nh = 2 * nu
    pieces = width // LANES
    span = nx * (keys + half)
    vmem = pl.BlockSpec(memory_space=pltpu.VMEM)
    dma = pltpu.SemaphoreType.DMA
    out = pl.pallas_call(
        functools.partial(kernel, nx, nu),
        out_shape=jax.ShapeDtypeStruct((entries * BLOCK, nh * HEAD_DIM), BF16),
        in_specs=[
            *[pl.BlockSpec(memory_space=pltpu.HBM)] * 6,
        ],
        out_specs=vmem,
        scratch_shapes=[
            pltpu.SMEM((entries,), jnp.int32),
            pltpu.VMEM((toks, width), BF16),
            pltpu.VMEM((2, *w_qkv.shape), BF16),
            pltpu.VMEM((2, HEAD_DIM), F32),
            pltpu.VMEM((keys, 2 * HEAD_DIM), BF16),
            pltpu.VMEM((keys, 2 * HEAD_DIM), BF16),
            pltpu.VMEM((nb, 1, LANES), jnp.int32),
            pltpu.VMEM((nu, BLOCK, LANES), F32),
            pltpu.VMEM((nb, pieces, LANES), F32),
            pltpu.VMEM((ny, entries, pieces, LANES), BF16),
            pltpu.VMEM((ny, entries, pieces, LANES), BF16),
            pltpu.VMEM((nx, nb // nx, width), BF16),
            pltpu.VMEM((nx, nb // nx, width), BF16),
            pltpu.VMEM((nu, nb // nx, width), BF16),
            pltpu.VMEM((nx, 2, 2, keys, HEAD_DIM), BF16),
            pltpu.VMEM((ny, 2 * half, HEAD_DIM), BF16),
            pltpu.VMEM((nx, 2, 2 * half, HEAD_DIM), BF16),
            pltpu.VMEM((2, span, 2 * HEAD_DIM), BF16),
            pltpu.VMEM((ny, 2 * half + 8, HEAD_DIM), BF16),
            pltpu.VMEM((ny, 2 * half + 8, HEAD_DIM), BF16),
            pltpu.VMEM((nu, 2, BLOCK, HEAD_DIM), BF16),
            pltpu.VMEM((nu, 2, BLOCK, HEAD_DIM), BF16),
            pltpu.VMEM((nb, nh, HEAD_DIM), F32),
            pltpu.VMEM((nb, nh, HEAD_DIM), BF16),
            pltpu.VMEM((nb, nh, HEAD_DIM), BF16),
            dma((6,)),
            dma, dma,
            dma((nb,)), dma((nb,)),
            dma((nu,)), dma((nu,)),
            dma((ny,)), dma((ny,)),
            dma((nx,)), dma((nx,)),
            dma((nu,)), dma((nu,)),
            dma((2,)), dma((2,)),
            dma((6,)), dma((nx, 2)),
            dma((ny,)), dma((ny,)),
            dma((nx,)), dma((nx,)),
            dma((ny,)), dma((ny,)),
            dma((nu,)), dma((nu,)),
            dma((nb,)), dma((nb,)),
        ],
        compiler_params=pltpu.CompilerParams(
            collective_id=0, has_side_effects=True, vmem_limit_bytes=63 * 1024 * 1024
        ),
    )(
        fresh_list.reshape(entries),
        hidden.reshape(toks, width),
        w_qkv,
        q_gain.reshape(2, HEAD_DIM),
        cache_k.reshape(keys, 2 * HEAD_DIM),
        cache_v.reshape(keys, 2 * HEAD_DIM),
    )
    return out.reshape(1, 1, 1, entries * BLOCK, nh * HEAD_DIM)


def solution(mesh):
    in_specs = (
        P("cfg", ("bal", "uly"), None),
        P(None, ("uly", "cfg")),
        P("uly"),
        P("cfg", "bal", "uly"),
        P("cfg", "bal", "uly"),
        P("cfg", "bal", "uly", None),
    )
    out_specs = P("cfg", "bal", "uly", None, None)
    return jax.shard_map(
        on_device, mesh=mesh, in_specs=in_specs, out_specs=out_specs, check_vma=False
    )
```
